32 devices in a mesh: groups: 2 (over x), ty: 16 (over z, y, core).
Axes of the slice: x: 2, y: 2, z: 4, core: 2. Of those that a mesh axis runs over, the one named last changes fastest.
Arguments:
- object_field: float32 [2, 8192, 2048], P(None, ('groups', 'ty')), parts along dimension 1, may hold values from -5 to 5
- probe_field: float32 [4, 256, 256], P('groups'), parts along dimension 0, may hold values from -4 to 4
- scan_offsets: int32 [192, 2], P(('groups', 'ty')), parts along dimension 0, may hold values from 0 to 3840, as said below
- tile_counts: int32 [32], P(('groups', 'ty')), parts along dimension 0, may hold values from 1 to 6, as said below
- measured: float32 [192, 256, 256], P(('groups', 'ty')), parts along dimension 0, may hold values from 0.1 to 2
Outputs:
- object_out: float32 [2, 8192, 2048], P(None, ('groups', 'ty')), parts along dimension 1
- probe_out: float32 [4, 256, 256], P('groups'), parts along dimension 0
The draws below stay inside these ranges and needn't reach their ends.
There are 2 independent parts, one for each index of `groups`. The reference program is written for one: setup_inputs(seed, part) draws one part's arguments, and reference() takes and returns one part's arrays. A program takes and returns all parts, laid end to end along the dimension named above; each array names one. Nothing has to cross between parts.
Inputs may be any that keep to these rules, and one draw needn't show every extreme that they name: `scan_offsets`: slots j in [d * 6, (d + 1) * 6) belong to tile d: their rows lie in [d * 256, (d + 1) * 256); every window of 256 x 256 pixels lies inside the 4096 x 2048 object. tile_counts[d] counts the used slots of tile d, its first ones; some tile has all 6 used and some has one.
All inputs are finite; a program needn't handle non-finite values.
Results may differ from the reference program's by a relative error of at most 0.0003.
Values sent between devices are 32-bit elements; how exact they have to be, the bound alone decides.
No kernel may reach another device: no remote copies, remote signals or barrier semaphores. Data moves between devices by JAX's collectives and lax.ppermute only.
A program may use at most 128 MiB of HBM per device.

```python
import math
import jax
import jax.numpy as jnp
from jax import lax

PS = 256
ROWS = 256
NX = 2048
CAP = 6
ITERS = 2
NY = 4096
POSITIONS = 96
N_TY = 16


def draw_scan_offsets(key, part):
    key = jax.random.fold_in(key, 11)
    row_key, column_key = jax.random.split(key)
    numbers = jnp.arange(N_TY * CAP, dtype=jnp.int32)
    owners = numbers // CAP
    highest = jnp.where(owners == N_TY - 1, ROWS - PS + 1, ROWS)
    local_row = jax.random.randint(row_key, (N_TY * CAP,), 0, highest)
    local_row = jnp.where(numbers == 0, 0, local_row)
    local_row = jnp.where(numbers == N_TY * CAP - CAP, ROWS - PS, local_row)
    column = jax.random.randint(column_key, (N_TY * CAP,), 0, NX - PS + 1)
    return jnp.stack([owners * ROWS + local_row, column], axis=1).astype(jnp.int32)


def draw_tile_counts(key, part):
    key = jax.random.fold_in(key, 23)
    count_key, pick_key = jax.random.split(key)
    counts = jax.random.randint(count_key, (N_TY,), 1, CAP + 1)
    busiest = jax.random.randint(pick_key, (), 0, N_TY)
    tiles = jnp.arange(N_TY, dtype=jnp.int32)
    counts = jnp.where(tiles == busiest, CAP, counts)
    counts = jnp.where(tiles == (busiest + 1) % N_TY, 1, counts)
    return counts.astype(jnp.int32)


def shard_levels(own_key, shape, cuts, low, top_value):
    def one(axis_at, parts):
        heights = jax.random.uniform(jax.random.fold_in(jax.random.fold_in(own_key, 6), axis_at), (parts,), jnp.float32, low / len(cuts), top_value / len(cuts))
        return jnp.repeat(jnp.exp(heights), shape[axis_at] // parts).reshape((-1,) + (1,) * (len(shape) - axis_at - 1))

    factor_of = one(*cuts[0])
    for cut in cuts[1:]:
        factor_of = factor_of * one(*cut)
    return factor_of


def scatter_about(key, extent, spread, bound, shards=(), held_as=jnp.bfloat16):
    drawn = spread * jax.random.normal(key, extent, jnp.float32)
    if shards:
        drawn = drawn * shard_levels(key, extent, shards, -0.22, 0.18)
    return jnp.clip(drawn, -bound, bound).astype(held_as)


def setup_inputs(seed: int = 0, part: int = 0) -> dict:
    seeds = jax.random.split(jax.random.key(seed), 6)
    own_keys = jax.random.split(jax.random.fold_in(seeds[5], part), 6)
    return {
        "object_field": scatter_about(own_keys[0], (2, NY, NX), 0.7, 5.0, ((1, 16),), jnp.float32),
        "probe_field": scatter_about(own_keys[1], (2, PS, PS), 0.5, 4.0, (), jnp.float32),
        "scan_offsets": draw_scan_offsets(jax.random.fold_in(jax.random.fold_in(seeds[5], part), 71), part),
        "tile_counts": draw_tile_counts(jax.random.fold_in(jax.random.fold_in(seeds[5], part), 71), part),
        "measured": jnp.clip(jnp.exp(math.log(2.0) - 2.9957323 * jax.random.uniform(own_keys[4], (POSITIONS, PS, PS), jnp.float32) ** shard_levels(own_keys[4], (POSITIONS, PS, PS), ((0, 16),), -0.2, 0.2)), 0.1, 2.0),
    }


def reference(object_field, probe_field, scan_offsets, tile_counts, measured):
    total = scan_offsets.shape[0]
    numbers = jnp.arange(total, dtype=jnp.int32)
    live = (numbers % CAP < tile_counts[numbers // CAP]).astype(jnp.float32)
    count = jnp.sum(live)
    zero = jnp.zeros((), jnp.int32)
    current = object_field
    probe_now = probe_field
    for iteration in range(ITERS):
        probe_complex = lax.complex(probe_now[0], probe_now[1])

        def visit(carry, item):
            grad_object, grad_probe = carry
            offset, intensity, weight = item
            anchor = (zero, offset[0].astype(jnp.int32), offset[1].astype(jnp.int32))
            window = lax.dynamic_slice(current, anchor, (2, PS, PS))
            window_complex = lax.complex(window[0], window[1])
            far_field = jnp.fft.fft2(probe_complex * window_complex, norm="ortho")
            misfit = (jnp.real(far_field) * jnp.real(far_field) + jnp.imag(far_field) * jnp.imag(far_field) - intensity) * weight
            back_field = jnp.fft.ifft2(misfit * far_field, norm="ortho")
            object_term = jnp.conj(probe_complex) * back_field
            probe_term = jnp.conj(window_complex) * back_field
            block = lax.dynamic_slice(grad_object, anchor, (2, PS, PS))
            block = block + jnp.stack([jnp.real(object_term), jnp.imag(object_term)])
            grad_object = lax.dynamic_update_slice(grad_object, block, anchor)
            grad_probe = grad_probe + jnp.stack([jnp.real(probe_term), jnp.imag(probe_term)])
            return (grad_object, grad_probe), weight

        start = (jnp.zeros_like(current), jnp.zeros_like(probe_now))
        (grad_object, grad_probe), unused = lax.scan(visit, start, (scan_offsets, measured, live))
        peak = jnp.max(probe_now[0] * probe_now[0] + probe_now[1] * probe_now[1])
        current = current - (2.0 / peak) * grad_object
        probe_now = probe_now - (4.0 / count) * grad_probe
    return current, probe_now
```

```python
import functools
import math

import jax
import jax.numpy as jnp
import ml_dtypes
import numpy as np
from jax import lax
from jax.experimental import pallas as pl
from jax.experimental.pallas import tpu as pltpu
from jax.sharding import PartitionSpec as P

ITERS = 2
PS = 256
HALF = 128
F32 = jnp.float32
BF16 = jnp.bfloat16


def split_table(table):
    high = table.astype(np.float32).astype(ml_dtypes.bfloat16)
    low = (table - high.astype(np.float64)).astype(np.float32).astype(ml_dtypes.bfloat16)
    return np.stack([high, low])


def dft_tables():
    points, bins = np.arange(HALF)[:, None], np.arange(HALF)[None, :]
    found = []
    for odd in (0, 1):
        phase = (points * (2 * bins + odd)) % PS
        angle = phase * (-2.0 * math.pi / PS)
        real, imag = np.cos(angle) / 16.0, np.sin(angle) / 16.0
        found.append(np.block([[real, imag], [-imag, real]]))
    even, odd = found
    return np.stack([split_table(t) for t in (even, even.T, odd, odd.T)])


def sort_table():
    table = np.zeros((PS, PS), np.float32)
    for k in range(HALF):
        table[2 * k, k] = 1.0
        table[2 * k + 1, HALF + k] = 1.0
    return table.astype(ml_dtypes.bfloat16)


def dot(a, b):
    return jnp.dot(a, b, preferred_element_type=F32)


def halves(x):
    high = x.astype(BF16)
    low = (x - high.astype(F32)).astype(BF16)
    return high, low


def times_right(x, table):
    high, low = halves(x)
    t_high, t_low = table[0], table[1]
    return dot(jnp.concatenate([high, low, high], 1), jnp.concatenate([t_high, t_high, t_low], 0))


def times_left(table, x):
    high, low = halves(x)
    t_high, t_low = table[0], table[1]
    return dot(jnp.concatenate([t_high, t_high, t_low], 1), jnp.concatenate([high, low, high], 0))


def lane(shape):
    return lax.broadcasted_iota(jnp.int32, shape, len(shape) - 1)


def row(shape):
    return lax.broadcasted_iota(jnp.int32, shape, len(shape) - 2)


def wrapped_columns(first, second, third, column):
    start = column % HALF
    side = (column // HALF) % 2
    mixed = jnp.where(lane(first.shape) >= start, first, third)
    left = jnp.where(side == 0, mixed, second)
    right = jnp.where(side == 0, second, mixed)
    return jnp.concatenate([left, right], axis=-1)


def column_specs(height, steps, at, blocks):
    def spec(step):
        def index(j, places):
            return (0, 0, jnp.minimum(places[at + 2 * j + 1] // HALF + step, blocks - 1))

        return pl.BlockSpec((2, height, HALF), index)

    return [spec(step) for step in range(steps)]


def pack_kernel(places, first, second, third, out):
    j = pl.program_id(0)
    column = places[2 * j + 1]
    out[0] = wrapped_columns(first[...], second[...], third[...], column)


def pack(places, current):
    slots = (places.shape[0] - 1) // 2
    blocks = current.shape[2] // HALF
    return pl.pallas_call(
        pack_kernel,
        out_shape=jax.ShapeDtypeStruct((slots, 2, PS, PS), F32),
        grid_spec=pltpu.PrefetchScalarGridSpec(
            num_scalar_prefetch=1,
            grid=(slots,),
            in_specs=column_specs(PS, 3, 0, blocks),
            out_specs=pl.BlockSpec((1, 2, PS, PS), lambda j, places: (j, 0, 0, 0)),
        ),
        name="pack_rows",
    )(places, current, current, current)


def sort_kernel(table, measured, out):
    high = measured[0].astype(BF16)
    rest = measured[0] - high.astype(F32)
    middle = rest.astype(BF16)
    low = (rest - middle.astype(F32)).astype(BF16)
    by_column = dot(high, table[...]) + dot(middle, table[...]) + dot(low, table[...])
    high = by_column.astype(BF16)
    rest = by_column - high.astype(F32)
    middle = rest.astype(BF16)
    low = (rest - middle.astype(F32)).astype(BF16)
    turned = table[...].T
    out[0] = dot(turned, high) + dot(turned, middle) + dot(turned, low)


def sort_measured(measured):
    slots = measured.shape[0]
    return pl.pallas_call(
        sort_kernel,
        out_shape=jax.ShapeDtypeStruct(measured.shape, F32),
        grid=(slots,),
        in_specs=[pl.BlockSpec((PS, PS), lambda j: (0, 0)), pl.BlockSpec((1, PS, PS), lambda j: (j, 0, 0))],
        out_specs=pl.BlockSpec((1, PS, PS), lambda j: (j, 0, 0)),
        cost_estimate=pl.CostEstimate(flops=slots * 6 * 2 * PS**3, bytes_accessed=slots * 2 * PS * PS * 4, transcendentals=0),
        name="sort_measured",
    )(sort_table(), measured)


def forward(real, imag, even, even_t, odd, odd_t):
    near = jnp.concatenate([real[:, :HALF] + real[:, HALF:], imag[:, :HALF] + imag[:, HALF:]], 1)
    far = jnp.concatenate([real[:, :HALF] - real[:, HALF:], imag[:, :HALF] - imag[:, HALF:]], 1)
    e = times_right(near, even)
    o = times_right(far, odd)
    e_sum, e_dif = e[:HALF] + e[HALF:], e[:HALF] - e[HALF:]
    o_sum, o_dif = o[:HALF] + o[HALF:], o[:HALF] - o[HALF:]

    def stack(first, second):
        return jnp.concatenate(
            [
                jnp.concatenate([first[:, :HALF], second[:, :HALF]], 1),
                jnp.concatenate([first[:, HALF:], second[:, HALF:]], 1),
            ],
            0,
        )

    return times_left(even_t, stack(e_sum, o_sum)), times_left(odd_t, stack(e_dif, o_dif))


def backward(rows_even, rows_odd, even, even_t, odd, odd_t):
    e = times_left(even, rows_even)
    o = times_left(odd, rows_odd)
    top, bottom = e + o, e - o

    def gather(lanes):
        return jnp.concatenate(
            [
                jnp.concatenate([top[:HALF, lanes], top[HALF:, lanes]], 1),
                jnp.concatenate([bottom[:HALF, lanes], bottom[HALF:, lanes]], 1),
            ],
            0,
        )

    e = times_right(gather(slice(0, HALF)), even_t)
    o = times_right(gather(slice(HALF, PS)), odd_t)
    plus, minus = e + o, e - o
    real = jnp.concatenate([plus[:, :HALF], minus[:, :HALF]], 1)
    imag = jnp.concatenate([plus[:, HALF:], minus[:, HALF:]], 1)
    return real, imag


def turn(x, rows, columns):
    return pltpu.roll(pltpu.roll(x, rows, 0), columns, 1)


def slot_kernel(places, first, second, third, halo, probe, measured, tables, grad, grad_probe):
    j = pl.program_id(0)
    row_at, column = places[2 * j], places[2 * j + 1]

    @pl.when(j == 0)
    def _():
        grad_probe[...] = jnp.zeros_like(grad_probe)

    @pl.when(j < places[2 * pl.num_programs(0)])
    def _():
        own = wrapped_columns(first[...], second[...], third[...], column)
        window = jnp.where(row(own.shape) >= row_at, own, halo[0])
        w_real, w_imag = window[0], window[1]
        right = column % PS
        p_real, p_imag = turn(probe[0], row_at, right), turn(probe[1], row_at, right)
        exit_real = p_real * w_real - p_imag * w_imag
        exit_imag = p_real * w_imag + p_imag * w_real
        even, even_t, odd, odd_t = tables[0], tables[1], tables[2], tables[3]
        far_even, far_odd = forward(exit_real, exit_imag, even, even_t, odd, odd_t)

        def misfit(far, seen):
            real, imag = far[:HALF], far[HALF:]
            weight = real * real + imag * imag - seen
            return jnp.concatenate([weight * real, weight * imag], 0)

        back_real, back_imag = backward(
            misfit(far_even, measured[0, :HALF]), misfit(far_odd, measured[0, HALF:]), even, even_t, odd, odd_t
        )
        grad[0, 0] = p_real * back_real + p_imag * back_imag
        grad[0, 1] = p_real * back_imag - p_imag * back_real
        down, left = (PS - row_at) % PS, (PS - right) % PS
        grad_probe[0] += turn(w_real * back_real + w_imag * back_imag, down, left)
        grad_probe[1] += turn(w_real * back_imag - w_imag * back_real, down, left)


def slot_gradients(places, current, halo, probe, measured, tables):
    slots = measured.shape[0]
    blocks = current.shape[2] // HALF
    return pl.pallas_call(
        slot_kernel,
        out_shape=(
            jax.ShapeDtypeStruct((slots, 2, PS, PS), F32),
            jax.ShapeDtypeStruct((2, PS, PS), F32),
        ),
        grid_spec=pltpu.PrefetchScalarGridSpec(
            num_scalar_prefetch=1,
            grid=(slots,),
            in_specs=column_specs(PS, 3, 0, blocks)
            + [
                pl.BlockSpec((1, 2, PS, PS), lambda j, places: (j, 0, 0, 0)),
                pl.BlockSpec((2, PS, PS), lambda j, places: (0, 0, 0)),
                pl.BlockSpec((1, PS, PS), lambda j, places: (j, 0, 0)),
                pl.BlockSpec((4, 2, PS, PS), lambda j, places: (0, 0, 0, 0)),
            ],
            out_specs=[
                pl.BlockSpec((1, 2, PS, PS), lambda j, places: (j, 0, 0, 0)),
                pl.BlockSpec((2, PS, PS), lambda j, places: (0, 0, 0)),
            ],
        ),
        compiler_params=pltpu.CompilerParams(vmem_limit_bytes=40 * 1024 * 1024),
        name="slot_gradients",
    )(places, current, current, current, halo, probe, measured, tables)


def merge_kernel(places, above, scale, current, own, arriving, out):
    slots = own.shape[0]
    out[...] = current[...]
    factor = scale[0]

    def place(j, source, block, keep_rows, row_at, column):
        start, at = column % HALF, column // HALF
        side = at % 2

        def add(step, keep):
            part = jnp.where((side + step) % 2 == 0, block[:, :, :HALF], block[:, :, HALF:])
            cells = pl.ds(pl.multiple_of(jnp.minimum(at + step, out.shape[2] // HALF - 1) * HALF, HALF), HALF)
            out[:, :, cells] -= jnp.where(keep, part, 0.0) * factor

        lanes = lane((2, PS, HALF))
        add(0, keep_rows & (lanes >= start))
        add(1, keep_rows)
        add(2, keep_rows & (lanes < start))

    rows = row((2, PS, HALF))

    def one(j, carry):
        @pl.when(j < places[2 * slots])
        def _():
            row_at = places[2 * j]
            place(j, own, own[j], rows >= row_at, row_at, places[2 * j + 1])

        @pl.when(j < above[2 * slots])
        def _():
            row_at = above[2 * j]
            place(j, arriving, arriving[j], rows < row_at, row_at, above[2 * j + 1])

        return carry

    lax.fori_loop(0, slots, one, 0)


def merge(places, above, scale, current, own, arriving):
    whole = pl.BlockSpec(memory_space=pltpu.VMEM)
    scalars = pl.BlockSpec(memory_space=pltpu.SMEM)
    return pl.pallas_call(
        merge_kernel,
        out_shape=jax.ShapeDtypeStruct(current.shape, F32),
        in_specs=[scalars, scalars, scalars, whole, whole, whole],
        out_specs=whole,
        compiler_params=pltpu.CompilerParams(vmem_limit_bytes=40 * 1024 * 1024),
        name="merge_gradients",
    )(places, above, scale, current, own, arriving)


def shifted(value, steps):
    count = lax.axis_size("ty")
    first, last = (max(0, -steps), min(count, count - steps))
    return lax.ppermute(value, "ty", [(source, source + steps) for source in range(first, last)])


def total_over_tiles(value):
    count = lax.axis_size("ty")
    if count & (count - 1) or value.shape[0] % count:
        return lax.psum(value, "ty")
    me = lax.axis_index("ty")
    bits = [1 << k for k in range(count.bit_length() - 1)]
    for bit in bits:
        half = value.shape[0] // 2
        side = (me // bit) % 2
        kept = lax.dynamic_slice_in_dim(value, side * half, half, 0)
        sent = lax.dynamic_slice_in_dim(value, (1 - side) * half, half, 0)
        value = kept + lax.ppermute(sent, "ty", [(i, i ^ bit) for i in range(count)])
    for bit in reversed(bits):
        side = (me // bit) % 2
        other = lax.ppermute(value, "ty", [(i, i ^ bit) for i in range(count)])
        value = jnp.where(side == 0, jnp.concatenate([value, other]), jnp.concatenate([other, value]))
    return value


def on_device(object_field, probe_field, scan_offsets, tile_counts, measured):
    rows = object_field.shape[1]
    used = tile_counts[0]
    local_rows = scan_offsets[:, 0] - lax.axis_index("ty") * rows
    places = jnp.concatenate([jnp.stack([local_rows, scan_offsets[:, 1]], 1).reshape(-1), tile_counts])
    above = shifted(places, 1)
    tables = jnp.asarray(dft_tables())
    seen = sort_measured(measured)
    count = lax.psum(used.astype(F32), "ty")
    current, probe_now = object_field, probe_field
    for iteration in range(ITERS):
        halo = shifted(pack(above, current), -1)
        grads, grad_probe = slot_gradients(places, current, halo, probe_now, seen, tables)
        arriving = shifted(grads, 1)
        total_probe = total_over_tiles(grad_probe.reshape(2 * PS, PS)).reshape(2, PS, PS)
        peak = jnp.max(probe_now[0] * probe_now[0] + probe_now[1] * probe_now[1])
        current = merge(places, above, (2.0 / peak).reshape(1), current, grads, arriving)
        probe_now = probe_now - 4.0 / count * total_probe
    return (current, probe_now)


def solution(mesh):
    return jax.shard_map(
        on_device,
        mesh=mesh,
        in_specs=(
            P(None, ("groups", "ty"), None),
            P("groups", None, None),
            P(("groups", "ty"), None),
            P(("groups", "ty")),
            P(("groups", "ty"), None, None),
        ),
        out_specs=(P(None, ("groups", "ty"), None), P("groups", None, None)),
        check_vma=False,
    )
```

```python
import functools
import math

import jax
import jax.numpy as jnp
import ml_dtypes
import numpy as np
from jax import lax
from jax.experimental import pallas as pl
from jax.experimental.pallas import tpu as pltpu
from jax.sharding import PartitionSpec as P

ITERS = 2
PS = 256
STEP = 16
FIRST = 512
VMEM_LIMIT = 48 * 1024 * 1024
HALF = 128
F32 = jnp.float32
BF16 = jnp.bfloat16


def split_table(table):
    high = table.astype(np.float32).astype(ml_dtypes.bfloat16)
    low = (table - high.astype(np.float64)).astype(np.float32).astype(ml_dtypes.bfloat16)
    return np.stack([high, low])


def dft_tables():
    points, bins = np.arange(HALF)[:, None], np.arange(HALF)[None, :]
    found = []
    for odd in (0, 1):
        phase = (points * (2 * bins + odd)) % PS
        angle = phase * (-2.0 * math.pi / PS)
        real, imag = np.cos(angle) / 16.0, np.sin(angle) / 16.0
        found.append(np.block([[real, imag], [-imag, real]]))
    even, odd = found
    return np.stack([split_table(t) for t in (even, even.T, odd, odd.T)])


def sort_table():
    table = np.zeros((PS, PS), np.float32)
    for k in range(HALF):
        table[2 * k, k] = 1.0
        table[2 * k + 1, HALF + k] = 1.0
    return table.astype(ml_dtypes.bfloat16)


def dot(a, b):
    return jnp.dot(a, b, preferred_element_type=F32)


def halves(x):
    high = x.astype(BF16)
    low = (x - high.astype(F32)).astype(BF16)
    return high, low


def times_right(x, table):
    high, low = halves(x)
    t_high, t_low = table[0], table[1]
    return dot(jnp.concatenate([high, low, high], 1), jnp.concatenate([t_high, t_high, t_low], 0))


def times_left(table, x):
    high, low = halves(x)
    t_high, t_low = table[0], table[1]
    return dot(jnp.concatenate([t_high, t_high, t_low], 1), jnp.concatenate([high, low, high], 0))


def lane(shape):
    return lax.broadcasted_iota(jnp.int32, shape, len(shape) - 1)


def row(shape):
    return lax.broadcasted_iota(jnp.int32, shape, len(shape) - 2)


def wrapped(mixed_first, whole, mixed_last, column):
    side = (column // HALF) % 2
    mixed = jnp.where(lane(mixed_first.shape) >= column % HALF, mixed_first, mixed_last)
    return jnp.where(side == 0, mixed, whole), jnp.where(side == 0, whole, mixed)


def cells(column, step, width):
    at = jnp.minimum(column // HALF + step, width // HALF - 1)
    return pl.ds(pl.multiple_of(at * HALF, HALF), HALF)


def load_wrapped(ref, plane, rows, column):
    blocks = [ref[plane, rows, cells(column, step, ref.shape[2])] for step in range(3)]
    return jnp.concatenate(wrapped(*blocks, column), axis=1)


def add_wrapped(ref, plane, rows, column, value):
    side, start = (column // HALF) % 2, column % HALF
    left, right = value[:, :HALF], value[:, HALF:]
    mixed = jnp.where(side == 0, left, right)
    other = jnp.where(side == 0, right, left)
    lanes = lane(mixed.shape)
    for step, part in ((0, jnp.where(lanes >= start, mixed, 0.0)), (1, other), (2, jnp.where(lanes < start, mixed, 0.0))):
        ref[plane, rows, cells(column, step, ref.shape[2])] += part


def up(value):
    return (value + STEP - 1) // STEP * STEP


def lengths(upper, lower, j):
    slots = (upper.shape[0] - 1) // 2
    reach, column = upper[2 * j], upper[2 * j + 1]
    first = reach
    for k in range(slots):
        near = (jnp.abs(lower[2 * k + 1] - column) < PS) & (k < lower[2 * slots])
        first = jnp.where(near, jnp.minimum(first, lower[2 * k]), first)
    live = j < upper[2 * slots]
    whole = jnp.where(live, up(reach), 0)
    shared = jnp.where(live & (first < reach), first // STEP * STEP, whole)
    return whole, shared


def each_piece(upper, lower, body):
    slots = (upper.shape[0] - 1) // 2

    def one(j, carry):
        at, at_shared = carry
        whole, shared = lengths(upper, lower, j)

        def piece(i, unused):
            body(j, pl.multiple_of(i * STEP, STEP), pl.multiple_of(at + i * STEP, STEP), pl.multiple_of(at_shared + i * STEP - shared, STEP), i * STEP >= shared)
            return unused

        lax.fori_loop(0, whole // STEP, piece, 0)
        return at + whole, at_shared + whole - shared

    return lax.fori_loop(0, slots, one, (0, 0))


def whole_spec(space):
    return pl.BlockSpec(memory_space=space)


VM, SM = pltpu.VMEM, pltpu.SMEM


def pack_kernel(mine, above, below, current, out, sizes):
    def piece(j, at, place, at_shared, is_shared):
        rows = pl.ds(at, STEP)
        for plane in range(2):
            out[pl.ds(place, STEP), plane * PS : (plane + 1) * PS] = load_wrapped(current, plane, rows, above[2 * j + 1])

    all_above, shared_above = each_piece(above, mine, piece)
    slots = (mine.shape[0] - 1) // 2

    def count(j, carry):
        whole, shared = lengths(mine, below, j)
        return carry[0] + whole, carry[1] + whole - shared

    all_below, shared_below = lax.fori_loop(0, slots, count, (0, 0))
    sizes[0], sizes[1], sizes[2], sizes[3] = all_above, shared_above, all_below, shared_below


def pack(mine, above, below, current):
    slots = (mine.shape[0] - 1) // 2
    return pl.pallas_call(
        pack_kernel,
        out_shape=(jax.ShapeDtypeStruct((slots * PS, 2 * PS), F32), jax.ShapeDtypeStruct((4,), jnp.int32)),
        in_specs=[whole_spec(SM)] * 3 + [whole_spec(VM)],
        out_specs=(whole_spec(VM), whole_spec(SM)),
        compiler_params=pltpu.CompilerParams(vmem_limit_bytes=VMEM_LIMIT),
        name="pack_rows",
    )(mine, above, below, current)


def sort_kernel(table, measured, out):
    high = measured[0].astype(BF16)
    rest = measured[0] - high.astype(F32)
    middle = rest.astype(BF16)
    low = (rest - middle.astype(F32)).astype(BF16)
    by_column = dot(high, table[...]) + dot(middle, table[...]) + dot(low, table[...])
    high = by_column.astype(BF16)
    rest = by_column - high.astype(F32)
    middle = rest.astype(BF16)
    low = (rest - middle.astype(F32)).astype(BF16)
    turned = table[...].T
    out[0] = dot(turned, high) + dot(turned, middle) + dot(turned, low)


def sort_measured(measured):
    slots = measured.shape[0]
    return pl.pallas_call(
        sort_kernel,
        out_shape=jax.ShapeDtypeStruct(measured.shape, F32),
        grid=(slots,),
        in_specs=[pl.BlockSpec((PS, PS), lambda j: (0, 0)), pl.BlockSpec((1, PS, PS), lambda j: (j, 0, 0))],
        out_specs=pl.BlockSpec((1, PS, PS), lambda j: (j, 0, 0)),
        cost_estimate=pl.CostEstimate(flops=slots * 6 * 2 * PS**3, bytes_accessed=slots * 2 * PS * PS * 4, transcendentals=0),
        name="sort_measured",
    )(sort_table(), measured)


def forward(real, imag, even, even_t, odd, odd_t):
    near = jnp.concatenate([real[:, :HALF] + real[:, HALF:], imag[:, :HALF] + imag[:, HALF:]], 1)
    far = jnp.concatenate([real[:, :HALF] - real[:, HALF:], imag[:, :HALF] - imag[:, HALF:]], 1)
    e = times_right(near, even)
    o = times_right(far, odd)
    e_sum, e_dif = e[:HALF] + e[HALF:], e[:HALF] - e[HALF:]
    o_sum, o_dif = o[:HALF] + o[HALF:], o[:HALF] - o[HALF:]

    def stack(first, second):
        return jnp.concatenate(
            [
                jnp.concatenate([first[:, :HALF], second[:, :HALF]], 1),
                jnp.concatenate([first[:, HALF:], second[:, HALF:]], 1),
            ],
            0,
        )

    return times_left(even_t, stack(e_sum, o_sum)), times_left(odd_t, stack(e_dif, o_dif))


def backward(rows_even, rows_odd, even, even_t, odd, odd_t):
    e = times_left(even, rows_even)
    o = times_left(odd, rows_odd)
    top, bottom = e + o, e - o

    def gather(lanes):
        return jnp.concatenate(
            [
                jnp.concatenate([top[:HALF, lanes], top[HALF:, lanes]], 1),
                jnp.concatenate([bottom[:HALF, lanes], bottom[HALF:, lanes]], 1),
            ],
            0,
        )

    e = times_right(gather(slice(0, HALF)), even_t)
    o = times_right(gather(slice(HALF, PS)), odd_t)
    plus, minus = e + o, e - o
    real = jnp.concatenate([plus[:, :HALF], minus[:, :HALF]], 1)
    imag = jnp.concatenate([plus[:, HALF:], minus[:, HALF:]], 1)
    return real, imag


def turn(x, rows, columns):
    return pltpu.roll(pltpu.roll(x, rows, 0), columns, 1)


def turn(x, rows, columns):
    return pltpu.roll(pltpu.roll(x, rows, 0), columns, 1)


def slot_kernel(has_base, mine, below, scale, current, halo, probe, measured, tables, *rest):
    base = rest[0] if has_base else None
    out, leaving, grad_probe = rest[has_base:]
    slots = measured.shape[0]
    out[...] = current[...]
    grad_probe[...] = jnp.zeros_like(grad_probe)
    factor = scale[0]

    def one(j, at):
        reach, column = mine[2 * j], mine[2 * j + 1]
        whole, shared = lengths(mine, below, j)
        place = pl.ds(pl.multiple_of(at, STEP), PS)
        rows = row((PS, PS))
        inside = rows >= reach
        all_rows = pl.ds(0, PS)
        w_real = jnp.where(inside, load_wrapped(current, 0, all_rows, column), halo[place, :PS])
        w_imag = jnp.where(inside, load_wrapped(current, 1, all_rows, column), halo[place, PS:])
        right = column % PS
        p_real, p_imag = turn(probe[0], reach, right), turn(probe[1], reach, right)
        exit_real = p_real * w_real - p_imag * w_imag
        exit_imag = p_real * w_imag + p_imag * w_real
        even, even_t, odd, odd_t = tables[0], tables[1], tables[2], tables[3]
        far_even, far_odd = forward(exit_real, exit_imag, even, even_t, odd, odd_t)

        def misfit(far, seen):
            real, imag = far[:HALF], far[HALF:]
            weight = real * real + imag * imag - seen
            return jnp.concatenate([weight * real, weight * imag], 0)

        back_real, back_imag = backward(
            misfit(far_even, measured[j, :HALF]), misfit(far_odd, measured[j, HALF:]), even, even_t, odd, odd_t
        )
        down, left = (PS - reach) % PS, (PS - right) % PS
        grad_probe[0] += turn(w_real * back_real + w_imag * back_imag, down, left)
        grad_probe[1] += turn(w_real * back_imag - w_imag * back_real, down, left)
        changes = (p_real * back_real + p_imag * back_imag) * -factor, (p_real * back_imag - p_imag * back_real) * -factor
        for plane, change in enumerate(changes):
            lanes = slice(plane * PS, (plane + 1) * PS)
            add_wrapped(out, plane, all_rows, column, jnp.where(inside, change, 0.0))
            below_part = jnp.where(inside, 0.0, change)
            if has_base:
                below_part += jnp.where(rows < shared, base[place, lanes], 0.0)
            leaving[place, lanes] = below_part
        return at + whole

    lax.fori_loop(0, mine[2 * slots], one, 0)


def visit_slots(mine, below, scale, current, halo, probe, measured, tables, base=None):
    operands = (mine, below, scale, current, halo, probe, measured, tables) + (() if base is None else (base,))
    return pl.pallas_call(
        functools.partial(slot_kernel, int(base is not None)),
        out_shape=(
            jax.ShapeDtypeStruct(current.shape, F32),
            jax.ShapeDtypeStruct(halo.shape, F32),
            jax.ShapeDtypeStruct(probe.shape, F32),
        ),
        in_specs=[whole_spec(SM)] * 3 + [whole_spec(VM)] * (len(operands) - 3),
        out_specs=(whole_spec(VM),) * 3,
        compiler_params=pltpu.CompilerParams(vmem_limit_bytes=VMEM_LIMIT),
        name="visit_slots",
    )(*operands)


def exchange_kernel(is_odd, mine, above, below, changed, leaving, cross_first, cross_rest, core_first, core_rest):
    def store(firsts, rests, to_cross, place, value):
        (cross_a, core_a), (cross_b, core_b) = firsts, rests
        here = place < FIRST

        def put(condition, ref, at):
            @pl.when(condition)
            def _():
                ref[pl.ds(pl.multiple_of(at, STEP), STEP), :] = value

        put(to_cross & here, cross_a, place)
        put(to_cross & ~here, cross_b, place - FIRST)
        put(~to_cross & here, core_a, place)
        put(~to_cross & ~here, core_b, place - FIRST)

    odd = is_odd[0] == 1
    refs = (cross_first, core_first), (cross_rest, core_rest)

    def rising(j, at, place, at_shared, is_shared):
        @pl.when(is_shared)
        def _():
            rows = pl.ds(at, STEP)
            planes = [load_wrapped(changed, plane, rows, above[2 * j + 1]) for plane in range(2)]
            store(*refs, ~odd, at_shared, jnp.concatenate(planes, axis=1))

    each_piece(above, mine, rising)

    def falling(j, at, place, at_shared, is_shared):
        @pl.when(is_shared)
        def _():
            store(*refs, odd, at_shared, leaving[pl.ds(place, STEP), :])

    each_piece(mine, below, falling)


def gather_exchange(is_odd, mine, above, below, changed, leaving):
    total, width = leaving.shape
    shapes = [jax.ShapeDtypeStruct((rows, width), F32) for rows in (FIRST, total - FIRST)] * 2
    return pl.pallas_call(
        exchange_kernel,
        out_shape=shapes,
        in_specs=[whole_spec(SM)] * 4 + [whole_spec(VM)] * 2,
        out_specs=[whole_spec(VM)] * 4,
        compiler_params=pltpu.CompilerParams(vmem_limit_bytes=VMEM_LIMIT),
        name="gather_exchange",
    )(is_odd, mine, above, below, changed, leaving)


def absorb_kernel(is_odd, mine, above, below, changed, halo, leaving, cross_first, cross_rest, core_first, core_rest, out, out_halo, under):
    odd = is_odd[0] == 1
    out[...] = changed[...]
    under[...] = jnp.zeros_like(under)

    def load(from_cross, place):
        near = pl.ds(pl.multiple_of(jnp.minimum(place, FIRST - STEP), STEP), STEP)
        far = pl.ds(pl.multiple_of(jnp.maximum(place - FIRST, 0), STEP), STEP)
        cross = jnp.where(place < FIRST, cross_first[near, :], cross_rest[far, :])
        core = jnp.where(place < FIRST, core_first[near, :], core_rest[far, :])
        return jnp.where(from_cross, cross, core)

    def from_above(j, at, place, at_shared, is_shared):
        @pl.when(is_shared)
        def _():
            part = load(~odd, at_shared)
            for plane in range(2):
                add_wrapped(out, plane, pl.ds(at, STEP), above[2 * j + 1], part[:, plane * PS : (plane + 1) * PS])

    each_piece(above, mine, from_above)

    def sum_under(j, at, place, at_shared, is_shared):
        for plane in range(2):
            part = leaving[pl.ds(place, STEP), plane * PS : (plane + 1) * PS]
            add_wrapped(under, plane, pl.ds(at, STEP), mine[2 * j + 1], part)

    each_piece(mine, below, sum_under)

    def renew(j, at, place, at_shared, is_shared):
        rows = pl.ds(place, STEP)
        kept = halo[rows, :]
        new = load(odd, jnp.maximum(at_shared, 0))
        changes = [load_wrapped(under, plane, pl.ds(at, STEP), mine[2 * j + 1]) for plane in range(2)]
        out_halo[rows, :] = jnp.where(is_shared, new, kept) + jnp.concatenate(changes, axis=1)

    each_piece(mine, below, renew)


def absorb_exchange(is_odd, mine, above, below, changed, halo, leaving, pieces):
    return pl.pallas_call(
        absorb_kernel,
        out_shape=(jax.ShapeDtypeStruct(changed.shape, F32), jax.ShapeDtypeStruct(halo.shape, F32)),
        in_specs=[whole_spec(SM)] * 4 + [whole_spec(VM)] * 7,
        out_specs=[whole_spec(VM)] * 2,
        scratch_shapes=[pltpu.VMEM(changed.shape, F32)],
        compiler_params=pltpu.CompilerParams(vmem_limit_bytes=VMEM_LIMIT),
        name="absorb_exchange",
    )(is_odd, mine, above, below, changed, halo, leaving, *pieces)


def finish_kernel(mine, above, changed, arriving, out):
    out[...] = changed[...]

    def piece(j, at, place, at_shared, is_shared):
        for plane in range(2):
            part = arriving[pl.ds(place, STEP), plane * PS : (plane + 1) * PS]
            add_wrapped(out, plane, pl.ds(at, STEP), above[2 * j + 1], part)

    each_piece(above, mine, piece)


def finish(mine, above, changed, arriving):
    return pl.pallas_call(
        finish_kernel,
        out_shape=jax.ShapeDtypeStruct(changed.shape, F32),
        in_specs=[whole_spec(SM)] * 2 + [whole_spec(VM)] * 2,
        out_specs=whole_spec(VM),
        compiler_params=pltpu.CompilerParams(vmem_limit_bytes=VMEM_LIMIT),
        name="add_arriving",
    )(mine, above, changed, arriving)


def shifted(value, steps):
    count = lax.axis_size("ty")
    first, last = (max(0, -steps), min(count, count - steps))
    return lax.ppermute(value, "ty", [(source, source + steps) for source in range(first, last)])


def swapped(value, first):
    pairs = [(k, k + 1) for k in range(first, lax.axis_size("ty") - 1, 2)]
    return lax.ppermute(value, "ty", pairs + [(b, a) for a, b in pairs])


def total_over_tiles(value, used):
    count = lax.axis_size("ty")
    if count & (count - 1) or value.shape[0] % count:
        return lax.psum((value, used), "ty")
    me = lax.axis_index("ty")
    bits = [1 << k for k in range(count.bit_length() - 1)]
    extra = jnp.full((8, value.shape[1]), used)
    for bit in bits:
        half = value.shape[0] // 2
        side = (me // bit) % 2
        kept = lax.dynamic_slice_in_dim(value, side * half, half, 0)
        sent = lax.dynamic_slice_in_dim(value, (1 - side) * half, half, 0)
        got = lax.ppermute(jnp.concatenate([sent, extra]), "ty", [(i, i ^ bit) for i in range(count)])
        value, extra = kept + got[:half], extra + got[half:]
    for bit in reversed(bits):
        side = (me // bit) % 2
        other = lax.ppermute(value, "ty", [(i, i ^ bit) for i in range(count)])
        value = jnp.where(side == 0, jnp.concatenate([value, other]), jnp.concatenate([other, value]))
    return value, extra[0, 0]


def on_device(object_field, probe_field, scan_offsets, tile_counts, measured):
    rows = object_field.shape[1]
    tile = lax.axis_index("ty")
    is_odd = (tile % 2).reshape(1)
    local_rows = scan_offsets[:, 0] - tile * rows
    mine = jnp.concatenate([jnp.stack([local_rows, scan_offsets[:, 1]], 1).reshape(-1), tile_counts])
    above, below = shifted(mine, 1), shifted(mine, -1)
    tables = jnp.asarray(dft_tables())
    packed, sizes = pack(mine, above, below, object_field)
    halo = shifted(packed, -1)
    seen = sort_measured(measured)
    used = tile_counts[0].astype(F32)

    def step_of(probe):
        return (2.0 / jnp.max(probe[0] * probe[0] + probe[1] * probe[1])).reshape(1)

    def moved(probe, grad_probe, number):
        total, number = total_over_tiles(grad_probe.reshape(2 * PS, PS), number)
        return probe - 4.0 / number * total.reshape(2, PS, PS)

    changed, leaving, grad_probe = visit_slots(mine, below, step_of(probe_field), object_field, halo, probe_field, seen, tables)
    probe_now = moved(probe_field, grad_probe, used)
    pieces = gather_exchange(is_odd, mine, above, below, changed, leaving)
    cross_shared = jnp.where(is_odd[0] == 1, sizes[3], sizes[1])
    arrived = [
        swapped(pieces[0], 1),
        lax.cond(cross_shared > FIRST, lambda piece: swapped(piece, 1), lambda piece: piece, pieces[1]),
        swapped(pieces[2], 0),
        swapped(pieces[3], 0),
    ]
    current, halo = absorb_exchange(is_odd, mine, above, below, changed, halo, leaving, arrived)
    changed, leaving, grad_probe = visit_slots(mine, below, step_of(probe_now), current, halo, probe_now, seen, tables, leaving)
    probe_now = moved(probe_now, grad_probe, used)
    return finish(mine, above, changed, shifted(leaving, 1)), probe_now


def solution(mesh):
    return jax.shard_map(
        on_device,
        mesh=mesh,
        in_specs=(
            P(None, ("groups", "ty"), None),
            P("groups", None, None),
            P(("groups", "ty"), None),
            P(("groups", "ty")),
            P(("groups", "ty"), None, None),
        ),
        out_specs=(P(None, ("groups", "ty"), None), P("groups", None, None)),
        check_vma=False,
    )
```

```python
import functools
import math

import jax
import jax.numpy as jnp
import ml_dtypes
import numpy as np
from jax import lax
from jax.experimental import pallas as pl
from jax.experimental.pallas import tpu as pltpu
from jax.sharding import PartitionSpec as P

ITERS = 2
PS = 256
STEP = 16
SHARED = 512
CHUNK = 256
SURE = 1024
MIB = 1024 * 1024
VISIT_LIMIT = 44 * MIB
HALF = 128
F32 = jnp.float32
BF16 = jnp.bfloat16


def split_table(table):
    high = table.astype(np.float32).astype(ml_dtypes.bfloat16)
    low = (table - high.astype(np.float64)).astype(np.float32).astype(ml_dtypes.bfloat16)
    return np.stack([high, low])


def dft_tables():
    points, bins = np.arange(HALF)[:, None], np.arange(HALF)[None, :]
    found = []
    for odd in (0, 1):
        phase = (points * (2 * bins + odd)) % PS
        angle = phase * (-2.0 * math.pi / PS)
        real, imag = np.cos(angle) / 16.0, np.sin(angle) / 16.0
        found.append(np.block([[real, imag], [-imag, real]]))
    even, odd = found
    return np.stack([split_table(t) for t in (even, even.T, odd, odd.T)])


def sort_table():
    table = np.zeros((PS, PS), np.float32)
    for k in range(HALF):
        table[2 * k, k] = 1.0
        table[2 * k + 1, HALF + k] = 1.0
    return table.astype(ml_dtypes.bfloat16)


def dot(a, b):
    return jnp.dot(a, b, preferred_element_type=F32)


def halves(x):
    high = x.astype(BF16)
    low = (x - high.astype(F32)).astype(BF16)
    return high, low


def times_right(x, table):
    high, low = halves(x)
    t_high, t_low = table[0], table[1]
    return dot(jnp.concatenate([high, low, high], 1), jnp.concatenate([t_high, t_high, t_low], 0))


def times_left(table, x):
    high, low = halves(x)
    t_high, t_low = table[0], table[1]
    return dot(jnp.concatenate([t_high, t_high, t_low], 1), jnp.concatenate([high, low, high], 0))


def lane(shape):
    return lax.broadcasted_iota(jnp.int32, shape, len(shape) - 1)


def row(shape):
    return lax.broadcasted_iota(jnp.int32, shape, len(shape) - 2)


def wrapped(mixed_first, whole, mixed_last, column):
    side = (column // HALF) % 2
    mixed = jnp.where(lane(mixed_first.shape) >= column % HALF, mixed_first, mixed_last)
    return jnp.where(side == 0, mixed, whole), jnp.where(side == 0, whole, mixed)


def cells(column, step, width):
    at = jnp.minimum(column // HALF + step, width // HALF - 1)
    return pl.ds(pl.multiple_of(at * HALF, HALF), HALF)


def load_wrapped(ref, plane, rows, column):
    blocks = [ref[plane, rows, cells(column, step, ref.shape[2])] for step in range(3)]
    return jnp.concatenate(wrapped(*blocks, column), axis=1)


def add_wrapped(ref, plane, rows, column, value):
    side, start = (column // HALF) % 2, column % HALF
    left, right = value[:, :HALF], value[:, HALF:]
    mixed = jnp.where(side == 0, left, right)
    other = jnp.where(side == 0, right, left)
    lanes = lane(mixed.shape)
    for step, part in ((0, jnp.where(lanes >= start, mixed, 0.0)), (1, other), (2, jnp.where(lanes < start, mixed, 0.0))):
        ref[plane, rows, cells(column, step, ref.shape[2])] += part


def up(value):
    return (value + STEP - 1) // STEP * STEP


def lengths(upper, lower, j):
    slots = (upper.shape[0] - 1) // 2
    reach, column = upper[2 * j], upper[2 * j + 1]
    first = reach
    for k in range(slots):
        near = (jnp.abs(lower[2 * k + 1] - column) < PS) & (k < lower[2 * slots])
        first = jnp.where(near, jnp.minimum(first, lower[2 * k]), first)
    live = j < upper[2 * slots]
    whole = jnp.where(live, up(reach), 0)
    shared = jnp.where(live & (first < reach), first // STEP * STEP, whole)
    return whole, shared


def each_piece(upper, lower, body):
    slots = (upper.shape[0] - 1) // 2

    def one(j, carry):
        at, at_shared = carry
        whole, shared = lengths(upper, lower, j)

        def piece(i, unused):
            body(j, pl.multiple_of(i * STEP, STEP), pl.multiple_of(at + i * STEP, STEP), pl.multiple_of(at_shared + i * STEP - shared, STEP), i * STEP >= shared)
            return unused

        lax.fori_loop(0, whole // STEP, piece, 0)
        return at + whole, at_shared + whole - shared

    return lax.fori_loop(0, slots, one, (0, 0))


def sum_lengths(upper, lower):
    def count(j, carry):
        whole, shared = lengths(upper, lower, j)
        return carry[0] + whole, carry[1] + whole - shared

    return lax.fori_loop(0, (upper.shape[0] - 1) // 2, count, (0, 0))


def whole_spec(space):
    return pl.BlockSpec(memory_space=space)


VM, SM = pltpu.VMEM, pltpu.SMEM


def pack_kernel(mine, above, below, current, sure, rest, sizes):
    def piece(j, at, place, at_shared, is_shared):
        rows = pl.ds(at, STEP)
        planes = [load_wrapped(current, plane, rows, above[2 * j + 1]) for plane in range(2)]
        value = jnp.concatenate(planes, axis=1)

        @pl.when(place < SURE)
        def _():
            sure[pl.ds(place, STEP), :] = value

        @pl.when(place >= SURE)
        def _():
            rest[pl.ds(pl.multiple_of(place - SURE, STEP), STEP), :] = value

    all_above, shared_above = each_piece(above, mine, piece)
    all_below, shared_below = sum_lengths(mine, below)
    sizes[0], sizes[1], sizes[2], sizes[3] = all_above, shared_above, all_below, shared_below


def pack(mine, above, below, current):
    total = (mine.shape[0] - 1) // 2 * PS
    return pl.pallas_call(
        pack_kernel,
        out_shape=(
            jax.ShapeDtypeStruct((SURE, 2 * PS), F32),
            jax.ShapeDtypeStruct((total - SURE, 2 * PS), F32),
            jax.ShapeDtypeStruct((4,), jnp.int32),
        ),
        in_specs=[whole_spec(SM)] * 3 + [whole_spec(VM)],
        out_specs=(whole_spec(VM), whole_spec(VM), whole_spec(SM)),
        compiler_params=pltpu.CompilerParams(vmem_limit_bytes=12 * MIB),
        name="pack_rows",
    )(mine, above, below, current)


def sort_kernel(table, measured, out):
    high = measured[0].astype(BF16)
    rest = measured[0] - high.astype(F32)
    middle = rest.astype(BF16)
    low = (rest - middle.astype(F32)).astype(BF16)
    by_column = dot(high, table[...]) + dot(middle, table[...]) + dot(low, table[...])
    high = by_column.astype(BF16)
    rest = by_column - high.astype(F32)
    middle = rest.astype(BF16)
    low = (rest - middle.astype(F32)).astype(BF16)
    turned = table[...].T
    out[0] = dot(turned, high) + dot(turned, middle) + dot(turned, low)


def sort_measured(measured):
    slots = measured.shape[0]
    return pl.pallas_call(
        sort_kernel,
        out_shape=jax.ShapeDtypeStruct(measured.shape, F32),
        grid=(slots,),
        in_specs=[pl.BlockSpec((PS, PS), lambda j: (0, 0)), pl.BlockSpec((1, PS, PS), lambda j: (j, 0, 0))],
        out_specs=pl.BlockSpec((1, PS, PS), lambda j: (j, 0, 0)),
        cost_estimate=pl.CostEstimate(flops=slots * 6 * 2 * PS**3, bytes_accessed=slots * 2 * PS * PS * 4, transcendentals=0),
        name="sort_measured",
    )(sort_table(), measured)


def forward(real, imag, even, even_t, odd, odd_t):
    near = jnp.concatenate([real[:, :HALF] + real[:, HALF:], imag[:, :HALF] + imag[:, HALF:]], 1)
    far = jnp.concatenate([real[:, :HALF] - real[:, HALF:], imag[:, :HALF] - imag[:, HALF:]], 1)
    e = times_right(near, even)
    o = times_right(far, odd)
    e_sum, e_dif = e[:HALF] + e[HALF:], e[:HALF] - e[HALF:]
    o_sum, o_dif = o[:HALF] + o[HALF:], o[:HALF] - o[HALF:]

    def stack(first, second):
        return jnp.concatenate(
            [
                jnp.concatenate([first[:, :HALF], second[:, :HALF]], 1),
                jnp.concatenate([first[:, HALF:], second[:, HALF:]], 1),
            ],
            0,
        )

    return times_left(even_t, stack(e_sum, o_sum)), times_left(odd_t, stack(e_dif, o_dif))


def backward(rows_even, rows_odd, even, even_t, odd, odd_t):
    e = times_left(even, rows_even)
    o = times_left(odd, rows_odd)
    top, bottom = e + o, e - o

    def gather(lanes):
        return jnp.concatenate(
            [
                jnp.concatenate([top[:HALF, lanes], top[HALF:, lanes]], 1),
                jnp.concatenate([bottom[:HALF, lanes], bottom[HALF:, lanes]], 1),
            ],
            0,
        )

    e = times_right(gather(slice(0, HALF)), even_t)
    o = times_right(gather(slice(HALF, PS)), odd_t)
    plus, minus = e + o, e - o
    real = jnp.concatenate([plus[:, :HALF], minus[:, :HALF]], 1)
    imag = jnp.concatenate([plus[:, HALF:], minus[:, HALF:]], 1)
    return real, imag


def turn(x, rows, columns):
    return pltpu.roll(pltpu.roll(x, rows, 0), columns, 1)


def turn(x, rows, columns):
    return pltpu.roll(pltpu.roll(x, rows, 0), columns, 1)


def visit(reach, column, current, halo, place, probe, seen_even, seen_odd, tables):
    inside = row((PS, PS)) >= reach
    all_rows = pl.ds(0, PS)
    w_real = jnp.where(inside, load_wrapped(current, 0, all_rows, column), halo[place, :PS])
    w_imag = jnp.where(inside, load_wrapped(current, 1, all_rows, column), halo[place, PS:])
    right = column % PS
    p_real, p_imag = turn(probe[0], reach, right), turn(probe[1], reach, right)
    exit_real = p_real * w_real - p_imag * w_imag
    exit_imag = p_real * w_imag + p_imag * w_real
    even, even_t, odd, odd_t = tables[0], tables[1], tables[2], tables[3]
    far_even, far_odd = forward(exit_real, exit_imag, even, even_t, odd, odd_t)

    def misfit(far, seen):
        real, imag = far[:HALF], far[HALF:]
        weight = real * real + imag * imag - seen
        return jnp.concatenate([weight * real, weight * imag], 0)

    back_real, back_imag = backward(misfit(far_even, seen_even), misfit(far_odd, seen_odd), even, even_t, odd, odd_t)
    down, left = (PS - reach) % PS, (PS - right) % PS
    probe_terms = (
        turn(w_real * back_real + w_imag * back_imag, down, left),
        turn(w_real * back_imag - w_imag * back_real, down, left),
    )
    object_terms = p_real * back_real + p_imag * back_imag, p_real * back_imag - p_imag * back_real
    return object_terms, probe_terms, inside


def lanes_of(plane):
    return slice(plane * PS, (plane + 1) * PS)


def first_kernel(
    is_odd, mine, above, below, scale, current, halo_sure, halo_core, halo_cross, probe, measured, tables,
    out, halo, leaving, grad_probe, cross_first, core_first, cross_rest, core_rest,
    under, cross_held, core_held, arrivals, departures,
):
    odd = is_odd[0] == 1
    factor = scale[0]
    all_below, shared_below = sum_lengths(mine, below)
    shared_above = sum_lengths(above, mine)[1]
    total = halo.shape[0]
    sure_copy = pltpu.make_async_copy(halo_sure, halo.at[pl.ds(0, SURE)], arrivals.at[0])
    rest_place = halo.at[pl.ds(SURE, total - SURE)]
    core_copy = pltpu.make_async_copy(halo_core, rest_place, arrivals.at[1])
    cross_copy = pltpu.make_async_copy(halo_cross, rest_place, arrivals.at[2])
    long_halo = all_below > SURE
    sure_copy.start()
    pl.when(long_halo & ~odd)(core_copy.start)
    pl.when(long_halo & odd)(cross_copy.start)
    out[...] = current[...]
    under[...] = jnp.zeros_like(under)
    grad_probe[...] = jnp.zeros_like(grad_probe)
    sure_copy.wait()
    pl.when(long_halo & ~odd)(core_copy.wait)
    pl.when(long_halo & odd)(cross_copy.wait)

    def one(j, at):
        reach, column = mine[2 * j], mine[2 * j + 1]
        whole, _ = lengths(mine, below, j)
        place = pl.ds(pl.multiple_of(at, STEP), PS)
        object_terms, probe_terms, inside = visit(
            reach, column, current, halo, place, probe, measured[j, :HALF], measured[j, HALF:], tables
        )
        for plane in range(2):
            grad_probe[plane] += probe_terms[plane]
            change = object_terms[plane] * -factor
            own, other = jnp.where(inside, change, 0.0), jnp.where(inside, 0.0, change)
            add_wrapped(out, plane, pl.ds(0, PS), column, own)
            add_wrapped(under, plane, pl.ds(0, PS), column, other)
            leaving[place, lanes_of(plane)] = other
        return at + whole

    lax.fori_loop(0, mine[2 * ((mine.shape[0] - 1) // 2)], one, 0)

    def store(to_cross, place, value):
        def put(condition, ref, at):
            @pl.when(condition)
            def _():
                ref[pl.ds(pl.multiple_of(at, STEP), STEP), :] = value

        put(to_cross & (place < SHARED), cross_first, place)
        put(to_cross & (place >= SHARED), cross_held, place - SHARED)
        put(~to_cross & (place < SHARED), core_first, place)
        put(~to_cross & (place >= SHARED), core_held, place - SHARED)

    def rising(j, at, place, at_shared, is_shared):
        @pl.when(is_shared)
        def _():
            rows = pl.ds(at, STEP)
            planes = [
                load_wrapped(out, plane, rows, above[2 * j + 1]) - load_wrapped(current, plane, rows, above[2 * j + 1])
                for plane in range(2)
            ]
            store(~odd, at_shared, jnp.concatenate(planes, axis=1))

    each_piece(above, mine, rising)

    def falling(j, at, place, at_shared, is_shared):
        rows = pl.ds(place, STEP)
        changes = [load_wrapped(under, plane, pl.ds(at, STEP), mine[2 * j + 1]) for plane in range(2)]
        halo[rows, :] += jnp.concatenate(changes, axis=1)

        @pl.when(is_shared)
        def _():
            store(odd, at_shared, leaving[rows, :])

    each_piece(mine, below, falling)
    long_cross = jnp.where(odd, shared_below, shared_above) > SHARED
    long_core = jnp.where(odd, shared_above, shared_below) > SHARED
    cross_out = pltpu.make_async_copy(cross_held, cross_rest, departures.at[0])
    core_out = pltpu.make_async_copy(core_held, core_rest, departures.at[1])
    pl.when(long_cross)(cross_out.start)
    pl.when(long_core)(core_out.start)
    pl.when(long_cross)(cross_out.wait)
    pl.when(long_core)(core_out.wait)


def cost(microseconds):
    return pl.CostEstimate(flops=microseconds * 10**9, bytes_accessed=microseconds * 2 * 10**6, transcendentals=0)


def first_visits(is_odd, mine, above, below, scale, current, halo, probe, measured, tables):
    total = halo[0].shape[0] + halo[1].shape[0]
    rest = total - SHARED

    def array(*shape):
        return jax.ShapeDtypeStruct(shape, F32)

    anywhere = whole_spec(pl.ANY)
    return pl.pallas_call(
        first_kernel,
        out_shape=(array(*current.shape), array(total, 2 * PS), array(total, 2 * PS), array(*probe.shape))
        + (array(SHARED, 2 * PS),) * 2 + (array(rest, 2 * PS),) * 2,
        in_specs=[whole_spec(SM)] * 5 + [whole_spec(VM)] + [anywhere] * 3 + [whole_spec(VM)] * 3,
        out_specs=(whole_spec(VM),) * 6 + (anywhere,) * 2,
        scratch_shapes=[pltpu.VMEM(current.shape, F32)] + [pltpu.VMEM((rest, 2 * PS), F32)] * 2
        + [pltpu.SemaphoreType.DMA((3,)), pltpu.SemaphoreType.DMA((2,))],
        compiler_params=pltpu.CompilerParams(vmem_limit_bytes=VISIT_LIMIT),
        cost_estimate=cost(12),
        name="first_visits",
    )(is_odd, mine, above, below, scale, current, *halo, probe, measured, tables)


def second_kernel(
    is_odd, mine, above, below, scale, changed, old_halo, base, cross_first, core_first, cross_rest, core_rest, probe,
    measured, tables, *rest
):
    slots = (mine.shape[0] - 1) // 2
    chunks = slots * PS // CHUNK
    leaving_out, (out, grad_probe, current, halo, leaving, cross, core, arrivals, departures) = rest[:chunks], rest[chunks:]
    odd = is_odd[0] == 1
    factor = scale[0]
    shared_below = sum_lengths(mine, below)[1]
    shared_above = sum_lengths(above, mine)[1]
    long_cross = jnp.where(odd, shared_below, shared_above) > SHARED
    long_core = jnp.where(odd, shared_above, shared_below) > SHARED
    copies = []
    for number, (first, more, held) in enumerate(((cross_first, cross_rest, cross), (core_first, core_rest, core))):
        copies.append(pltpu.make_async_copy(first, held.at[pl.ds(0, SHARED)], arrivals.at[2 * number]))
        copies.append(pltpu.make_async_copy(more, held.at[pl.ds(SHARED, slots * PS - SHARED)], arrivals.at[2 * number + 1]))
    copies[0].start()
    copies[2].start()
    pl.when(long_cross)(copies[1].start)
    pl.when(long_core)(copies[3].start)
    current[...] = changed[...]
    grad_probe[...] = jnp.zeros_like(grad_probe)
    copies[0].wait()
    copies[2].wait()
    pl.when(long_cross)(copies[1].wait)
    pl.when(long_core)(copies[3].wait)

    def from_above(j, at, place, at_shared, is_shared):
        @pl.when(is_shared)
        def _():
            rows = pl.ds(at_shared, STEP)
            part = jnp.where(odd, core[rows, :], cross[rows, :])
            for plane in range(2):
                add_wrapped(current, plane, pl.ds(at, STEP), above[2 * j + 1], part[:, lanes_of(plane)])

    each_piece(above, mine, from_above)
    out[...] = current[...]

    def renew(j, at, place, at_shared, is_shared):
        rows = pl.ds(pl.multiple_of(jnp.maximum(at_shared, 0), STEP), STEP)
        new = jnp.where(odd, cross[rows, :], core[rows, :])
        kept = pl.ds(place, STEP)
        halo[kept, :] = old_halo[kept, :] + jnp.where(is_shared, new, 0.0)

    each_piece(mine, below, renew)

    def one(j, at):
        reach, column = mine[2 * j], mine[2 * j + 1]
        whole, shared = lengths(mine, below, j)
        place = pl.ds(pl.multiple_of(at, STEP), PS)
        object_terms, probe_terms, inside = visit(
            reach, column, current, halo, place, probe, measured[j, :HALF], measured[j, HALF:], tables
        )
        unsent = row((PS, PS)) < shared
        for plane in range(2):
            grad_probe[plane] += probe_terms[plane]
            change = object_terms[plane] * -factor
            add_wrapped(out, plane, pl.ds(0, PS), column, jnp.where(inside, change, 0.0))
            lanes = lanes_of(plane)
            leaving[place, lanes] = jnp.where(inside, 0.0, change) + jnp.where(unsent, base[place, lanes], 0.0)
        return at + whole

    lax.fori_loop(0, mine[2 * slots], one, 0)
    sends = [
        pltpu.make_async_copy(leaving.at[pl.ds(CHUNK * k, CHUNK)], leaving_out[k], departures.at[k]) for k in range(chunks)
    ]
    for send in sends:
        send.start()
    for send in sends:
        send.wait()


def second_visits(is_odd, mine, above, below, scale, changed, halo, base, pieces, probe, measured, tables):
    total = halo.shape[0]
    anywhere = whole_spec(pl.ANY)
    chunks = total // CHUNK
    found = pl.pallas_call(
        second_kernel,
        out_shape=(jax.ShapeDtypeStruct((CHUNK, 2 * PS), F32),) * chunks
        + (jax.ShapeDtypeStruct(changed.shape, F32), jax.ShapeDtypeStruct(probe.shape, F32)),
        in_specs=[whole_spec(SM)] * 5 + [whole_spec(VM)] * 3 + [anywhere] * 4 + [whole_spec(VM)] * 3,
        out_specs=(anywhere,) * chunks + (whole_spec(VM),) * 2,
        scratch_shapes=[pltpu.VMEM(changed.shape, F32)] + [pltpu.VMEM((total, 2 * PS), F32)] * 4
        + [pltpu.SemaphoreType.DMA((4,)), pltpu.SemaphoreType.DMA((chunks,))],
        compiler_params=pltpu.CompilerParams(vmem_limit_bytes=VISIT_LIMIT),
        cost_estimate=cost(12),
        name="second_visits",
    )(is_odd, mine, above, below, scale, changed, halo, base, *pieces, probe, measured, tables)
    return found[:chunks], found[chunks], found[chunks + 1]


def finish_kernel(mine, above, changed, *rest):
    arriving, out = rest[:-1], rest[-1]
    out[...] = changed[...]

    def piece(j, at, place, at_shared, is_shared):
        for number, chunk in enumerate(arriving):
            @pl.when(place // CHUNK == number)
            def _(number=number, chunk=chunk):
                rows = pl.ds(pl.multiple_of(place - number * CHUNK, STEP), STEP)
                for plane in range(2):
                    add_wrapped(out, plane, pl.ds(at, STEP), above[2 * j + 1], chunk[rows, lanes_of(plane)])

    each_piece(above, mine, piece)


def finish(mine, above, changed, arriving):
    return pl.pallas_call(
        finish_kernel,
        out_shape=jax.ShapeDtypeStruct(changed.shape, F32),
        in_specs=[whole_spec(SM)] * 2 + [whole_spec(VM)] * (1 + len(arriving)),
        out_specs=whole_spec(VM),
        compiler_params=pltpu.CompilerParams(vmem_limit_bytes=16 * MIB),
        name="add_arriving",
    )(mine, above, changed, *arriving)


def shifted(value, steps):
    count = lax.axis_size("ty")
    first, last = (max(0, -steps), min(count, count - steps))
    return lax.ppermute(value, "ty", [(source, source + steps) for source in range(first, last)])


def pairs_from(first):
    return [(k, k + 1) for k in range(first, lax.axis_size("ty") - 1, 2)]


def swapped(value, first):
    pairs = pairs_from(first)
    return lax.ppermute(value, "ty", pairs + [(b, a) for a, b in pairs])


def raised(value, first):
    return lax.ppermute(value, "ty", [(b, a) for a, b in pairs_from(first)])


def lowered(value, first):
    return lax.ppermute(value, "ty", pairs_from(first))


def if_needed(needed, move, value):
    return lax.cond(needed, move, lambda kept: kept, value)


def total_over_tiles(value, used, between=lambda step, value: value):
    count = lax.axis_size("ty")
    if count & (count - 1) or value.shape[0] % count:
        return lax.psum((value, used), "ty")
    me = lax.axis_index("ty")
    bits = [1 << k for k in range(count.bit_length() - 1)]
    extra = None if used is None else jnp.full((8, value.shape[1]), used)
    for number, bit in enumerate(bits):
        half = value.shape[0] // 2
        side = (me // bit) % 2
        kept = lax.dynamic_slice_in_dim(value, side * half, half, 0)
        sent = lax.dynamic_slice_in_dim(value, (1 - side) * half, half, 0)
        if extra is not None:
            sent = jnp.concatenate([sent, extra])
        got = lax.ppermute(sent, "ty", [(i, i ^ bit) for i in range(count)])
        value = between(number, kept + got[:half])
        if extra is not None:
            extra = extra + got[half:]
    for number, bit in enumerate(reversed(bits)):
        side = (me // bit) % 2
        other = lax.ppermute(value, "ty", [(i, i ^ bit) for i in range(count)])
        value = jnp.where(side == 0, jnp.concatenate([value, other]), jnp.concatenate([other, value]))
        value = between(len(bits) + number, value)
    return value, None if extra is None else extra[0, 0]


def on_device(object_field, probe_field, scan_offsets, tile_counts, measured):
    rows = object_field.shape[1]
    tile = lax.axis_index("ty")
    is_odd = (tile % 2).reshape(1)
    odd = is_odd[0] == 1
    local_rows = scan_offsets[:, 0] - tile * rows
    mine = jnp.concatenate([jnp.stack([local_rows, scan_offsets[:, 1]], 1).reshape(-1), tile_counts])
    above, below = shifted(mine, 1), shifted(mine, -1)
    tables = jnp.asarray(dft_tables())
    sure, rest, sizes = pack(mine, above, below, object_field)
    cross_whole = jnp.where(odd, sizes[2], sizes[0])
    cross_shared = jnp.where(odd, sizes[3], sizes[1])
    halo = (
        shifted(sure, -1),
        raised(rest, 0),
        if_needed(cross_whole > SURE, lambda part: raised(part, 1), rest),
    )
    seen = sort_measured(measured)

    def step_of(probe):
        return (2.0 / jnp.max(probe[0] * probe[0] + probe[1] * probe[1])).reshape(1)

    changed, halo, leaving, grad_probe, *pieces = first_visits(
        is_odd, mine, above, below, step_of(probe_field), object_field, halo, probe_field, seen, tables
    )
    arrived = [
        swapped(pieces[0], 1),
        swapped(pieces[1], 0),
        if_needed(cross_shared > SHARED, lambda part: swapped(part, 1), pieces[2]),
        swapped(pieces[3], 0),
    ]
    total, number = total_over_tiles(grad_probe.reshape(2 * PS, PS), tile_counts[0].astype(F32))
    probe_now = probe_field - 4.0 / number * total.reshape(2, PS, PS)
    chunks, changed, grad_probe = second_visits(
        is_odd, mine, above, below, step_of(probe_now), changed, halo, leaving, arrived, probe_now, seen, tables
    )
    sure_chunks = SURE // CHUNK
    waiting = list(chunks)
    arriving = [shifted(waiting[0], 1)]

    def between(step, value):
        if step >= 1 and len(arriving) < sure_chunks:
            chunk, value = lax.optimization_barrier((waiting[len(arriving)], value))
            arriving.append(shifted(chunk, 1))
        return value

    total, _ = total_over_tiles(grad_probe.reshape(2 * PS, PS), None, between)
    for chunk in waiting[len(arriving) : sure_chunks]:
        arriving.append(shifted(chunk, 1))
    late = waiting[sure_chunks:]
    by_core = [lowered(chunk, 0) for chunk in late]
    by_cross = if_needed(cross_whole > SURE, lambda parts: [lowered(part, 1) for part in parts], late)
    arriving += [jnp.where(odd, a, b) for a, b in zip(by_core, by_cross)]
    probe_now = probe_now - 4.0 / number * total.reshape(2, PS, PS)
    return finish(mine, above, changed, arriving), probe_now


def solution(mesh):
    return jax.shard_map(
        on_device,
        mesh=mesh,
        in_specs=(
            P(None, ("groups", "ty"), None),
            P("groups", None, None),
            P(("groups", "ty"), None),
            P(("groups", "ty")),
            P(("groups", "ty"), None, None),
        ),
        out_specs=(P(None, ("groups", "ty"), None), P("groups", None, None)),
        check_vma=False,
    )
```

```python
import functools
import math

import jax
import jax.numpy as jnp
import ml_dtypes
import numpy as np
from jax import lax
from jax.experimental import pallas as pl
from jax.experimental.pallas import tpu as pltpu
from jax.sharding import PartitionSpec as P

ITERS = 2
PS = 256
STEP = 16
SHARED = 512
CHUNK = 256
SURE = 1024
MIB = 1024 * 1024
VISIT_LIMIT = 28 * MIB
HALF = 128
F32 = jnp.float32
BF16 = jnp.bfloat16


def split_table(table):
    high = table.astype(np.float32).astype(ml_dtypes.bfloat16)
    low = (table - high.astype(np.float64)).astype(np.float32).astype(ml_dtypes.bfloat16)
    return np.stack([high, low])


def dft_tables():
    points, bins = np.arange(HALF)[:, None], np.arange(HALF)[None, :]
    found = []
    for odd in (0, 1):
        phase = (points * (2 * bins + odd)) % PS
        angle = phase * (-2.0 * math.pi / PS)
        real, imag = np.cos(angle) / 16.0, np.sin(angle) / 16.0
        found.append(np.block([[real, imag], [-imag, real]]))
    even, odd = found
    return np.stack([split_table(t) for t in (even, even.T, odd, odd.T)])


def sort_table():
    table = np.zeros((PS, PS), np.float32)
    for k in range(HALF):
        table[2 * k, k] = 1.0
        table[2 * k + 1, HALF + k] = 1.0
    return table.astype(ml_dtypes.bfloat16)


def dot(a, b):
    return jnp.dot(a, b, preferred_element_type=F32)


def halves(x):
    high = x.astype(BF16)
    low = (x - high.astype(F32)).astype(BF16)
    return high, low


def times_right(x, table):
    high, low = halves(x)
    t_high, t_low = table[0], table[1]
    return dot(jnp.concatenate([high, low, high], 1), jnp.concatenate([t_high, t_high, t_low], 0))


def times_left(table, x):
    high, low = halves(x)
    t_high, t_low = table[0], table[1]
    return dot(jnp.concatenate([t_high, t_high, t_low], 1), jnp.concatenate([high, low, high], 0))


def lane(shape):
    return lax.broadcasted_iota(jnp.int32, shape, len(shape) - 1)


def row(shape):
    return lax.broadcasted_iota(jnp.int32, shape, len(shape) - 2)


def wrapped(mixed_first, whole, mixed_last, column):
    side = (column // HALF) % 2
    mixed = jnp.where(lane(mixed_first.shape) >= column % HALF, mixed_first, mixed_last)
    return jnp.where(side == 0, mixed, whole), jnp.where(side == 0, whole, mixed)


def cells(column, step, width):
    at = jnp.minimum(column // HALF + step, width // HALF - 1)
    return pl.ds(pl.multiple_of(at * HALF, HALF), HALF)


def load_wrapped(ref, plane, rows, column):
    blocks = [ref[plane, rows, cells(column, step, ref.shape[2])] for step in range(3)]
    return jnp.concatenate(wrapped(*blocks, column), axis=1)


def add_wrapped(ref, plane, rows, column, value):
    side, start = (column // HALF) % 2, column % HALF
    left, right = value[:, :HALF], value[:, HALF:]
    mixed = jnp.where(side == 0, left, right)
    other = jnp.where(side == 0, right, left)
    lanes = lane(mixed.shape)
    for step, part in ((0, jnp.where(lanes >= start, mixed, 0.0)), (1, other), (2, jnp.where(lanes < start, mixed, 0.0))):
        ref[plane, rows, cells(column, step, ref.shape[2])] += part


def up(value):
    return (value + STEP - 1) // STEP * STEP


def lengths(upper, lower, j):
    slots = (upper.shape[0] - 1) // 2
    reach, column = upper[2 * j], upper[2 * j + 1]
    first = reach
    for k in range(slots):
        near = (jnp.abs(lower[2 * k + 1] - column) < PS) & (k < lower[2 * slots])
        first = jnp.where(near, jnp.minimum(first, lower[2 * k]), first)
    live = j < upper[2 * slots]
    whole = jnp.where(live, up(reach), 0)
    shared = jnp.where(live & (first < reach), first // STEP * STEP, whole)
    return whole, shared


def each_piece(upper, lower, body):
    slots = (upper.shape[0] - 1) // 2

    def one(j, carry):
        at, at_shared = carry
        whole, shared = lengths(upper, lower, j)

        def piece(i, unused):
            body(j, pl.multiple_of(i * STEP, STEP), pl.multiple_of(at + i * STEP, STEP), pl.multiple_of(at_shared + i * STEP - shared, STEP), i * STEP >= shared)
            return unused

        lax.fori_loop(0, whole // STEP, piece, 0)
        return at + whole, at_shared + whole - shared

    return lax.fori_loop(0, slots, one, (0, 0))


def sum_lengths(upper, lower):
    def count(j, carry):
        whole, shared = lengths(upper, lower, j)
        return carry[0] + whole, carry[1] + whole - shared

    return lax.fori_loop(0, (upper.shape[0] - 1) // 2, count, (0, 0))


def whole_spec(space):
    return pl.BlockSpec(memory_space=space)


VM, SM = pltpu.VMEM, pltpu.SMEM


def pack_kernel(mine, above, below, current, sure, rest, sizes):
    def piece(j, at, place, at_shared, is_shared):
        rows = pl.ds(at, STEP)
        planes = [load_wrapped(current, plane, rows, above[2 * j + 1]) for plane in range(2)]
        value = jnp.concatenate(planes, axis=1)

        @pl.when(place < SURE)
        def _():
            sure[pl.ds(place, STEP), :] = value

        @pl.when(place >= SURE)
        def _():
            rest[pl.ds(pl.multiple_of(place - SURE, STEP), STEP), :] = value

    all_above, shared_above = each_piece(above, mine, piece)
    all_below, shared_below = sum_lengths(mine, below)
    sizes[0], sizes[1], sizes[2], sizes[3] = all_above, shared_above, all_below, shared_below


def pack(mine, above, below, current):
    total = (mine.shape[0] - 1) // 2 * PS
    return pl.pallas_call(
        pack_kernel,
        out_shape=(
            jax.ShapeDtypeStruct((SURE, 2 * PS), F32),
            jax.ShapeDtypeStruct((total - SURE, 2 * PS), F32),
            jax.ShapeDtypeStruct((4,), jnp.int32),
        ),
        in_specs=[whole_spec(SM)] * 3 + [whole_spec(VM)],
        out_specs=(whole_spec(VM), whole_spec(VM), whole_spec(SM)),
        compiler_params=pltpu.CompilerParams(vmem_limit_bytes=12 * MIB),
        name="pack_rows",
    )(mine, above, below, current)


def sort_kernel(table, measured, out):
    high = measured[0].astype(BF16)
    rest = measured[0] - high.astype(F32)
    middle = rest.astype(BF16)
    low = (rest - middle.astype(F32)).astype(BF16)
    by_column = dot(high, table[...]) + dot(middle, table[...]) + dot(low, table[...])
    high = by_column.astype(BF16)
    rest = by_column - high.astype(F32)
    middle = rest.astype(BF16)
    low = (rest - middle.astype(F32)).astype(BF16)
    turned = table[...].T
    out[0] = dot(turned, high) + dot(turned, middle) + dot(turned, low)


def sort_measured(measured):
    slots = measured.shape[0]
    return pl.pallas_call(
        sort_kernel,
        out_shape=jax.ShapeDtypeStruct(measured.shape, F32),
        grid=(slots,),
        in_specs=[pl.BlockSpec((PS, PS), lambda j: (0, 0)), pl.BlockSpec((1, PS, PS), lambda j: (j, 0, 0))],
        out_specs=pl.BlockSpec((1, PS, PS), lambda j: (j, 0, 0)),
        cost_estimate=pl.CostEstimate(flops=slots * 6 * 2 * PS**3, bytes_accessed=slots * 2 * PS * PS * 4, transcendentals=0),
        name="sort_measured",
    )(sort_table(), measured)


def forward(real, imag, even, even_t, odd, odd_t):
    near = jnp.concatenate([real[:, :HALF] + real[:, HALF:], imag[:, :HALF] + imag[:, HALF:]], 1)
    far = jnp.concatenate([real[:, :HALF] - real[:, HALF:], imag[:, :HALF] - imag[:, HALF:]], 1)
    e = times_right(near, even)
    o = times_right(far, odd)
    e_sum, e_dif = e[:HALF] + e[HALF:], e[:HALF] - e[HALF:]
    o_sum, o_dif = o[:HALF] + o[HALF:], o[:HALF] - o[HALF:]

    def stack(first, second):
        return jnp.concatenate(
            [
                jnp.concatenate([first[:, :HALF], second[:, :HALF]], 1),
                jnp.concatenate([first[:, HALF:], second[:, HALF:]], 1),
            ],
            0,
        )

    return times_left(even_t, stack(e_sum, o_sum)), times_left(odd_t, stack(e_dif, o_dif))


def backward(rows_even, rows_odd, even, even_t, odd, odd_t):
    e = times_left(even, rows_even)
    o = times_left(odd, rows_odd)
    top, bottom = e + o, e - o

    def gather(lanes):
        return jnp.concatenate(
            [
                jnp.concatenate([top[:HALF, lanes], top[HALF:, lanes]], 1),
                jnp.concatenate([bottom[:HALF, lanes], bottom[HALF:, lanes]], 1),
            ],
            0,
        )

    e = times_right(gather(slice(0, HALF)), even_t)
    o = times_right(gather(slice(HALF, PS)), odd_t)
    plus, minus = e + o, e - o
    real = jnp.concatenate([plus[:, :HALF], minus[:, :HALF]], 1)
    imag = jnp.concatenate([plus[:, HALF:], minus[:, HALF:]], 1)
    return real, imag


def turn(x, rows, columns):
    return pltpu.roll(pltpu.roll(x, rows, 0), columns, 1)


def double(probe, twice):
    for plane in range(2):
        for part in range(2):
            twice[plane, part * PS : (part + 1) * PS, :] = probe[plane]


def lower_rows(value, steps):
    groups = value.reshape(-1, 8, value.shape[1])
    turned = pltpu.roll(groups, steps, 1)
    before = jnp.concatenate([turned[-1:], turned[:-1]], 0)
    return jnp.where(row(groups.shape) < steps, before, turned).reshape(value.shape)


def raise_rows(value, steps):
    groups = value.reshape(-1, 8, value.shape[1])
    turned = pltpu.roll(groups, (8 - steps) % 8, 1)
    after = jnp.concatenate([turned[1:], turned[:1]], 0)
    return jnp.where(row(groups.shape) < 8 - steps, turned, after).reshape(value.shape)


def add_turned(held, plane, value, reach):
    held[plane, pl.ds(pl.multiple_of(PS - reach // 8 * 8, 8), PS), :] += raise_rows(value, reach % 8)


def visit(live, reach, column, current, halo, place, probe, seen_even, seen_odd, tables):
    inside = row((PS, PS)) >= jnp.where(live, reach, 0)
    weight_of = live.astype(F32)
    all_rows = pl.ds(0, PS)
    w_real = jnp.where(inside, load_wrapped(current, 0, all_rows, column), halo[place, :PS])
    w_imag = jnp.where(inside, load_wrapped(current, 1, all_rows, column), halo[place, PS:])
    right = column % PS
    turned = pl.ds(pl.multiple_of(PS - reach // 8 * 8, 8), PS)
    p_real, p_imag = (pltpu.roll(lower_rows(probe[plane, turned, :], reach % 8), right, 1) for plane in range(2))
    exit_real = p_real * w_real - p_imag * w_imag
    exit_imag = p_real * w_imag + p_imag * w_real
    even, even_t, odd, odd_t = tables[0], tables[1], tables[2], tables[3]
    far_even, far_odd = forward(exit_real, exit_imag, even, even_t, odd, odd_t)

    def misfit(far, seen):
        real, imag = far[:HALF], far[HALF:]
        weight = (real * real + imag * imag - seen) * weight_of
        return jnp.concatenate([weight * real, weight * imag], 0)

    back_real, back_imag = backward(misfit(far_even, seen_even), misfit(far_odd, seen_odd), even, even_t, odd, odd_t)
    left = (PS - right) % PS
    probe_terms = (
        pltpu.roll(w_real * back_real + w_imag * back_imag, left, 1),
        pltpu.roll(w_real * back_imag - w_imag * back_real, left, 1),
    )
    object_terms = p_real * back_real + p_imag * back_imag, p_real * back_imag - p_imag * back_real
    return object_terms, probe_terms, inside


def lanes_of(plane):
    return slice(plane * PS, (plane + 1) * PS)


def first_kernel(
    is_odd, mine, above, below, scale, current, halo_sure, halo_core, halo_cross, probe, measured, tables,
    out, halo, leaving, grad_probe, cross_first, core_first, cross_rest, core_rest,
    under, cross_held, core_held, twice, held, arrivals, departures,
):
    odd = is_odd[0] == 1
    factor = scale[0]
    all_below, shared_below = sum_lengths(mine, below)
    shared_above = sum_lengths(above, mine)[1]
    total = halo.shape[0]
    sure_copy = pltpu.make_async_copy(halo_sure, halo.at[pl.ds(0, SURE)], arrivals.at[0])
    rest_place = halo.at[pl.ds(SURE, total - SURE)]
    core_copy = pltpu.make_async_copy(halo_core, rest_place, arrivals.at[1])
    cross_copy = pltpu.make_async_copy(halo_cross, rest_place, arrivals.at[2])
    long_halo = all_below > SURE
    sure_copy.start()
    pl.when(long_halo & ~odd)(core_copy.start)
    pl.when(long_halo & odd)(cross_copy.start)
    out[...] = current[...]
    under[...] = jnp.zeros_like(under)
    held[...] = jnp.zeros_like(held)
    double(probe, twice)
    sure_copy.wait()
    pl.when(long_halo & ~odd)(core_copy.wait)
    pl.when(long_halo & odd)(cross_copy.wait)

    slots = (mine.shape[0] - 1) // 2

    def two(pair, at):
        found = []
        for step in range(2):
            j = jnp.minimum(2 * pair + step, slots - 1)
            live = 2 * pair + step < mine[2 * slots]
            reach, column = mine[2 * j], mine[2 * j + 1]
            place = pl.ds(pl.multiple_of(jnp.minimum(at, (slots - 1) * PS), STEP), PS)
            terms = visit(live, reach, column, current, halo, place, twice, measured[j, :HALF], measured[j, HALF:], tables)
            found.append((reach, column, place) + terms)
            at = at + jnp.where(live, lengths(mine, below, j)[0], 0)
        for step, (reach, column, place, object_terms, probe_terms, inside) in enumerate(found):
            for plane in range(2):
                add_turned(held, plane, probe_terms[plane], reach)
                change = object_terms[plane] * -factor
                own, other = jnp.where(inside, change, 0.0), jnp.where(inside, 0.0, change)
                add_wrapped(out, plane, pl.ds(0, PS), column, own)
                add_wrapped(under, plane, pl.ds(0, PS), column, other)
                leaving[place, lanes_of(plane)] = other
        return at

    lax.fori_loop(0, (mine[2 * slots] + 1) // 2, two, 0)
    grad_probe[...] = held[:, :PS, :] + held[:, PS:, :]

    def store(to_cross, place, value):
        def put(condition, ref, at):
            @pl.when(condition)
            def _():
                ref[pl.ds(pl.multiple_of(at, STEP), STEP), :] = value

        put(to_cross & (place < SHARED), cross_first, place)
        put(to_cross & (place >= SHARED), cross_held, place - SHARED)
        put(~to_cross & (place < SHARED), core_first, place)
        put(~to_cross & (place >= SHARED), core_held, place - SHARED)

    def rising(j, at, place, at_shared, is_shared):
        @pl.when(is_shared)
        def _():
            rows = pl.ds(at, STEP)
            planes = [
                load_wrapped(out, plane, rows, above[2 * j + 1]) - load_wrapped(current, plane, rows, above[2 * j + 1])
                for plane in range(2)
            ]
            store(~odd, at_shared, jnp.concatenate(planes, axis=1))

    each_piece(above, mine, rising)

    def falling(j, at, place, at_shared, is_shared):
        rows = pl.ds(place, STEP)
        changes = [load_wrapped(under, plane, pl.ds(at, STEP), mine[2 * j + 1]) for plane in range(2)]
        halo[rows, :] += jnp.concatenate(changes, axis=1)

        @pl.when(is_shared)
        def _():
            store(odd, at_shared, leaving[rows, :])

    each_piece(mine, below, falling)
    long_cross = jnp.where(odd, shared_below, shared_above) > SHARED
    long_core = jnp.where(odd, shared_above, shared_below) > SHARED
    cross_out = pltpu.make_async_copy(cross_held, cross_rest, departures.at[0])
    core_out = pltpu.make_async_copy(core_held, core_rest, departures.at[1])
    pl.when(long_cross)(cross_out.start)
    pl.when(long_core)(core_out.start)
    pl.when(long_cross)(cross_out.wait)
    pl.when(long_core)(core_out.wait)


def cost(microseconds):
    return pl.CostEstimate(flops=microseconds * 10**9, bytes_accessed=microseconds * 2 * 10**6, transcendentals=0)


def first_visits(is_odd, mine, above, below, scale, current, halo, probe, measured, tables):
    total = halo[0].shape[0] + halo[1].shape[0]
    rest = total - SHARED

    def array(*shape):
        return jax.ShapeDtypeStruct(shape, F32)

    anywhere = whole_spec(pl.ANY)
    return pl.pallas_call(
        first_kernel,
        out_shape=(
            pltpu.VMEM(current.shape, F32),
            pltpu.VMEM((total, 2 * PS), F32),
            pltpu.VMEM((total, 2 * PS), F32),
            array(*probe.shape),
        )
        + (array(SHARED, 2 * PS),) * 2 + (array(rest, 2 * PS),) * 2,
        in_specs=[whole_spec(SM)] * 5 + [whole_spec(VM)] + [anywhere] * 3 + [whole_spec(VM)] * 3,
        out_specs=(whole_spec(VM),) * 6 + (anywhere,) * 2,
        scratch_shapes=[pltpu.VMEM(current.shape, F32)] + [pltpu.VMEM((rest, 2 * PS), F32)] * 2
        + [pltpu.VMEM((2, 2 * PS, PS), F32), pltpu.VMEM((2, 2 * PS, PS), F32)]
        + [pltpu.SemaphoreType.DMA((3,)), pltpu.SemaphoreType.DMA((2,))],
        compiler_params=pltpu.CompilerParams(vmem_limit_bytes=VISIT_LIMIT),
        cost_estimate=cost(12),
        name="first_visits",
    )(is_odd, mine, above, below, scale, current, *halo, probe, measured, tables)


def second_kernel(
    is_odd, mine, above, below, scale, changed, old_halo, base, cross_first, core_first, cross_rest, core_rest, probe,
    measured, tables, *rest
):
    slots = (mine.shape[0] - 1) // 2
    chunks = slots * PS // CHUNK
    leaving_out, rest = rest[:chunks], rest[chunks:]
    out, grad_probe, current, halo, leaving, cross, core, twice, held, arrivals, departures = rest
    odd = is_odd[0] == 1
    factor = scale[0]
    shared_below = sum_lengths(mine, below)[1]
    shared_above = sum_lengths(above, mine)[1]
    long_cross = jnp.where(odd, shared_below, shared_above) > SHARED
    long_core = jnp.where(odd, shared_above, shared_below) > SHARED
    copies = []
    for number, (first, more, into) in enumerate(((cross_first, cross_rest, cross), (core_first, core_rest, core))):
        copies.append(pltpu.make_async_copy(first, into.at[pl.ds(0, SHARED)], arrivals.at[2 * number]))
        copies.append(pltpu.make_async_copy(more, into.at[pl.ds(SHARED, slots * PS - SHARED)], arrivals.at[2 * number + 1]))
    copies[0].start()
    copies[2].start()
    pl.when(long_cross)(copies[1].start)
    pl.when(long_core)(copies[3].start)
    current[...] = changed[...]
    held[...] = jnp.zeros_like(held)
    double(probe, twice)
    copies[0].wait()
    copies[2].wait()
    pl.when(long_cross)(copies[1].wait)
    pl.when(long_core)(copies[3].wait)

    def from_above(j, at, place, at_shared, is_shared):
        @pl.when(is_shared)
        def _():
            rows = pl.ds(at_shared, STEP)
            part = jnp.where(odd, core[rows, :], cross[rows, :])
            for plane in range(2):
                add_wrapped(current, plane, pl.ds(at, STEP), above[2 * j + 1], part[:, lanes_of(plane)])

    each_piece(above, mine, from_above)
    out[...] = current[...]

    def renew(j, at, place, at_shared, is_shared):
        rows = pl.ds(pl.multiple_of(jnp.maximum(at_shared, 0), STEP), STEP)
        new = jnp.where(odd, cross[rows, :], core[rows, :])
        kept = pl.ds(place, STEP)
        halo[kept, :] = old_halo[kept, :] + jnp.where(is_shared, new, 0.0)

    each_piece(mine, below, renew)

    def two(pair, at):
        found = []
        for step in range(2):
            j = jnp.minimum(2 * pair + step, slots - 1)
            live = 2 * pair + step < mine[2 * slots]
            reach, column = mine[2 * j], mine[2 * j + 1]
            whole, shared = lengths(mine, below, j)
            place = pl.ds(pl.multiple_of(jnp.minimum(at, (slots - 1) * PS), STEP), PS)
            terms = visit(live, reach, column, current, halo, place, twice, measured[j, :HALF], measured[j, HALF:], tables)
            found.append((reach, column, shared, place) + terms)
            at = at + jnp.where(live, whole, 0)
        for step, (reach, column, shared, place, object_terms, probe_terms, inside) in enumerate(found):
            unsent = row((PS, PS)) < shared
            for plane in range(2):
                add_turned(held, plane, probe_terms[plane], reach)
                change = object_terms[plane] * -factor
                add_wrapped(out, plane, pl.ds(0, PS), column, jnp.where(inside, change, 0.0))
                lanes = lanes_of(plane)
                leaving[place, lanes] = jnp.where(inside, 0.0, change) + jnp.where(unsent, base[place, lanes], 0.0)
        return at

    lax.fori_loop(0, (mine[2 * slots] + 1) // 2, two, 0)
    grad_probe[...] = held[:, :PS, :] + held[:, PS:, :]
    sends = [
        pltpu.make_async_copy(leaving.at[pl.ds(CHUNK * k, CHUNK)], leaving_out[k], departures.at[k]) for k in range(chunks)
    ]
    for send in sends:
        send.start()
    for send in sends:
        send.wait()


def second_visits(is_odd, mine, above, below, scale, changed, halo, base, pieces, probe, measured, tables):
    total = halo.shape[0]
    anywhere = whole_spec(pl.ANY)
    chunks = total // CHUNK
    found = pl.pallas_call(
        second_kernel,
        out_shape=(jax.ShapeDtypeStruct((CHUNK, 2 * PS), F32),) * chunks
        + (pltpu.VMEM(changed.shape, F32), jax.ShapeDtypeStruct(probe.shape, F32)),
        in_specs=[whole_spec(SM)] * 5 + [whole_spec(VM)] * 3 + [anywhere] * 4 + [whole_spec(VM)] * 3,
        out_specs=(anywhere,) * chunks + (whole_spec(VM),) * 2,
        scratch_shapes=[pltpu.VMEM(changed.shape, F32)] + [pltpu.VMEM((total, 2 * PS), F32)] * 4
        + [pltpu.VMEM((2, 2 * PS, PS), F32), pltpu.VMEM((2, 2 * PS, PS), F32)]
        + [pltpu.SemaphoreType.DMA((4,)), pltpu.SemaphoreType.DMA((chunks,))],
        compiler_params=pltpu.CompilerParams(vmem_limit_bytes=VISIT_LIMIT),
        cost_estimate=cost(12),
        name="second_visits",
    )(is_odd, mine, above, below, scale, changed, halo, base, *pieces, probe, measured, tables)
    return found[:chunks], found[chunks], found[chunks + 1]


def finish_kernel(mine, above, changed, *rest):
    arriving, out = rest[:-1], rest[-1]
    out[...] = changed[...]

    def piece(j, at, place, at_shared, is_shared):
        for number, chunk in enumerate(arriving):
            @pl.when(place // CHUNK == number)
            def _(number=number, chunk=chunk):
                rows = pl.ds(pl.multiple_of(place - number * CHUNK, STEP), STEP)
                for plane in range(2):
                    add_wrapped(out, plane, pl.ds(at, STEP), above[2 * j + 1], chunk[rows, lanes_of(plane)])

    each_piece(above, mine, piece)


def finish(mine, above, changed, arriving):
    return pl.pallas_call(
        finish_kernel,
        out_shape=jax.ShapeDtypeStruct(changed.shape, F32),
        in_specs=[whole_spec(SM)] * 2 + [whole_spec(VM)] * (1 + len(arriving)),
        out_specs=whole_spec(VM),
        compiler_params=pltpu.CompilerParams(vmem_limit_bytes=16 * MIB),
        name="add_arriving",
    )(mine, above, changed, *arriving)


def shifted(value, steps):
    count = lax.axis_size("ty")
    first, last = (max(0, -steps), min(count, count - steps))
    return lax.ppermute(value, "ty", [(source, source + steps) for source in range(first, last)])


def pairs_from(first):
    return [(k, k + 1) for k in range(first, lax.axis_size("ty") - 1, 2)]


def swapped(value, first):
    pairs = pairs_from(first)
    return lax.ppermute(value, "ty", pairs + [(b, a) for a, b in pairs])


def raised(value, first):
    return lax.ppermute(value, "ty", [(b, a) for a, b in pairs_from(first)])


def lowered(value, first):
    return lax.ppermute(value, "ty", pairs_from(first))


def if_needed(needed, move, value):
    return lax.cond(needed, move, lambda kept: kept, value)


def total_over_tiles(value, used, between=lambda step, value: value):
    count = lax.axis_size("ty")
    if count & (count - 1) or value.shape[0] % count:
        return lax.psum((value, used), "ty")
    me = lax.axis_index("ty")
    bits = [1 << k for k in range(count.bit_length() - 1)]
    extra = None if used is None else jnp.full((8, value.shape[1]), used)
    for number, bit in enumerate(bits):
        half = value.shape[0] // 2
        side = (me // bit) % 2
        kept = lax.dynamic_slice_in_dim(value, side * half, half, 0)
        sent = lax.dynamic_slice_in_dim(value, (1 - side) * half, half, 0)
        if extra is not None:
            sent = jnp.concatenate([sent, extra])
        got = lax.ppermute(sent, "ty", [(i, i ^ bit) for i in range(count)])
        value = between(number, kept + got[:half])
        if extra is not None:
            extra = extra + got[half:]
    for number, bit in enumerate(reversed(bits)):
        side = (me // bit) % 2
        other = lax.ppermute(value, "ty", [(i, i ^ bit) for i in range(count)])
        value = jnp.where(side == 0, jnp.concatenate([value, other]), jnp.concatenate([other, value]))
        value = between(len(bits) + number, value)
    return value, None if extra is None else extra[0, 0]


def on_device(object_field, probe_field, scan_offsets, tile_counts, measured):
    rows = object_field.shape[1]
    tile = lax.axis_index("ty")
    is_odd = (tile % 2).reshape(1)
    odd = is_odd[0] == 1
    local_rows = scan_offsets[:, 0] - tile * rows
    mine = jnp.concatenate([jnp.stack([local_rows, scan_offsets[:, 1]], 1).reshape(-1), tile_counts])
    above, below = shifted(mine, 1), shifted(mine, -1)
    tables = jnp.asarray(dft_tables())
    sure, rest, sizes = pack(mine, above, below, object_field)
    cross_whole = jnp.where(odd, sizes[2], sizes[0])
    cross_shared = jnp.where(odd, sizes[3], sizes[1])
    halo = (
        shifted(sure, -1),
        raised(rest, 0),
        if_needed(cross_whole > SURE, lambda part: raised(part, 1), rest),
    )
    seen = sort_measured(measured)

    def step_of(probe):
        return (2.0 / jnp.max(probe[0] * probe[0] + probe[1] * probe[1])).reshape(1)

    changed, halo, leaving, grad_probe, *pieces = first_visits(
        is_odd, mine, above, below, step_of(probe_field), object_field, halo, probe_field, seen, tables
    )
    arrived = [
        swapped(pieces[0], 1),
        swapped(pieces[1], 0),
        if_needed(cross_shared > SHARED, lambda part: swapped(part, 1), pieces[2]),
        swapped(pieces[3], 0),
    ]
    total, number = total_over_tiles(grad_probe.reshape(2 * PS, PS), tile_counts[0].astype(F32))
    probe_now = probe_field - 4.0 / number * total.reshape(2, PS, PS)
    chunks, changed, grad_probe = second_visits(
        is_odd, mine, above, below, step_of(probe_now), changed, halo, leaving, arrived, probe_now, seen, tables
    )
    sure_chunks = SURE // CHUNK
    waiting = list(chunks)
    arriving = [shifted(waiting[0], 1)]

    def between(step, value):
        if step >= 1 and len(arriving) < sure_chunks:
            chunk, value = lax.optimization_barrier((waiting[len(arriving)], value))
            arriving.append(shifted(chunk, 1))
        return value

    total, _ = total_over_tiles(grad_probe.reshape(2 * PS, PS), None, between)
    for chunk in waiting[len(arriving) : sure_chunks]:
        arriving.append(shifted(chunk, 1))
    late = waiting[sure_chunks:]
    by_core = [lowered(chunk, 0) for chunk in late]
    by_cross = if_needed(cross_whole > SURE, lambda parts: [lowered(part, 1) for part in parts], late)
    arriving += [jnp.where(odd, a, b) for a, b in zip(by_core, by_cross)]
    probe_now = probe_now - 4.0 / number * total.reshape(2, PS, PS)
    return finish(mine, above, changed, arriving), probe_now


def solution(mesh):
    return jax.shard_map(
        on_device,
        mesh=mesh,
        in_specs=(
            P(None, ("groups", "ty"), None),
            P("groups", None, None),
            P(("groups", "ty"), None),
            P(("groups", "ty")),
            P(("groups", "ty"), None, None),
        ),
        out_specs=(P(None, ("groups", "ty"), None), P("groups", None, None)),
        check_vma=False,
    )
```

```python
import functools
import math

import jax
import jax.numpy as jnp
import ml_dtypes
import numpy as np
from jax import lax
from jax.experimental import pallas as pl
from jax.experimental.pallas import tpu as pltpu
from jax.sharding import PartitionSpec as P

ITERS = 2
PS = 256
STEP = 16
STRETCH = 64
SHARED = 512
EXTRA = 8
SURE = 1024
MIB = 1024 * 1024
WAYS = 3
BLOCK = 256
VISIT_LIMIT = 48 * MIB
HALF = 128
F32 = jnp.float32
BF16 = jnp.bfloat16


def split_table(table):
    high = table.astype(np.float32).astype(ml_dtypes.bfloat16)
    low = (table - high.astype(np.float64)).astype(np.float32).astype(ml_dtypes.bfloat16)
    return np.stack([high, low])


def dft_tables():
    points, bins = np.arange(HALF)[:, None], np.arange(HALF)[None, :]
    found = []
    for odd in (0, 1):
        phase = (points * (2 * bins + odd)) % PS
        angle = phase * (-2.0 * math.pi / PS)
        real, imag = np.cos(angle) / 16.0, np.sin(angle) / 16.0
        found.append(np.block([[real, imag], [-imag, real]]))
    even, odd = found
    return np.stack([split_table(t) for t in (even, even.T, odd, odd.T)])


def sort_table():
    table = np.zeros((PS, PS), np.float32)
    for k in range(HALF):
        table[2 * k, k] = 1.0
        table[2 * k + 1, HALF + k] = 1.0
    return table.astype(ml_dtypes.bfloat16)


def dot(a, b):
    return jnp.dot(a, b, preferred_element_type=F32)


def halves(x):
    high = x.astype(BF16)
    low = (x - high.astype(F32)).astype(BF16)
    return high, low


def lane(shape):
    return lax.broadcasted_iota(jnp.int32, shape, len(shape) - 1)


def row(shape):
    return lax.broadcasted_iota(jnp.int32, shape, len(shape) - 2)


def wrapped(mixed_first, whole, mixed_last, column):
    side = (column // HALF) % 2
    mixed = jnp.where(lane(mixed_first.shape) >= column % HALF, mixed_first, mixed_last)
    return jnp.where(side == 0, mixed, whole), jnp.where(side == 0, whole, mixed)


def cells(column, step, width):
    at = jnp.minimum(column // HALF + step, width // HALF - 1)
    return pl.ds(pl.multiple_of(at * HALF, HALF), HALF)


def load_wrapped(ref, plane, rows, column):
    blocks = [ref[plane, rows, cells(column, step, ref.shape[2])] for step in range(3)]
    return jnp.concatenate(wrapped(*blocks, column), axis=1)


def add_wrapped(ref, plane, rows, column, value):
    side, start = (column // HALF) % 2, column % HALF
    left, right = value[:, :HALF], value[:, HALF:]
    mixed = jnp.where(side == 0, left, right)
    other = jnp.where(side == 0, right, left)
    lanes = lane(mixed.shape)
    for step, part in ((0, jnp.where(lanes >= start, mixed, 0.0)), (1, other), (2, jnp.where(lanes < start, mixed, 0.0))):
        ref[plane, rows, cells(column, step, ref.shape[2])] += part


def up(value):
    return (value + STEP - 1) // STEP * STEP


def lengths(upper, lower, j):
    slots = (upper.shape[0] - 1) // 2
    reach, column = upper[2 * j], upper[2 * j + 1]
    first = reach
    for k in range(slots):
        near = (jnp.abs(lower[2 * k + 1] - column) < PS) & (k < lower[2 * slots])
        first = jnp.where(near, jnp.minimum(first, lower[2 * k]), first)
    live = j < upper[2 * slots]
    whole = jnp.where(live, up(reach), 0)
    shared = jnp.where(live & (first < reach), first // STEP * STEP, whole)
    return whole, shared


def each_window(upper, lower, body):
    def one(j, carry):
        at, at_shared = carry
        whole, shared = lengths(upper, lower, j)
        body(j, at, at_shared, whole, shared)
        return at + whole, at_shared + whole - shared

    return lax.fori_loop(0, (upper.shape[0] - 1) // 2, one, (0, 0))


def each_shared_piece(upper, lower, body):
    def window(j, at, at_shared, whole, shared):
        def piece(i, carry):
            start = pl.multiple_of(shared + i * STEP, STEP)
            body(j, start, pl.multiple_of(at + start, STEP), pl.multiple_of(at_shared + i * STEP, STEP))
            return carry

        lax.fori_loop(0, (whole - shared) // STEP, piece, 0)

    return each_window(upper, lower, window)


def each_stretch(upper, lower, body):
    def window(j, at, at_shared, whole, shared):
        def stretch(i, carry):
            start = pl.multiple_of(i * STRETCH, STRETCH)
            body(j, start, pl.multiple_of(at + start, STEP), whole - start)
            return carry

        lax.fori_loop(0, (whole + STRETCH - 1) // STRETCH, stretch, 0)

    return each_window(upper, lower, window)


def block_copies(source, source_at, target, target_at, rows, needed, semaphores, first=0):
    return [
        (
            needed > start,
            pltpu.make_async_copy(
                source.at[pl.ds(source_at + start, BLOCK)], target.at[pl.ds(target_at + start, BLOCK)], semaphores.at[first + number]
            ),
        )
        for number, start in enumerate(range(0, rows, BLOCK))
    ]


def start_all(copies):
    for needed, copy in copies:
        pl.when(needed)(copy.start)


def wait_all(copies):
    for needed, copy in copies:
        pl.when(needed)(copy.wait)


def sum_lengths(upper, lower):
    def count(j, carry):
        whole, shared = lengths(upper, lower, j)
        return carry[0] + whole, carry[1] + whole - shared

    return lax.fori_loop(0, (upper.shape[0] - 1) // 2, count, (0, 0))


def whole_spec(space):
    return pl.BlockSpec(memory_space=space)


VM, SM = pltpu.VMEM, pltpu.SMEM


def pack_kernel(mine, above, below, object_field, sure, rest, sizes, current, packed, arrival, departures):
    load = pltpu.make_async_copy(object_field, current, arrival)
    load.start()
    all_above, shared_above = sum_lengths(above, mine)
    all_below, shared_below = sum_lengths(mine, below)
    sizes[0], sizes[1], sizes[2], sizes[3] = all_above, shared_above, all_below, shared_below
    load.wait()

    def stretch(j, start, place, used):
        rows = pl.ds(start, STRETCH)
        for plane in range(2):
            packed[pl.ds(place, STRETCH), lanes_of(plane)] = load_wrapped(current, plane, rows, above[2 * j + 1])

    each_stretch(above, mine, stretch)
    sends = block_copies(packed, 0, sure, 0, SURE, all_above, departures)
    sends += block_copies(packed, SURE, rest, 0, packed.shape[0] - SURE, all_above - SURE, departures, SURE // BLOCK)
    start_all(sends)
    wait_all(sends)


def pack(mine, above, below, current):
    total = (mine.shape[0] - 1) // 2 * PS
    anywhere = whole_spec(pl.ANY)
    return pl.pallas_call(
        pack_kernel,
        out_shape=(
            jax.ShapeDtypeStruct((SURE, 2 * PS), F32),
            jax.ShapeDtypeStruct((total - SURE, 2 * PS), F32),
            jax.ShapeDtypeStruct((4,), jnp.int32),
        ),
        in_specs=[whole_spec(SM)] * 3 + [anywhere],
        out_specs=(anywhere, anywhere, whole_spec(SM)),
        scratch_shapes=[
            pltpu.VMEM(current.shape, F32),
            pltpu.VMEM((total, 2 * PS), F32),
            pltpu.SemaphoreType.DMA,
            pltpu.SemaphoreType.DMA((total // BLOCK,)),
        ],
        compiler_params=pltpu.CompilerParams(vmem_limit_bytes=16 * MIB),
        name="pack_rows",
    )(mine, above, below, current)


def three_parts(x):
    high = x.astype(BF16)
    rest = x - high.astype(F32)
    middle = rest.astype(BF16)
    return high, middle, (rest - middle.astype(F32)).astype(BF16)


def prepare_kernel(table, measured, seen):
    by_place = table[...]
    by_row = by_place.T

    def one(j, carry):
        by_column = sum(dot(part, by_place) for part in three_parts(measured[j]))
        seen[j] = sum(dot(by_row, part) for part in three_parts(by_column))
        return carry

    lax.fori_loop(0, measured.shape[0], one, 0)


def prepare(measured):
    return pl.pallas_call(
        prepare_kernel,
        out_shape=jax.ShapeDtypeStruct(measured.shape, F32),
        in_specs=[whole_spec(VM), whole_spec(VM)],
        out_specs=whole_spec(VM),
        compiler_params=pltpu.CompilerParams(vmem_limit_bytes=16 * MIB),
        cost_estimate=cost(6),
        name="prepare",
    )(sort_table(), measured)


PIECE = 32


def times_right(x, table):
    high, low = x[:, :PS], x[:, PS:]
    return dot(jnp.concatenate([high, low, high], 1), jnp.concatenate([table[0], table[0], table[1]], 0))


def times_left(table, x):
    high, low = x[:PS, :], x[PS:, :]
    return dot(jnp.concatenate([table[0], table[0], table[1]], 1), jnp.concatenate([high, low, high], 0))


def put_columns(ref, rows, at, first, second):
    for place, part in ((at, first), (at + HALF, second)):
        high, low = halves(part)
        ref[rows, place : place + HALF] = high
        ref[rows, place + PS : place + PS + HALF] = low


def put_rows(ref, number, at, first, second):
    for place, part in ((at, first), (at + HALF, second)):
        high, low = halves(part)
        ref[number, place : place + PIECE, :] = high
        ref[number, PS + place : PS + place + PIECE, :] = low


def visit_stages(live, reach, column, at, current, halo, probe, seen, j, tables, held, scratch, emit):
    turned, window, wide, tall, product = scratch
    even, even_t, odd, odd_t = (tables.at[k] for k in range(4))
    right, left = column % PS, (PS - column % PS) % PS
    shift = reach % 8
    base = pl.multiple_of(PS - reach // 8 * 8, 8)
    own_from = jnp.where(live, reach, 0)
    weight_of = live.astype(F32)

    def rows_of(start, count=PIECE):
        return slice(start, start + count)

    def is_inside(start):
        return row((PIECE, PS)) + start >= own_from

    for start in range(0, PS, PIECE):
        inside = is_inside(start)
        rows = rows_of(start)
        for plane in range(2):
            below = halo[pl.ds(pl.multiple_of(at + start, 8), PIECE), lanes_of(plane)]
            window[plane, rows, :] = jnp.where(inside, load_wrapped(current, plane, rows, column), below)
            groups = probe[plane, pl.ds(pl.multiple_of(base + start - 8, 8), PIECE + 8), :].reshape(-1, 8, PS)
            groups = pltpu.roll(groups, shift, 1)
            lowered_rows = jnp.where(row((PIECE // 8, 8, PS)) < shift, groups[:-1], groups[1:]).reshape(PIECE, PS)
            turned[plane, rows, :] = pltpu.roll(lowered_rows, right, 1)
        w_real, w_imag = window[0, rows, :], window[1, rows, :]
        p_real, p_imag = turned[0, rows, :], turned[1, rows, :]
        real = p_real * w_real - p_imag * w_imag
        imag = p_real * w_imag + p_imag * w_real
        put_columns(wide, rows, 0, real[:, :HALF] + real[:, HALF:], imag[:, :HALF] + imag[:, HALF:])
        put_columns(wide, rows, 2 * PS, real[:, :HALF] - real[:, HALF:], imag[:, :HALF] - imag[:, HALF:])
    yield
    product[0] = times_right(wide[:, : 2 * PS], even)
    product[1] = times_right(wide[:, 2 * PS :], odd)
    yield
    for start in range(0, HALF, PIECE):
        top, bottom = [product[k, rows_of(start), :] for k in range(2)], [product[k, rows_of(HALF + start), :] for k in range(2)]
        plus, minus = [a + b for a, b in zip(top, bottom)], [a - b for a, b in zip(top, bottom)]
        for number, part in enumerate((plus, minus)):
            real = jnp.concatenate([x[:, :HALF] for x in part], 1)
            imag = jnp.concatenate([x[:, HALF:] for x in part], 1)
            put_rows(tall, number, start, real, imag)
    yield
    product[0] = times_left(even_t, tall[0])
    product[1] = times_left(odd_t, tall[1])
    yield
    for number in range(2):
        for start in range(0, HALF, PIECE):
            real, imag = product[number, rows_of(start), :], product[number, rows_of(HALF + start), :]
            weight = (real * real + imag * imag - seen[j, rows_of(number * HALF + start), :]) * weight_of
            put_rows(tall, number, start, weight * real, weight * imag)
    yield
    product[0] = times_left(even, tall[0])
    product[1] = times_left(odd, tall[1])
    yield
    for start in range(0, HALF, PIECE):
        real, imag = [product[k, rows_of(start), :] for k in range(2)], [product[k, rows_of(HALF + start), :] for k in range(2)]
        for place, real_part, imag_part in (
            (start, real[0] + real[1], imag[0] + imag[1]),
            (HALF + start, real[0] - real[1], imag[0] - imag[1]),
        ):
            rows = rows_of(place)
            put_columns(wide, rows, 0, real_part[:, :HALF], imag_part[:, :HALF])
            put_columns(wide, rows, 2 * PS, real_part[:, HALF:], imag_part[:, HALF:])
    yield
    product[0] = times_right(wide[:, : 2 * PS], even_t)
    product[1] = times_right(wide[:, 2 * PS :], odd_t)
    yield
    for start in range(0, PS, PIECE):
        rows = rows_of(start)
        first, second = product[0, rows, :], product[1, rows, :]
        plus, minus = first + second, first - second
        real = jnp.concatenate([plus[:, :HALF], minus[:, :HALF]], 1)
        imag = jnp.concatenate([plus[:, HALF:], minus[:, HALF:]], 1)
        w_real, w_imag = window[0, rows, :], window[1, rows, :]
        p_real, p_imag = turned[0, rows, :], turned[1, rows, :]
        emit(start, is_inside(start), (p_real * real + p_imag * imag, p_real * imag - p_imag * real))
        for plane, term in enumerate((w_real * real + w_imag * imag, w_real * imag - w_imag * real)):
            groups = pltpu.roll(pltpu.roll(term, left, 1).reshape(-1, 8, PS), (8 - shift) % 8, 1)
            stays = row(groups.shape) < 8 - shift
            here = pl.ds(pl.multiple_of(base + start, 8), PIECE)
            before = pl.ds(pl.multiple_of(base + start - 8, 8), PIECE)
            held[plane, here, :] += jnp.where(stays, groups, 0.0).reshape(PIECE, PS)
            held[plane, before, :] += jnp.where(stays, 0.0, groups).reshape(PIECE, PS)
    yield


def stage_scratch():
    return [
        pltpu.VMEM((2, PS, PS), F32),
        pltpu.VMEM((2, PS, PS), F32),
        pltpu.VMEM((PS, 4 * PS), BF16),
        pltpu.VMEM((2, 2 * PS, PS), BF16),
        pltpu.VMEM((2, PS, PS), F32),
    ]


def visit_all(mine, below, current, halo, probe, seen, tables, held, scratch, emit):
    slots = (mine.shape[0] - 1) // 2
    ways = len(scratch) // 5

    def some(turn, at):
        stages = []
        for way in range(ways):
            j = jnp.minimum(ways * turn + way, slots - 1)
            live = ways * turn + way < mine[2 * slots]
            reach, column = mine[2 * j], mine[2 * j + 1]
            whole, shared = lengths(mine, below, j)
            place = pl.multiple_of(jnp.minimum(at, (slots - 1) * PS), STEP)
            stages.append(
                visit_stages(
                    live, reach, column, place, current, halo, probe, seen, j, tables, held, scratch[5 * way : 5 * way + 5],
                    functools.partial(emit, live, column, place, shared),
                )
            )
            at = at + jnp.where(live, whole, 0)
        open_stages = list(stages)
        step = 0
        while open_stages:
            for way, stage in enumerate(stages):
                if stage in open_stages and way <= step and next(stage, True) is True:
                    open_stages.remove(stage)
            step += 1
        return at

    lax.fori_loop(0, (mine[2 * slots] + ways - 1) // ways, some, 0)


def split_gradient(held, odd, used, keep, send):
    real = held[0, :PS, :] + held[0, PS:, :]
    imag = held[1, :PS, :] + held[1, PS:, :]
    keep[:PS, :] = jnp.where(odd, imag, real)
    send[:PS, :] = jnp.where(odd, real, imag)
    number = jnp.full((EXTRA, PS), used.astype(F32))
    keep[PS:, :] = number
    send[PS:, :] = number


def lanes_of(plane):
    return slice(plane * PS, (plane + 1) * PS)


def first_kernel(
    is_odd, mine, above, below, scale, object_field, halo_sure, halo_core, halo_cross, probe, measured, tables,
    out_changed, out_halo, out_leaving, keep, send, cross_first, core_first, cross_rest, core_rest,
    current, out, under, halo, leaving, cross, core, probe_held, seen, tables_held, held, arrivals, departures, *scratch,
):
    slots = (mine.shape[0] - 1) // 2
    used = mine[2 * slots]
    odd = is_odd[0] == 1
    factor = scale[0]
    total = halo.shape[0]
    all_below, shared_below = sum_lengths(mine, below)
    shared_above = sum_lengths(above, mine)[1]
    loads = [
        (used >= 0, pltpu.make_async_copy(source, target, arrivals.at[number]))
        for number, (source, target) in enumerate(
            ((object_field, current), (tables, tables_held), (probe, probe_held), (measured, seen))
        )
    ]
    loads += block_copies(halo_sure, 0, halo, 0, SURE, all_below, arrivals, 4)
    after = 4 + SURE // BLOCK
    for needed, source in ((~odd, halo_core), (odd, halo_cross)):
        more = jnp.where(needed, all_below - SURE, 0)
        loads += block_copies(source, 0, halo, SURE, total - SURE, more, arrivals, after)
    start_all(loads)
    under[...] = jnp.zeros_like(under)
    held[...] = jnp.zeros_like(held)
    loads[0][1].wait()
    out[...] = current[...]
    wait_all(loads[1:])

    def emit(live, column, place, shared, start, inside, terms):
        rows = slice(start, start + PIECE)
        for plane in range(2):
            change = terms[plane] * -factor
            own, other = jnp.where(inside, change, 0.0), jnp.where(inside, 0.0, change)
            add_wrapped(out, plane, rows, column, own)
            add_wrapped(under, plane, rows, column, other)
            leaving[pl.ds(pl.multiple_of(place + start, STEP), PIECE), lanes_of(plane)] = other

    visit_all(mine, below, current, halo, probe_held, seen, tables_held, held, scratch, emit)
    sends = [(used >= 0, pltpu.make_async_copy(out, out_changed, departures.at[0]))]
    sends += block_copies(leaving, 0, out_leaving, 0, total, all_below, departures, 1)
    start_all(sends)
    split_gradient(held, odd, used, keep, send)

    def store(to_cross, place, value):
        @pl.when(to_cross)
        def _():
            cross[pl.ds(place, STEP), :] = value

        @pl.when(~to_cross)
        def _():
            core[pl.ds(place, STEP), :] = value

    def rising(j, at, place, at_shared):
        rows = pl.ds(at, STEP)
        planes = [
            load_wrapped(out, plane, rows, above[2 * j + 1]) - load_wrapped(current, plane, rows, above[2 * j + 1])
            for plane in range(2)
        ]
        store(~odd, at_shared, jnp.concatenate(planes, axis=1))

    each_shared_piece(above, mine, rising)

    def falling(j, at, place, at_shared):
        store(odd, at_shared, leaving[pl.ds(place, STEP), :])

    each_shared_piece(mine, below, falling)
    in_cross, in_core = jnp.where(odd, shared_below, shared_above), jnp.where(odd, shared_above, shared_below)
    count = total // BLOCK
    pieces = []
    for number, (source, first, rest, rows) in enumerate(((cross, cross_first, cross_rest, in_cross), (core, core_first, core_rest, in_core))):
        at = 1 + count * (1 + number)
        pieces += block_copies(source, 0, first, 0, SHARED, rows, departures, at)
        pieces += block_copies(source, SHARED, rest, 0, total - SHARED, rows - SHARED, departures, at + SHARED // BLOCK)
    start_all(pieces)

    def renew(j, start, place, inside):
        rows = pl.ds(place, STRETCH)
        within = row((STRETCH, PS)) < inside
        for plane in range(2):
            change = load_wrapped(under, plane, pl.ds(start, STRETCH), mine[2 * j + 1])
            halo[rows, lanes_of(plane)] += jnp.where(within, change, 0.0)

    each_stretch(mine, below, renew)
    last = block_copies(halo, 0, out_halo, 0, total, all_below, departures, 1 + 3 * count)
    start_all(last)
    wait_all(sends + pieces + last)


def cost(microseconds):
    return pl.CostEstimate(flops=microseconds * 10**9, bytes_accessed=microseconds * 2 * 10**6, transcendentals=0)


def array(*shape):
    return jax.ShapeDtypeStruct(shape, F32)


def visit_scratch(tile, total, measured, tables):
    return [
        pltpu.VMEM((2, 2 * PS, PS), F32),
        pltpu.VMEM(measured, F32),
        pltpu.VMEM(tables, BF16),
        pltpu.VMEM((2, 2 * PS, PS), F32),
    ]


def first_visits(is_odd, mine, above, below, scale, current, halo, probe, measured, tables):
    total = halo[0].shape[0] + halo[1].shape[0]
    rest = total - SHARED
    blocks = total // BLOCK
    anywhere = whole_spec(pl.ANY)
    tile, row_list = pltpu.VMEM(current.shape, F32), pltpu.VMEM((total, 2 * PS), F32)
    return pl.pallas_call(
        first_kernel,
        out_shape=(array(*current.shape), array(total, 2 * PS), array(total, 2 * PS))
        + (array(PS + EXTRA, PS),) * 2
        + (array(SHARED, 2 * PS),) * 2
        + (array(rest, 2 * PS),) * 2,
        in_specs=[whole_spec(SM)] * 5 + [anywhere] * 7,
        out_specs=(anywhere,) * 3 + (whole_spec(VM),) * 2 + (anywhere,) * 4,
        scratch_shapes=[tile] * 3 + [row_list] * 4 + visit_scratch(current.shape, total, measured.shape, tables.shape)
        + [pltpu.SemaphoreType.DMA((4 + blocks,)), pltpu.SemaphoreType.DMA((1 + 4 * blocks,))]
        + stage_scratch() * WAYS,
        compiler_params=pltpu.CompilerParams(vmem_limit_bytes=VISIT_LIMIT),
        cost_estimate=cost(12),
        name="first_visits",
    )(is_odd, mine, above, below, scale, current, *halo, probe, measured, tables)


def second_kernel(
    is_odd, mine, above, below, scale, changed, old_halo, old_leaving, cross_first, other_first, core_first, cross_rest,
    core_rest, probe, measured, tables,
    out_changed, leaving_sure, leaving_rest, keep, send,
    current, out, halo, leaving, base, cross, core, probe_held, seen, tables_held, held, arrivals, departures, *scratch,
):
    slots = (mine.shape[0] - 1) // 2
    used = mine[2 * slots]
    odd = is_odd[0] == 1
    factor = scale[0]
    total = halo.shape[0]
    count = total // BLOCK
    all_below, shared_below = sum_lengths(mine, below)
    shared_above = sum_lengths(above, mine)[1]
    in_cross, in_core = jnp.where(odd, shared_below, shared_above), jnp.where(odd, shared_above, shared_below)
    loads = [
        (used >= 0, pltpu.make_async_copy(source, target, arrivals.at[number]))
        for number, (source, target) in enumerate(
            ((changed, current), (tables, tables_held), (probe, probe_held), (measured, seen))
        )
    ]
    at_other = is_odd[1] == 1
    pieces = block_copies(cross_first, 0, cross, 0, SHARED, jnp.where(at_other, 0, in_cross), arrivals, 4)
    pieces += block_copies(other_first, 0, cross, 0, SHARED, jnp.where(at_other, in_cross, 0), arrivals, 4)
    pieces += block_copies(cross_rest, 0, cross, SHARED, total - SHARED, in_cross - SHARED, arrivals, 4 + SHARED // BLOCK)
    pieces += block_copies(core_first, 0, core, 0, SHARED, in_core, arrivals, 4 + count)
    pieces += block_copies(core_rest, 0, core, SHARED, total - SHARED, in_core - SHARED, arrivals, 4 + count + SHARED // BLOCK)
    lists = block_copies(old_halo, 0, halo, 0, total, all_below, arrivals, 4 + 2 * count)
    lists += block_copies(old_leaving, 0, base, 0, total, all_below, arrivals, 4 + 3 * count)
    start_all(loads[:1] + pieces + lists + loads[1:])
    held[...] = jnp.zeros_like(held)
    wait_all(loads[:1] + pieces)

    def from_above(j, at, place, at_shared):
        rows = pl.ds(at_shared, STEP)
        part = jnp.where(odd, core[rows, :], cross[rows, :])
        for plane in range(2):
            add_wrapped(current, plane, pl.ds(at, STEP), above[2 * j + 1], part[:, lanes_of(plane)])

    each_shared_piece(above, mine, from_above)
    out[...] = current[...]
    wait_all(lists + loads[1:])

    def renew(j, at, place, at_shared):
        rows = pl.ds(at_shared, STEP)
        halo[pl.ds(place, STEP), :] += jnp.where(odd, cross[rows, :], core[rows, :])

    each_shared_piece(mine, below, renew)

    def emit(live, column, place, shared, start, inside, terms):
        rows = slice(start, start + PIECE)
        unsent = row((PIECE, PS)) + start < shared
        for plane in range(2):
            lanes, here = lanes_of(plane), pl.ds(pl.multiple_of(place + start, STEP), PIECE)
            change = terms[plane] * -factor
            add_wrapped(out, plane, rows, column, jnp.where(inside, change, 0.0))
            leaving[here, lanes] = jnp.where(inside, 0.0, change) + jnp.where(unsent, base[here, lanes], 0.0)

    visit_all(mine, below, current, halo, probe_held, seen, tables_held, held, scratch, emit)
    sends = block_copies(leaving, 0, leaving_sure, 0, SURE, all_below, departures, 1)
    sends += block_copies(leaving, SURE, leaving_rest, 0, total - SURE, all_below - SURE, departures, 1 + SURE // BLOCK)
    sends += [(used >= 0, pltpu.make_async_copy(out, out_changed, departures.at[0]))]
    start_all(sends)
    split_gradient(held, odd, used, keep, send)
    wait_all(sends)


def second_visits(is_odd, mine, above, below, scale, changed, halo, base, pieces, probe, measured, tables):
    total = halo.shape[0]
    blocks = total // BLOCK
    anywhere = whole_spec(pl.ANY)
    tile, row_list = pltpu.VMEM(changed.shape, F32), pltpu.VMEM((total, 2 * PS), F32)
    return pl.pallas_call(
        second_kernel,
        out_shape=(array(*changed.shape), array(SURE, 2 * PS), array(total - SURE, 2 * PS)) + (array(PS + EXTRA, PS),) * 2,
        in_specs=[whole_spec(SM)] * 5 + [anywhere] * 11,
        out_specs=(anywhere,) * 3 + (whole_spec(VM),) * 2,
        scratch_shapes=[tile] * 2 + [row_list] * 5 + visit_scratch(changed.shape, total, measured.shape, tables.shape)
        + [pltpu.SemaphoreType.DMA((4 + 4 * blocks,)), pltpu.SemaphoreType.DMA((1 + blocks,))]
        + stage_scratch() * WAYS,
        compiler_params=pltpu.CompilerParams(vmem_limit_bytes=VISIT_LIMIT),
        cost_estimate=cost(12),
        name="second_visits",
    )(is_odd, mine, above, below, scale, changed, halo, base, *pieces, probe, measured, tables)


def finish_kernel(is_odd, mine, above, changed, sure, core_rest, cross_rest, out, arrived, arrivals):
    odd = is_odd[0] == 1
    total = arrived.shape[0]
    all_above = sum_lengths(above, mine)[0]
    load = pltpu.make_async_copy(changed, out, arrivals.at[0])
    load.start()
    loads = block_copies(sure, 0, arrived, 0, SURE, all_above, arrivals, 1)
    for needed, source in ((odd, core_rest), (~odd, cross_rest)):
        more = jnp.where(needed, all_above - SURE, 0)
        loads += block_copies(source, 0, arrived, SURE, total - SURE, more, arrivals, 1 + SURE // BLOCK)
    start_all(loads)
    load.wait()
    wait_all(loads)

    def stretch(j, start, place, used):
        within = row((STRETCH, PS)) < used
        for plane in range(2):
            part = jnp.where(within, arrived[pl.ds(place, STRETCH), lanes_of(plane)], 0.0)
            add_wrapped(out, plane, pl.ds(start, STRETCH), above[2 * j + 1], part)

    each_stretch(above, mine, stretch)


def finish(is_odd, mine, above, changed, sure, core_rest, cross_rest):
    anywhere = whole_spec(pl.ANY)
    total = sure.shape[0] + core_rest.shape[0]
    return pl.pallas_call(
        finish_kernel,
        out_shape=jax.ShapeDtypeStruct(changed.shape, F32),
        in_specs=[whole_spec(SM)] * 3 + [anywhere] * 4,
        out_specs=whole_spec(VM),
        scratch_shapes=[pltpu.VMEM((total, 2 * PS), F32), pltpu.SemaphoreType.DMA((1 + total // BLOCK,))],
        compiler_params=pltpu.CompilerParams(vmem_limit_bytes=20 * MIB),
        name="add_arriving",
    )(is_odd, mine, above, changed, sure, core_rest, cross_rest)


def tied(kernel, name, inputs, in_specs, outs, out_specs, ties):
    count, found = len(inputs), len(outs)

    def body(*refs):
        kernel(*refs[:count], *refs[count + len(ties) : count + len(ties) + found])

    anywhere = whole_spec(pl.ANY)
    results = pl.pallas_call(
        body,
        out_shape=tuple(outs) + tuple(jax.ShapeDtypeStruct(t.shape, t.dtype) for t in ties),
        in_specs=list(in_specs) + [anywhere] * len(ties),
        out_specs=tuple(out_specs) + (anywhere,) * len(ties),
        input_output_aliases={count + k: found + k for k in range(len(ties))},
        compiler_params=pltpu.CompilerParams(vmem_limit_bytes=8 * MIB),
        name=name,
    )(*inputs, *ties)
    return results[:found], list(results[found:])


def halve_kernel(side, kept, got, keep, send):
    half = keep.shape[0] - EXTRA
    total = kept[...] + got[...]
    low, high = total[:half], total[half : 2 * half]
    first = side[0] == 0
    keep[:half, :] = jnp.where(first, low, high)
    send[:half, :] = jnp.where(first, high, low)
    keep[half:, :] = total[2 * half :]
    send[half:, :] = total[2 * half :]


def sum_kernel(kept, got, out):
    out[...] = kept[...] + got[...]


def join_kernel(side, mine, other, out):
    height = mine.shape[0] - EXTRA
    first = side[0] == 0
    out[:height, :] = jnp.where(first, mine[:height, :], other[:height, :])
    out[height : 2 * height, :] = jnp.where(first, other[:height, :], mine[:height, :])
    out[2 * height :, :] = mine[height:, :]


def move_kernel(side, mine, other, probe, out, twice, scale):
    first = side[0] == 0
    step = 4.0 / mine[PS : PS + 1, :]
    real = probe[0] - step * jnp.where(first, mine[:PS, :], other[:PS, :])
    imag = probe[1] - step * jnp.where(first, other[:PS, :], mine[:PS, :])
    out[0] = real
    out[1] = imag
    for part in range(2):
        rows = slice(part * PS, (part + 1) * PS)
        twice[0, rows, :] = real
        twice[1, rows, :] = imag
    scale[0] = 2.0 / jnp.max(real * real + imag * imag)


def moved_probe(probe, keep, send, tie):
    count = lax.axis_size("ty")
    me = lax.axis_index("ty")
    bits = [1 << k for k in range((count - 1).bit_length())]
    vm, sm = whole_spec(VM), whole_spec(SM)

    def swap(value, bit):
        return lax.ppermute(value, "ty", [(i, i ^ bit) for i in range(count)])

    def side_of(bit):
        return (me // bit % 2).reshape(1)

    def call(step, kernel, name, inputs, in_specs, outs):
        ties, back = tie(step)
        found, ties = tied(kernel, name, inputs, in_specs, outs, [vm] * len(outs), ties)
        back(ties)
        return found

    got = swap(send, 1)
    shape = array((keep.shape[0] - EXTRA) // 2 + EXTRA, PS)
    keep, send = call(0, halve_kernel, "halve_sum", (side_of(2), keep, got), [sm, vm, vm], [shape, shape])
    value, bit = keep, 2
    got = swap(send, 2)
    step = 1
    for bit in bits[2:] + [0]:
        (value,) = call(step, sum_kernel, "add_sum", (value, got), [vm, vm], [array(value.shape[0], PS)])
        step += 1
        if bit:
            got = swap(value, bit)
    other = swap(value, 2)
    shape = array(2 * (value.shape[0] - EXTRA) + EXTRA, PS)
    (value,) = call(step, join_kernel, "join_sum", (side_of(2), value, other), [sm, vm, vm], [shape])
    other = swap(value, 1)
    return pl.pallas_call(
        move_kernel,
        out_shape=(
            jax.ShapeDtypeStruct(probe.shape, F32),
            jax.ShapeDtypeStruct((2, 2 * PS, PS), F32),
            jax.ShapeDtypeStruct((1,), F32),
        ),
        in_specs=[sm, vm, vm, vm],
        out_specs=(vm, vm, sm),
        compiler_params=pltpu.CompilerParams(vmem_limit_bytes=8 * MIB),
        name="move_probe",
    )(side_of(1), value, other, probe)


def unwritten(shape):
    return pl.pallas_call(
        lambda out: None, out_shape=shape, out_specs=whole_spec(pl.ANY), compiler_params=pltpu.CompilerParams(has_side_effects=False), name="unwritten"
    )()


def shifted(value, steps):
    count = lax.axis_size("ty")
    first, last = (max(0, -steps), min(count, count - steps))
    return lax.ppermute(value, "ty", [(source, source + steps) for source in range(first, last)])


def pairs_from(first, step=2):
    return [(k, k + 1) for k in range(first, lax.axis_size("ty") - 1, step)]


def swapped(value, pairs):
    return lax.ppermute(value, "ty", pairs + [(b, a) for a, b in pairs])


def raised(value, pairs):
    return lax.ppermute(value, "ty", [(b, a) for a, b in pairs])


def lowered(value, pairs):
    return lax.ppermute(value, "ty", pairs)


def if_needed(needed, move, value):
    return lax.cond(needed, move, lambda kept: unwritten(jax.ShapeDtypeStruct(kept.shape, kept.dtype)), value)


def on_device(object_field, probe_field, scan_offsets, tile_counts, measured):
    rows = object_field.shape[1]
    tile = lax.axis_index("ty")
    odd = tile % 2 == 1
    is_odd = jnp.stack([tile % 2, ((tile + 1) % 4 < 2).astype(jnp.int32)])
    core, cross = pairs_from(0), pairs_from(1)
    local_rows = scan_offsets[:, 0] - tile * rows
    mine = jnp.concatenate([jnp.stack([local_rows, scan_offsets[:, 1]], 1).reshape(-1), tile_counts])
    above, below = shifted(mine, 1), shifted(mine, -1)
    sure, rest, sizes = pack(mine, above, below, object_field)
    cross_whole = jnp.where(odd, sizes[2], sizes[0])
    cross_shared = jnp.where(odd, sizes[3], sizes[1])
    halo = (
        shifted(sure, -1),
        raised(rest, core),
        if_needed(cross_whole > SURE, lambda part: raised(part, cross), rest),
    )
    seen = prepare(measured)
    tables = jnp.asarray(dft_tables())
    twice = jnp.concatenate([probe_field, probe_field], 1)
    scale = (2.0 / jnp.max(probe_field[0] * probe_field[0] + probe_field[1] * probe_field[1])).reshape(1)
    changed, halo, leaving, keep, send, cross_first, core_first, cross_rest, core_rest = first_visits(
        is_odd, mine, above, below, scale, object_field, halo, twice, seen, tables
    )
    arrived = {}
    arrived["other"] = swapped(cross_first, pairs_from(3, 4))
    arrived["core"] = swapped(core_first, core)

    def tie_exchange(step):
        if step == 1:
            def back(ties):
                arrived["other"], arrived["core"] = ties[0], ties[1]
                arrived["cross"] = swapped(ties[2], pairs_from(1, 4))
            return [arrived["other"], arrived["core"], cross_first], back
        return [], lambda ties: None

    probe_now, twice, scale = moved_probe(probe_field, keep, send, tie_exchange)
    pieces = [
        arrived["cross"],
        arrived["other"],
        arrived["core"],
        if_needed(cross_shared > SHARED, lambda part: swapped(part, cross), cross_rest),
        swapped(core_rest, core),
    ]
    changed, leaving, leaving_rest, keep, send = second_visits(
        is_odd, mine, above, below, scale, changed, halo, leaving, pieces, twice, seen, tables
    )
    arriving = [shifted(leaving, 1)]

    def tie_arriving(step):
        if step == 1:
            def back(ties):
                arriving[0] = ties[0]
            return arriving[:1], back
        return [], lambda ties: None

    probe_now, _, _ = moved_probe(probe_now, keep, send, tie_arriving)
    by_core = lowered(leaving_rest, core)
    by_cross = if_needed(cross_whole > SURE, lambda part: lowered(part, cross), leaving_rest)
    return finish(is_odd, mine, above, changed, arriving[0], by_core, by_cross), probe_now


def solution(mesh):
    return jax.shard_map(
        on_device,
        mesh=mesh,
        in_specs=(
            P(None, ("groups", "ty"), None),
            P("groups", None, None),
            P(("groups", "ty"), None),
            P(("groups", "ty")),
            P(("groups", "ty"), None, None),
        ),
        out_specs=(P(None, ("groups", "ty"), None), P("groups", None, None)),
        check_vma=False,
    )
```

```python
import functools
import math

import jax
import jax.numpy as jnp
import ml_dtypes
import numpy as np
from jax import lax
from jax.experimental import pallas as pl
from jax.experimental.pallas import tpu as pltpu
from jax.sharding import PartitionSpec as P

ITERS = 2
PS = 256
STEP = 16
STRETCH = 64
LAST_TIE = 3
OTHER_TIE = 4
SHARED = 512
EXTRA = 8
SURE = 1024
MIB = 1024 * 1024
WAYS = 3
BLOCK = 256
VISIT_LIMIT = 48 * MIB
HALF = 128
F32 = jnp.float32
BF16 = jnp.bfloat16


def split_table(table):
    high = table.astype(np.float32).astype(ml_dtypes.bfloat16)
    low = (table - high.astype(np.float64)).astype(np.float32).astype(ml_dtypes.bfloat16)
    return np.stack([high, low])


def dft_tables():
    points, bins = np.arange(HALF)[:, None], np.arange(HALF)[None, :]
    found = []
    for odd in (0, 1):
        phase = (points * (2 * bins + odd)) % PS
        angle = phase * (-2.0 * math.pi / PS)
        real, imag = np.cos(angle) / 16.0, np.sin(angle) / 16.0
        found.append(np.block([[real, imag], [-imag, real]]))
    even, odd = found
    return np.stack([split_table(t) for t in (even, even.T, odd, odd.T)])


def sort_table():
    table = np.zeros((PS, PS), np.float32)
    for k in range(HALF):
        table[2 * k, k] = 1.0
        table[2 * k + 1, HALF + k] = 1.0
    return table.astype(ml_dtypes.bfloat16)


def dot(a, b):
    return jnp.dot(a, b, preferred_element_type=F32)


def halves(x):
    high = x.astype(BF16)
    low = (x - high.astype(F32)).astype(BF16)
    return high, low


def lane(shape):
    return lax.broadcasted_iota(jnp.int32, shape, len(shape) - 1)


def row(shape):
    return lax.broadcasted_iota(jnp.int32, shape, len(shape) - 2)


def wrapped(mixed_first, whole, mixed_last, column):
    side = (column // HALF) % 2
    mixed = jnp.where(lane(mixed_first.shape) >= column % HALF, mixed_first, mixed_last)
    return jnp.where(side == 0, mixed, whole), jnp.where(side == 0, whole, mixed)


def cells(column, step, width):
    at = jnp.minimum(column // HALF + step, width // HALF - 1)
    return pl.ds(pl.multiple_of(at * HALF, HALF), HALF)


def load_wrapped(ref, plane, rows, column):
    blocks = [ref[plane, rows, cells(column, step, ref.shape[2])] for step in range(3)]
    return jnp.concatenate(wrapped(*blocks, column), axis=1)


def add_wrapped(ref, plane, rows, column, value):
    side, start = (column // HALF) % 2, column % HALF
    left, right = value[:, :HALF], value[:, HALF:]
    mixed = jnp.where(side == 0, left, right)
    other = jnp.where(side == 0, right, left)
    lanes = lane(mixed.shape)
    for step, part in ((0, jnp.where(lanes >= start, mixed, 0.0)), (1, other), (2, jnp.where(lanes < start, mixed, 0.0))):
        ref[plane, rows, cells(column, step, ref.shape[2])] += part


def up(value):
    return (value + STEP - 1) // STEP * STEP


def lengths(upper, lower, j):
    slots = (upper.shape[0] - 1) // 2
    reach, column = upper[2 * j], upper[2 * j + 1]
    first = reach
    for k in range(slots):
        near = (jnp.abs(lower[2 * k + 1] - column) < PS) & (k < lower[2 * slots])
        first = jnp.where(near, jnp.minimum(first, lower[2 * k]), first)
    live = j < upper[2 * slots]
    whole = jnp.where(live, up(reach), 0)
    shared = jnp.where(live & (first < reach), first // STEP * STEP, whole)
    return whole, shared


def each_window(upper, lower, body):
    def one(j, carry):
        at, at_shared = carry
        whole, shared = lengths(upper, lower, j)
        body(j, at, at_shared, whole, shared)
        return at + whole, at_shared + whole - shared

    return lax.fori_loop(0, (upper.shape[0] - 1) // 2, one, (0, 0))


def each_shared_piece(upper, lower, body):
    def window(j, at, at_shared, whole, shared):
        def piece(i, carry):
            start = pl.multiple_of(shared + i * STEP, STEP)
            body(j, start, pl.multiple_of(at + start, STEP), pl.multiple_of(at_shared + i * STEP, STEP))
            return carry

        lax.fori_loop(0, (whole - shared) // STEP, piece, 0)

    return each_window(upper, lower, window)


def each_stretch(upper, lower, body):
    def window(j, at, at_shared, whole, shared):
        def stretch(i, carry):
            start = pl.multiple_of(i * STRETCH, STRETCH)
            body(j, start, pl.multiple_of(at + start, STEP), whole - start)
            return carry

        lax.fori_loop(0, (whole + STRETCH - 1) // STRETCH, stretch, 0)

    return each_window(upper, lower, window)


def block_copies(source, source_at, target, target_at, rows, needed, semaphores, first=0):
    return [
        (
            needed > start,
            pltpu.make_async_copy(
                source.at[pl.ds(source_at + start, BLOCK)], target.at[pl.ds(target_at + start, BLOCK)], semaphores.at[first + number]
            ),
        )
        for number, start in enumerate(range(0, rows, BLOCK))
    ]


def start_all(copies):
    for needed, copy in copies:
        pl.when(needed)(copy.start)


def wait_all(copies):
    for needed, copy in copies:
        pl.when(needed)(copy.wait)


def sum_lengths(upper, lower):
    def count(j, carry):
        whole, shared = lengths(upper, lower, j)
        return carry[0] + whole, carry[1] + whole - shared

    return lax.fori_loop(0, (upper.shape[0] - 1) // 2, count, (0, 0))


def whole_spec(space):
    return pl.BlockSpec(memory_space=space)


VM, SM = pltpu.VMEM, pltpu.SMEM


def pack_kernel(mine, above, below, object_field, sure, rest, sizes, current, packed, arrival, departures):
    load = pltpu.make_async_copy(object_field, current, arrival)
    load.start()
    all_above, shared_above = sum_lengths(above, mine)
    all_below, shared_below = sum_lengths(mine, below)
    sizes[0], sizes[1], sizes[2], sizes[3] = all_above, shared_above, all_below, shared_below
    load.wait()

    def stretch(j, start, place, used):
        rows = pl.ds(start, STRETCH)
        for plane in range(2):
            packed[pl.ds(place, STRETCH), lanes_of(plane)] = load_wrapped(current, plane, rows, above[2 * j + 1])

    each_stretch(above, mine, stretch)
    sends = block_copies(packed, 0, sure, 0, SURE, all_above, departures)
    sends += block_copies(packed, SURE, rest, 0, packed.shape[0] - SURE, all_above - SURE, departures, SURE // BLOCK)
    start_all(sends)
    wait_all(sends)


def pack(mine, above, below, current):
    total = (mine.shape[0] - 1) // 2 * PS
    anywhere = whole_spec(pl.ANY)
    return pl.pallas_call(
        pack_kernel,
        out_shape=(
            jax.ShapeDtypeStruct((SURE, 2 * PS), F32),
            jax.ShapeDtypeStruct((total - SURE, 2 * PS), F32),
            jax.ShapeDtypeStruct((4,), jnp.int32),
        ),
        in_specs=[whole_spec(SM)] * 3 + [anywhere],
        out_specs=(anywhere, anywhere, whole_spec(SM)),
        scratch_shapes=[
            pltpu.VMEM(current.shape, F32),
            pltpu.VMEM((total, 2 * PS), F32),
            pltpu.SemaphoreType.DMA,
            pltpu.SemaphoreType.DMA((total // BLOCK,)),
        ],
        compiler_params=pltpu.CompilerParams(vmem_limit_bytes=16 * MIB),
        name="pack_rows",
    )(mine, above, below, *in_hbm(current))


def three_parts(x):
    high = x.astype(BF16)
    rest = x - high.astype(F32)
    middle = rest.astype(BF16)
    return high, middle, (rest - middle.astype(F32)).astype(BF16)


def prepare_kernel(table, measured, seen):
    by_place = table[...]
    by_row = by_place.T

    def one(j, carry):
        by_column = sum(dot(part, by_place) for part in three_parts(measured[j]))
        seen[j] = sum(dot(by_row, part) for part in three_parts(by_column))
        return carry

    lax.fori_loop(0, measured.shape[0], one, 0)


def prepare(measured):
    return pl.pallas_call(
        prepare_kernel,
        out_shape=jax.ShapeDtypeStruct(measured.shape, F32),
        in_specs=[whole_spec(VM), whole_spec(VM)],
        out_specs=whole_spec(VM),
        compiler_params=pltpu.CompilerParams(vmem_limit_bytes=16 * MIB),
        cost_estimate=cost(6),
        name="prepare",
    )(sort_table(), measured)


PIECE = 32


def times_right(x, table):
    high, low = x[:, :PS], x[:, PS:]
    return dot(jnp.concatenate([high, low, high], 1), jnp.concatenate([table[0], table[0], table[1]], 0))


def times_left(table, x):
    high, low = x[:PS, :], x[PS:, :]
    return dot(jnp.concatenate([table[0], table[0], table[1]], 1), jnp.concatenate([high, low, high], 0))


def put_columns(ref, rows, at, first, second):
    for place, part in ((at, first), (at + HALF, second)):
        high, low = halves(part)
        ref[rows, place : place + HALF] = high
        ref[rows, place + PS : place + PS + HALF] = low


def put_rows(ref, number, at, first, second):
    for place, part in ((at, first), (at + HALF, second)):
        high, low = halves(part)
        ref[number, place : place + PIECE, :] = high
        ref[number, PS + place : PS + place + PIECE, :] = low


def visit_stages(live, reach, column, at, current, halo, probe, seen, j, tables, held, scratch, emit):
    turned, window, wide, tall, product = scratch
    even, even_t, odd, odd_t = (tables.at[k] for k in range(4))
    right, left = column % PS, (PS - column % PS) % PS
    shift = reach % 8
    base = pl.multiple_of(PS - reach // 8 * 8, 8)
    own_from = jnp.where(live, reach, 0)
    weight_of = live.astype(F32)

    def rows_of(start, count=PIECE):
        return slice(start, start + count)

    def is_inside(start):
        return row((PIECE, PS)) + start >= own_from

    for start in range(0, PS, PIECE):
        inside = is_inside(start)
        rows = rows_of(start)
        for plane in range(2):
            below = halo[pl.ds(pl.multiple_of(at + start, 8), PIECE), lanes_of(plane)]
            window[plane, rows, :] = jnp.where(inside, load_wrapped(current, plane, rows, column), below)
            groups = probe[plane, pl.ds(pl.multiple_of(base + start - 8, 8), PIECE + 8), :].reshape(-1, 8, PS)
            groups = pltpu.roll(groups, shift, 1)
            lowered_rows = jnp.where(row((PIECE // 8, 8, PS)) < shift, groups[:-1], groups[1:]).reshape(PIECE, PS)
            turned[plane, rows, :] = pltpu.roll(lowered_rows, right, 1)
        w_real, w_imag = window[0, rows, :], window[1, rows, :]
        p_real, p_imag = turned[0, rows, :], turned[1, rows, :]
        real = p_real * w_real - p_imag * w_imag
        imag = p_real * w_imag + p_imag * w_real
        put_columns(wide, rows, 0, real[:, :HALF] + real[:, HALF:], imag[:, :HALF] + imag[:, HALF:])
        put_columns(wide, rows, 2 * PS, real[:, :HALF] - real[:, HALF:], imag[:, :HALF] - imag[:, HALF:])
    yield
    product[0] = times_right(wide[:, : 2 * PS], even)
    product[1] = times_right(wide[:, 2 * PS :], odd)
    yield
    for start in range(0, HALF, PIECE):
        top, bottom = [product[k, rows_of(start), :] for k in range(2)], [product[k, rows_of(HALF + start), :] for k in range(2)]
        plus, minus = [a + b for a, b in zip(top, bottom)], [a - b for a, b in zip(top, bottom)]
        for number, part in enumerate((plus, minus)):
            real = jnp.concatenate([x[:, :HALF] for x in part], 1)
            imag = jnp.concatenate([x[:, HALF:] for x in part], 1)
            put_rows(tall, number, start, real, imag)
    yield
    product[0] = times_left(even_t, tall[0])
    product[1] = times_left(odd_t, tall[1])
    yield
    for number in range(2):
        for start in range(0, HALF, PIECE):
            real, imag = product[number, rows_of(start), :], product[number, rows_of(HALF + start), :]
            weight = (real * real + imag * imag - seen[j, rows_of(number * HALF + start), :]) * weight_of
            put_rows(tall, number, start, weight * real, weight * imag)
    yield
    product[0] = times_left(even, tall[0])
    product[1] = times_left(odd, tall[1])
    yield
    for start in range(0, HALF, PIECE):
        real, imag = [product[k, rows_of(start), :] for k in range(2)], [product[k, rows_of(HALF + start), :] for k in range(2)]
        for place, real_part, imag_part in (
            (start, real[0] + real[1], imag[0] + imag[1]),
            (HALF + start, real[0] - real[1], imag[0] - imag[1]),
        ):
            rows = rows_of(place)
            put_columns(wide, rows, 0, real_part[:, :HALF], imag_part[:, :HALF])
            put_columns(wide, rows, 2 * PS, real_part[:, HALF:], imag_part[:, HALF:])
    yield
    product[0] = times_right(wide[:, : 2 * PS], even_t)
    product[1] = times_right(wide[:, 2 * PS :], odd_t)
    yield
    for start in range(0, PS, PIECE):
        rows = rows_of(start)
        first, second = product[0, rows, :], product[1, rows, :]
        plus, minus = first + second, first - second
        real = jnp.concatenate([plus[:, :HALF], minus[:, :HALF]], 1)
        imag = jnp.concatenate([plus[:, HALF:], minus[:, HALF:]], 1)
        w_real, w_imag = window[0, rows, :], window[1, rows, :]
        p_real, p_imag = turned[0, rows, :], turned[1, rows, :]
        emit(start, is_inside(start), (p_real * real + p_imag * imag, p_real * imag - p_imag * real))
        for plane, term in enumerate((w_real * real + w_imag * imag, w_real * imag - w_imag * real)):
            groups = pltpu.roll(pltpu.roll(term, left, 1).reshape(-1, 8, PS), (8 - shift) % 8, 1)
            stays = row(groups.shape) < 8 - shift
            here = pl.ds(pl.multiple_of(base + start, 8), PIECE)
            before = pl.ds(pl.multiple_of(base + start - 8, 8), PIECE)
            held[plane, here, :] += jnp.where(stays, groups, 0.0).reshape(PIECE, PS)
            held[plane, before, :] += jnp.where(stays, 0.0, groups).reshape(PIECE, PS)
    yield


def stage_scratch():
    return [
        pltpu.VMEM((2, PS, PS), F32),
        pltpu.VMEM((2, PS, PS), F32),
        pltpu.VMEM((PS, 4 * PS), BF16),
        pltpu.VMEM((2, 2 * PS, PS), BF16),
        pltpu.VMEM((2, PS, PS), F32),
    ]


def visit_all(mine, below, current, halo, probe, seen, tables, held, scratch, emit):
    slots = (mine.shape[0] - 1) // 2
    ways = len(scratch) // 5

    def some(turn, at):
        stages = []
        for way in range(ways):
            j = jnp.minimum(ways * turn + way, slots - 1)
            live = ways * turn + way < mine[2 * slots]
            reach, column = mine[2 * j], mine[2 * j + 1]
            whole, shared = lengths(mine, below, j)
            place = pl.multiple_of(jnp.minimum(at, (slots - 1) * PS), STEP)
            stages.append(
                visit_stages(
                    live, reach, column, place, current, halo, probe, seen, j, tables, held, scratch[5 * way : 5 * way + 5],
                    functools.partial(emit, live, column, place, shared),
                )
            )
            at = at + jnp.where(live, whole, 0)
        open_stages = list(stages)
        step = 0
        while open_stages:
            for way, stage in enumerate(stages):
                if stage in open_stages and way <= step and next(stage, True) is True:
                    open_stages.remove(stage)
            step += 1
        return at

    lax.fori_loop(0, (mine[2 * slots] + ways - 1) // ways, some, 0)


def split_gradient(held, odd, used, keep, send):
    real = held[0, :PS, :] + held[0, PS:, :]
    imag = held[1, :PS, :] + held[1, PS:, :]
    keep[:PS, :] = jnp.where(odd, imag, real)
    send[:PS, :] = jnp.where(odd, real, imag)
    number = jnp.full((EXTRA, PS), used.astype(F32))
    keep[PS:, :] = number
    send[PS:, :] = number


def lanes_of(plane):
    return slice(plane * PS, (plane + 1) * PS)


def first_kernel(
    is_odd, mine, above, below, scale, object_field, halo_sure, halo_core, halo_cross, probe, measured, tables,
    out_changed, out_halo, out_leaving, keep, send, cross_first, core_first, cross_rest, core_rest,
    current, out, under, halo, leaving, cross, core, probe_held, seen, tables_held, held, arrivals, departures, *scratch,
):
    slots = (mine.shape[0] - 1) // 2
    used = mine[2 * slots]
    odd = is_odd[0] == 1
    factor = scale[0]
    total = halo.shape[0]
    all_below, shared_below = sum_lengths(mine, below)
    shared_above = sum_lengths(above, mine)[1]
    loads = [
        (used >= 0, pltpu.make_async_copy(source, target, arrivals.at[number]))
        for number, (source, target) in enumerate(
            ((object_field, current), (tables, tables_held), (probe, probe_held), (measured, seen))
        )
    ]
    loads += block_copies(halo_sure, 0, halo, 0, SURE, all_below, arrivals, 4)
    after = 4 + SURE // BLOCK
    for needed, source in ((~odd, halo_core), (odd, halo_cross)):
        more = jnp.where(needed, all_below - SURE, 0)
        loads += block_copies(source, 0, halo, SURE, total - SURE, more, arrivals, after)
    start_all(loads)
    under[...] = jnp.zeros_like(under)
    held[...] = jnp.zeros_like(held)
    loads[0][1].wait()
    out[...] = current[...]
    wait_all(loads[1:])

    def emit(live, column, place, shared, start, inside, terms):
        rows = slice(start, start + PIECE)
        for plane in range(2):
            change = terms[plane] * -factor
            own, other = jnp.where(inside, change, 0.0), jnp.where(inside, 0.0, change)
            add_wrapped(out, plane, rows, column, own)
            add_wrapped(under, plane, rows, column, other)
            leaving[pl.ds(pl.multiple_of(place + start, STEP), PIECE), lanes_of(plane)] = other

    visit_all(mine, below, current, halo, probe_held, seen, tables_held, held, scratch, emit)
    sends = [(used >= 0, pltpu.make_async_copy(out, out_changed, departures.at[0]))]
    sends += block_copies(leaving, 0, out_leaving, 0, total, all_below, departures, 1)
    start_all(sends)
    split_gradient(held, odd, used, keep, send)

    def store(to_cross, place, value):
        @pl.when(to_cross)
        def _():
            cross[pl.ds(place, STEP), :] = value

        @pl.when(~to_cross)
        def _():
            core[pl.ds(place, STEP), :] = value

    def rising(j, at, place, at_shared):
        rows = pl.ds(at, STEP)
        planes = [
            load_wrapped(out, plane, rows, above[2 * j + 1]) - load_wrapped(current, plane, rows, above[2 * j + 1])
            for plane in range(2)
        ]
        store(~odd, at_shared, jnp.concatenate(planes, axis=1))

    each_shared_piece(above, mine, rising)

    def falling(j, at, place, at_shared):
        store(odd, at_shared, leaving[pl.ds(place, STEP), :])

    each_shared_piece(mine, below, falling)
    in_cross, in_core = jnp.where(odd, shared_below, shared_above), jnp.where(odd, shared_above, shared_below)
    count = total // BLOCK
    pieces = []
    for number, (source, first, rest, rows) in enumerate(((cross, cross_first, cross_rest, in_cross), (core, core_first, core_rest, in_core))):
        at = 1 + count * (1 + number)
        pieces += block_copies(source, 0, first, 0, SHARED, rows, departures, at)
        pieces += block_copies(source, SHARED, rest, 0, total - SHARED, rows - SHARED, departures, at + SHARED // BLOCK)
    start_all(pieces)

    def renew(j, start, place, inside):
        rows = pl.ds(place, STRETCH)
        within = row((STRETCH, PS)) < inside
        for plane in range(2):
            change = load_wrapped(under, plane, pl.ds(start, STRETCH), mine[2 * j + 1])
            halo[rows, lanes_of(plane)] += jnp.where(within, change, 0.0)

    each_stretch(mine, below, renew)
    last = block_copies(halo, 0, out_halo, 0, total, all_below, departures, 1 + 3 * count)
    start_all(last)
    wait_all(sends + pieces + last)


def in_hbm(*arrays):
    return [pltpu.with_memory_space_constraint(array, pltpu.HBM) for array in arrays]


def cost(microseconds):
    return pl.CostEstimate(flops=microseconds * 10**9, bytes_accessed=microseconds * 2 * 10**6, transcendentals=0)


def array(*shape):
    return jax.ShapeDtypeStruct(shape, F32)


def visit_scratch(tile, total, measured, tables):
    return [
        pltpu.VMEM((2, 2 * PS, PS), F32),
        pltpu.VMEM(measured, F32),
        pltpu.VMEM(tables, BF16),
        pltpu.VMEM((2, 2 * PS, PS), F32),
    ]


def first_visits(is_odd, mine, above, below, scale, current, halo, probe, measured, tables):
    total = halo[0].shape[0] + halo[1].shape[0]
    rest = total - SHARED
    blocks = total // BLOCK
    anywhere = whole_spec(pl.ANY)
    tile, row_list = pltpu.VMEM(current.shape, F32), pltpu.VMEM((total, 2 * PS), F32)
    return pl.pallas_call(
        first_kernel,
        out_shape=(array(*current.shape), array(total, 2 * PS), array(total, 2 * PS))
        + (array(PS + EXTRA, PS),) * 2
        + (array(SHARED, 2 * PS),) * 2
        + (array(rest, 2 * PS),) * 2,
        in_specs=[whole_spec(SM)] * 5 + [anywhere] * 7,
        out_specs=(anywhere,) * 3 + (whole_spec(VM),) * 2 + (anywhere,) * 4,
        scratch_shapes=[tile] * 3 + [row_list] * 4 + visit_scratch(current.shape, total, measured.shape, tables.shape)
        + [pltpu.SemaphoreType.DMA((4 + blocks,)), pltpu.SemaphoreType.DMA((1 + 4 * blocks,))]
        + stage_scratch() * WAYS,
        compiler_params=pltpu.CompilerParams(vmem_limit_bytes=VISIT_LIMIT),
        cost_estimate=cost(12),
        name="first_visits",
    )(is_odd, mine, above, below, scale, *in_hbm(current, *halo, probe, measured, tables))


def second_kernel(
    is_odd, mine, above, below, scale, changed, old_halo, old_leaving, cross_first, other_first, core_first, cross_rest,
    core_rest, probe, measured, tables,
    out_changed, leaving_sure, leaving_rest, keep, send,
    current, out, halo, leaving, base, cross, core, probe_held, seen, tables_held, held, arrivals, departures, *scratch,
):
    slots = (mine.shape[0] - 1) // 2
    used = mine[2 * slots]
    odd = is_odd[0] == 1
    factor = scale[0]
    total = halo.shape[0]
    count = total // BLOCK
    all_below, shared_below = sum_lengths(mine, below)
    shared_above = sum_lengths(above, mine)[1]
    in_cross, in_core = jnp.where(odd, shared_below, shared_above), jnp.where(odd, shared_above, shared_below)
    loads = [
        (used >= 0, pltpu.make_async_copy(source, target, arrivals.at[number]))
        for number, (source, target) in enumerate(
            ((changed, current), (tables, tables_held), (probe, probe_held), (measured, seen))
        )
    ]
    at_other = is_odd[1] == 1
    pieces = block_copies(cross_first, 0, cross, 0, SHARED, jnp.where(at_other, 0, in_cross), arrivals, 4)
    pieces += block_copies(other_first, 0, cross, 0, SHARED, jnp.where(at_other, in_cross, 0), arrivals, 4)
    pieces += block_copies(cross_rest, 0, cross, SHARED, total - SHARED, in_cross - SHARED, arrivals, 4 + SHARED // BLOCK)
    pieces += block_copies(core_first, 0, core, 0, SHARED, in_core, arrivals, 4 + count)
    pieces += block_copies(core_rest, 0, core, SHARED, total - SHARED, in_core - SHARED, arrivals, 4 + count + SHARED // BLOCK)
    lists = block_copies(old_halo, 0, halo, 0, total, all_below, arrivals, 4 + 2 * count)
    lists += block_copies(old_leaving, 0, base, 0, total, all_below, arrivals, 4 + 3 * count)
    start_all(loads[:1] + pieces + lists + loads[1:])
    held[...] = jnp.zeros_like(held)
    wait_all(loads[:1] + pieces)

    def from_above(j, at, place, at_shared):
        rows = pl.ds(at_shared, STEP)
        part = jnp.where(odd, core[rows, :], cross[rows, :])
        for plane in range(2):
            add_wrapped(current, plane, pl.ds(at, STEP), above[2 * j + 1], part[:, lanes_of(plane)])

    each_shared_piece(above, mine, from_above)
    out[...] = current[...]
    wait_all(lists + loads[1:])

    def renew(j, at, place, at_shared):
        rows = pl.ds(at_shared, STEP)
        halo[pl.ds(place, STEP), :] += jnp.where(odd, cross[rows, :], core[rows, :])

    each_shared_piece(mine, below, renew)

    def emit(live, column, place, shared, start, inside, terms):
        rows = slice(start, start + PIECE)
        unsent = row((PIECE, PS)) + start < shared
        for plane in range(2):
            lanes, here = lanes_of(plane), pl.ds(pl.multiple_of(place + start, STEP), PIECE)
            change = terms[plane] * -factor
            add_wrapped(out, plane, rows, column, jnp.where(inside, change, 0.0))
            leaving[here, lanes] = jnp.where(inside, 0.0, change) + jnp.where(unsent, base[here, lanes], 0.0)

    visit_all(mine, below, current, halo, probe_held, seen, tables_held, held, scratch, emit)
    sends = block_copies(leaving, 0, leaving_sure, 0, SURE, all_below, departures, 1)
    sends += block_copies(leaving, SURE, leaving_rest, 0, total - SURE, all_below - SURE, departures, 1 + SURE // BLOCK)
    sends += [(used >= 0, pltpu.make_async_copy(out, out_changed, departures.at[0]))]
    start_all(sends)
    split_gradient(held, odd, used, keep, send)
    wait_all(sends)


def second_visits(is_odd, mine, above, below, scale, changed, halo, base, pieces, probe, measured, tables):
    total = halo.shape[0]
    blocks = total // BLOCK
    anywhere = whole_spec(pl.ANY)
    tile, row_list = pltpu.VMEM(changed.shape, F32), pltpu.VMEM((total, 2 * PS), F32)
    return pl.pallas_call(
        second_kernel,
        out_shape=(array(*changed.shape), array(SURE, 2 * PS), array(total - SURE, 2 * PS)) + (array(PS + EXTRA, PS),) * 2,
        in_specs=[whole_spec(SM)] * 5 + [anywhere] * 11,
        out_specs=(anywhere,) * 3 + (whole_spec(VM),) * 2,
        scratch_shapes=[tile] * 2 + [row_list] * 5 + visit_scratch(changed.shape, total, measured.shape, tables.shape)
        + [pltpu.SemaphoreType.DMA((4 + 4 * blocks,)), pltpu.SemaphoreType.DMA((1 + blocks,))]
        + stage_scratch() * WAYS,
        compiler_params=pltpu.CompilerParams(vmem_limit_bytes=VISIT_LIMIT),
        cost_estimate=cost(12),
        name="second_visits",
    )(is_odd, mine, above, below, scale, *in_hbm(changed, halo, base, *pieces, probe, measured, tables))


def finish_kernel(is_odd, mine, above, changed, sure, core_rest, cross_rest, out, arrived, arrivals):
    odd = is_odd[0] == 1
    total = arrived.shape[0]
    all_above = sum_lengths(above, mine)[0]
    load = pltpu.make_async_copy(changed, out, arrivals.at[0])
    load.start()
    loads = block_copies(sure, 0, arrived, 0, SURE, all_above, arrivals, 1)
    for needed, source in ((odd, core_rest), (~odd, cross_rest)):
        more = jnp.where(needed, all_above - SURE, 0)
        loads += block_copies(source, 0, arrived, SURE, total - SURE, more, arrivals, 1 + SURE // BLOCK)
    start_all(loads)
    load.wait()
    wait_all(loads)

    def stretch(j, start, place, used):
        within = row((STRETCH, PS)) < used
        for plane in range(2):
            part = jnp.where(within, arrived[pl.ds(place, STRETCH), lanes_of(plane)], 0.0)
            add_wrapped(out, plane, pl.ds(start, STRETCH), above[2 * j + 1], part)

    each_stretch(above, mine, stretch)


def finish(is_odd, mine, above, changed, sure, core_rest, cross_rest):
    anywhere = whole_spec(pl.ANY)
    total = sure.shape[0] + core_rest.shape[0]
    return pl.pallas_call(
        finish_kernel,
        out_shape=jax.ShapeDtypeStruct(changed.shape, F32),
        in_specs=[whole_spec(SM)] * 3 + [anywhere] * 4,
        out_specs=whole_spec(VM),
        scratch_shapes=[pltpu.VMEM((total, 2 * PS), F32), pltpu.SemaphoreType.DMA((1 + total // BLOCK,))],
        compiler_params=pltpu.CompilerParams(vmem_limit_bytes=20 * MIB),
        name="add_arriving",
    )(is_odd, mine, above, *in_hbm(changed, sure, core_rest, cross_rest))


def tied(kernel, name, inputs, in_specs, outs, out_specs, ties):
    count, found = len(inputs), len(outs)

    def body(*refs):
        kernel(*refs[:count], *refs[count + len(ties) : count + len(ties) + found])

    anywhere = whole_spec(pl.ANY)
    results = pl.pallas_call(
        body,
        out_shape=tuple(outs) + tuple(jax.ShapeDtypeStruct(t.shape, t.dtype) for t in ties),
        in_specs=list(in_specs) + [anywhere] * len(ties),
        out_specs=tuple(out_specs) + (anywhere,) * len(ties),
        input_output_aliases={count + k: found + k for k in range(len(ties))},
        compiler_params=pltpu.CompilerParams(vmem_limit_bytes=8 * MIB),
        name=name,
    )(*inputs, *ties)
    return results[:found], list(results[found:])


def halve_kernel(side, kept, got, keep, send):
    half = keep.shape[0] - EXTRA
    total = kept[...] + got[...]
    low, high = total[:half], total[half : 2 * half]
    first = side[0] == 0
    keep[:half, :] = jnp.where(first, low, high)
    send[:half, :] = jnp.where(first, high, low)
    keep[half:, :] = total[2 * half :]
    send[half:, :] = total[2 * half :]


def sum_kernel(kept, got, out):
    out[...] = kept[...] + got[...]


def join_kernel(side, mine, other, out):
    height = mine.shape[0] - EXTRA
    first = side[0] == 0
    out[:height, :] = jnp.where(first, mine[:height, :], other[:height, :])
    out[height : 2 * height, :] = jnp.where(first, other[:height, :], mine[:height, :])
    out[2 * height :, :] = mine[height:, :]


def move_kernel(side, mine, other, probe, out, twice, scale):
    first = side[0] == 0
    step = 4.0 / mine[PS : PS + 1, :]
    real = probe[0] - step * jnp.where(first, mine[:PS, :], other[:PS, :])
    imag = probe[1] - step * jnp.where(first, other[:PS, :], mine[:PS, :])
    out[0] = real
    out[1] = imag
    for part in range(2):
        rows = slice(part * PS, (part + 1) * PS)
        twice[0, rows, :] = real
        twice[1, rows, :] = imag
    scale[0] = 2.0 / jnp.max(real * real + imag * imag)


def moved_probe(probe, keep, send, tie):
    count = lax.axis_size("ty")
    me = lax.axis_index("ty")
    bits = [1 << k for k in range((count - 1).bit_length())]
    vm, sm = whole_spec(VM), whole_spec(SM)

    def swap(value, bit):
        return lax.ppermute(value, "ty", [(i, i ^ bit) for i in range(count)])

    def side_of(bit):
        return (me // bit % 2).reshape(1)

    def call(step, kernel, name, inputs, in_specs, outs):
        ties, back = tie(step)
        found, ties = tied(kernel, name, inputs, in_specs, outs, [vm] * len(outs), ties)
        back(ties)
        return found

    got = swap(send, 1)
    shape = array((keep.shape[0] - EXTRA) // 2 + EXTRA, PS)
    keep, send = call(0, halve_kernel, "halve_sum", (side_of(2), keep, got), [sm, vm, vm], [shape, shape])
    value, bit = keep, 2
    got = swap(send, 2)
    step = 1
    for bit in bits[2:] + [0]:
        (value,) = call(step, sum_kernel, "add_sum", (value, got), [vm, vm], [array(value.shape[0], PS)])
        step += 1
        if bit:
            got = swap(value, bit)
    other = swap(value, 2)
    shape = array(2 * (value.shape[0] - EXTRA) + EXTRA, PS)
    (value,) = call(step, join_kernel, "join_sum", (side_of(2), value, other), [sm, vm, vm], [shape])
    other = swap(value, 1)
    return pl.pallas_call(
        move_kernel,
        out_shape=(
            jax.ShapeDtypeStruct(probe.shape, F32),
            jax.ShapeDtypeStruct((2, 2 * PS, PS), F32),
            jax.ShapeDtypeStruct((1,), F32),
        ),
        in_specs=[sm, vm, vm, vm],
        out_specs=(vm, vm, sm),
        compiler_params=pltpu.CompilerParams(vmem_limit_bytes=8 * MIB),
        name="move_probe",
    )(side_of(1), value, other, probe)


def unwritten(shape):
    return pl.pallas_call(
        lambda out: None, out_shape=shape, out_specs=whole_spec(pl.ANY), compiler_params=pltpu.CompilerParams(has_side_effects=False), name="unwritten"
    )()


def shifted(value, steps):
    count = lax.axis_size("ty")
    first, last = (max(0, -steps), min(count, count - steps))
    return lax.ppermute(value, "ty", [(source, source + steps) for source in range(first, last)])


def pairs_from(first, step=2):
    return [(k, k + 1) for k in range(first, lax.axis_size("ty") - 1, step)]


def swapped(value, pairs):
    return lax.ppermute(value, "ty", pairs + [(b, a) for a, b in pairs])


def raised(value, pairs):
    return lax.ppermute(value, "ty", [(b, a) for a, b in pairs])


def lowered(value, pairs):
    return lax.ppermute(value, "ty", pairs)


def if_needed(rows, move, value):
    shape = jax.ShapeDtypeStruct(value.shape, value.dtype)

    def part(height):
        def branch(kept):
            if height == 0:
                return unwritten(shape)
            if height == kept.shape[0]:
                return move(kept)
            rest = jax.ShapeDtypeStruct((kept.shape[0] - height, kept.shape[1]), kept.dtype)
            return jnp.concatenate([move(kept[:height]), unwritten(rest)])

        return branch

    heights = [0]
    while heights[-1] < value.shape[0]:
        heights.append(min(max(BLOCK, 2 * heights[-1]), value.shape[0]))
    number = sum((rows > height).astype(jnp.int32) for height in heights[:-1])
    return lax.switch(number, [part(height) for height in heights], value)


def on_device(object_field, probe_field, scan_offsets, tile_counts, measured):
    rows = object_field.shape[1]
    tile = lax.axis_index("ty")
    odd = tile % 2 == 1
    is_odd = jnp.stack([tile % 2, ((tile + 1) % 4 < 2).astype(jnp.int32)])
    core, cross = pairs_from(0), pairs_from(1)
    local_rows = scan_offsets[:, 0] - tile * rows
    mine = jnp.concatenate([jnp.stack([local_rows, scan_offsets[:, 1]], 1).reshape(-1), tile_counts])
    above, below = shifted(mine, 1), shifted(mine, -1)
    sure, rest, sizes = pack(mine, above, below, object_field)
    cross_whole = jnp.where(odd, sizes[2], sizes[0])
    cross_shared = jnp.where(odd, sizes[3], sizes[1])
    halo = (
        shifted(sure, -1),
        raised(rest, core),
        if_needed(cross_whole - SURE, lambda part: raised(part, cross), rest),
    )
    seen = prepare(measured)
    tables = jnp.asarray(dft_tables())
    twice = jnp.concatenate([probe_field, probe_field], 1)
    scale = (2.0 / jnp.max(probe_field[0] * probe_field[0] + probe_field[1] * probe_field[1])).reshape(1)
    changed, halo, leaving, keep, send, cross_first, core_first, cross_rest, core_rest = first_visits(
        is_odd, mine, above, below, scale, object_field, halo, twice, seen, tables
    )
    arrived = {}

    def tie_exchange(step):
        if step == 0:
            def back(ties):
                arrived["core"] = swapped(ties[0], core)
            return [core_first], back
        if step == 1:
            def back(ties):
                arrived["core"] = ties[0]
                arrived["cross"] = swapped(ties[1], pairs_from(1, 4))
                arrived["core_rest"] = swapped(ties[2], core)
            return [arrived["core"], cross_first, core_rest], back
        if step == OTHER_TIE:
            def back(ties):
                arrived["cross"], arrived["core_rest"] = ties[:2]
                arrived["other"] = swapped(ties[2], pairs_from(3, 4))
            return [arrived["cross"], arrived["core_rest"], cross_first], back
        return [], lambda ties: None

    probe_now, twice, scale = moved_probe(probe_field, keep, send, tie_exchange)
    pieces = [
        arrived["cross"],
        arrived["other"],
        arrived["core"],
        if_needed(cross_shared - SHARED, lambda part: swapped(part, cross), cross_rest),
        arrived["core_rest"],
    ]
    changed, leaving, leaving_rest, keep, send = second_visits(
        is_odd, mine, above, below, scale, changed, halo, leaving, pieces, twice, seen, tables
    )
    arriving = [shifted(leaving, 1), lowered(leaving_rest, core)]

    def tie_arriving(step):
        if step == 1:
            def back(ties):
                arriving[:] = ties
            return arriving[:], back
        if step == LAST_TIE:
            by_cross = if_needed(cross_whole - SURE, lambda part: lowered(part, cross), leaving_rest)
            finished = finish(is_odd, mine, above, changed, *arriving, by_cross)

            def back(ties):
                arriving.append(ties[0])
            return [finished], back
        return [], lambda ties: None

    probe_now, _, _ = moved_probe(probe_now, keep, send, tie_arriving)
    return arriving[2], probe_now


def solution(mesh):
    return jax.shard_map(
        on_device,
        mesh=mesh,
        in_specs=(
            P(None, ("groups", "ty"), None),
            P("groups", None, None),
            P(("groups", "ty"), None),
            P(("groups", "ty")),
            P(("groups", "ty"), None, None),
        ),
        out_specs=(P(None, ("groups", "ty"), None), P("groups", None, None)),
        check_vma=False,
    )
```

```python
import functools
import math

import jax
import jax.numpy as jnp
import ml_dtypes
import numpy as np
from jax import lax
from jax.experimental import pallas as pl
from jax.experimental.pallas import tpu as pltpu
from jax.sharding import PartitionSpec as P

ITERS = 2
PS = 256
STEP = 8
STRETCH = 64
LAST_TIE = 3
OTHER_TIE = 4
SHARED = 512
EXTRA = 8
SURE = 1024
MIB = 1024 * 1024
WAYS = 6
BLOCK = 256
VISIT_LIMIT = 58 * MIB
HALF = 128
F32 = jnp.float32
BF16 = jnp.bfloat16


def split_table(table):
    high = table.astype(np.float32).astype(ml_dtypes.bfloat16)
    low = (table - high.astype(np.float64)).astype(np.float32).astype(ml_dtypes.bfloat16)
    return np.stack([high, low])


def dft_tables():
    points, bins = np.arange(HALF)[:, None], np.arange(HALF)[None, :]
    found = []
    for odd in (0, 1):
        phase = (points * (2 * bins + odd)) % PS
        angle = phase * (-2.0 * math.pi / PS)
        real, imag = np.cos(angle) / 16.0, np.sin(angle) / 16.0
        found.append(np.block([[real, imag], [-imag, real]]))
    even, odd = found
    return np.stack([split_table(t) for t in (even, even.T, odd, odd.T)])


def sort_table():
    table = np.zeros((PS, PS), np.float32)
    for k in range(HALF):
        table[2 * k, k] = 1.0
        table[2 * k + 1, HALF + k] = 1.0
    return table.astype(ml_dtypes.bfloat16)


def dot(a, b):
    return jnp.dot(a, b, preferred_element_type=F32)


def halves(x):
    high = x.astype(BF16)
    low = (x - high.astype(F32)).astype(BF16)
    return high, low


def lane(shape):
    return lax.broadcasted_iota(jnp.int32, shape, len(shape) - 1)


def row(shape):
    return lax.broadcasted_iota(jnp.int32, shape, len(shape) - 2)


def wrapped(mixed_first, whole, mixed_last, column):
    side = (column // HALF) % 2
    mixed = jnp.where(lane(mixed_first.shape) >= column % HALF, mixed_first, mixed_last)
    return jnp.where(side == 0, mixed, whole), jnp.where(side == 0, whole, mixed)


def cells(column, step, width):
    at = jnp.minimum(column // HALF + step, width // HALF - 1)
    return pl.ds(pl.multiple_of(at * HALF, HALF), HALF)


def load_wrapped(ref, plane, rows, column):
    blocks = [ref[plane, rows, cells(column, step, ref.shape[2])] for step in range(3)]
    return jnp.concatenate(wrapped(*blocks, column), axis=1)


def add_wrapped(ref, plane, rows, column, value):
    side, start = (column // HALF) % 2, column % HALF
    left, right = value[:, :HALF], value[:, HALF:]
    mixed = jnp.where(side == 0, left, right)
    other = jnp.where(side == 0, right, left)
    lanes = lane(mixed.shape)
    for step, part in ((0, jnp.where(lanes >= start, mixed, 0.0)), (1, other), (2, jnp.where(lanes < start, mixed, 0.0))):
        ref[plane, rows, cells(column, step, ref.shape[2])] += part


def up(value):
    return (value + STEP - 1) // STEP * STEP


def lengths(upper, lower, j):
    slots = (upper.shape[0] - 1) // 2
    reach, column = upper[2 * j], upper[2 * j + 1]
    first = reach
    for k in range(slots):
        near = (jnp.abs(lower[2 * k + 1] - column) < PS) & (k < lower[2 * slots])
        first = jnp.where(near, jnp.minimum(first, lower[2 * k]), first)
    live = j < upper[2 * slots]
    whole = jnp.where(live, up(reach), 0)
    shared = jnp.where(live & (first < reach), first // STEP * STEP, whole)
    return whole, shared


def each_window(upper, lower, body):
    def one(j, carry):
        at, at_shared = carry
        whole, shared = lengths(upper, lower, j)
        body(j, at, at_shared, whole, shared)
        return at + whole, at_shared + whole - shared

    return lax.fori_loop(0, (upper.shape[0] - 1) // 2, one, (0, 0))


def each_shared_piece(upper, lower, body):
    def window(j, at, at_shared, whole, shared):
        def piece(i, carry):
            start = pl.multiple_of(shared + i * STEP, STEP)
            body(j, start, pl.multiple_of(at + start, STEP), pl.multiple_of(at_shared + i * STEP, STEP))
            return carry

        lax.fori_loop(0, (whole - shared) // STEP, piece, 0)

    return each_window(upper, lower, window)


def each_stretch(upper, lower, body):
    def window(j, at, at_shared, whole, shared):
        def stretch(i, carry):
            start = pl.multiple_of(i * STRETCH, STRETCH)
            body(j, start, pl.multiple_of(at + start, STEP), whole - start)
            return carry

        lax.fori_loop(0, (whole + STRETCH - 1) // STRETCH, stretch, 0)

    return each_window(upper, lower, window)


def block_copies(source, source_at, target, target_at, rows, needed, semaphores, first=0):
    return [
        (
            needed > start,
            pltpu.make_async_copy(
                source.at[pl.ds(source_at + start, BLOCK)], target.at[pl.ds(target_at + start, BLOCK)], semaphores.at[first + number]
            ),
        )
        for number, start in enumerate(range(0, rows, BLOCK))
    ]


def start_all(copies):
    for needed, copy in copies:
        pl.when(needed)(copy.start)


def wait_all(copies):
    for needed, copy in copies:
        pl.when(needed)(copy.wait)


def sum_lengths(upper, lower):
    def count(j, carry):
        whole, shared = lengths(upper, lower, j)
        return carry[0] + whole, carry[1] + whole - shared

    return lax.fori_loop(0, (upper.shape[0] - 1) // 2, count, (0, 0))


def whole_spec(space):
    return pl.BlockSpec(memory_space=space)


VM, SM = pltpu.VMEM, pltpu.SMEM


def pack_kernel(mine, above, below, object_field, sure, rest, sizes, current, packed, arrival, departures):
    load = pltpu.make_async_copy(object_field, current, arrival)
    load.start()
    all_above, shared_above = sum_lengths(above, mine)
    all_below, shared_below = sum_lengths(mine, below)
    sizes[0], sizes[1], sizes[2], sizes[3] = all_above, shared_above, all_below, shared_below
    load.wait()

    def stretch(j, start, place, used):
        rows = pl.ds(start, STRETCH)
        for plane in range(2):
            packed[pl.ds(place, STRETCH), lanes_of(plane)] = load_wrapped(current, plane, rows, above[2 * j + 1])

    each_stretch(above, mine, stretch)
    sends = block_copies(packed, 0, sure, 0, SURE, all_above, departures)
    sends += block_copies(packed, SURE, rest, 0, packed.shape[0] - SURE, all_above - SURE, departures, SURE // BLOCK)
    start_all(sends)
    wait_all(sends)


def pack(mine, above, below, current):
    total = (mine.shape[0] - 1) // 2 * PS
    anywhere = whole_spec(pl.ANY)
    return pl.pallas_call(
        pack_kernel,
        out_shape=(
            jax.ShapeDtypeStruct((SURE, 2 * PS), F32),
            jax.ShapeDtypeStruct((total - SURE, 2 * PS), F32),
            jax.ShapeDtypeStruct((4,), jnp.int32),
        ),
        in_specs=[whole_spec(SM)] * 3 + [anywhere],
        out_specs=(anywhere, anywhere, whole_spec(SM)),
        scratch_shapes=[
            pltpu.VMEM(current.shape, F32),
            pltpu.VMEM((total, 2 * PS), F32),
            pltpu.SemaphoreType.DMA,
            pltpu.SemaphoreType.DMA((total // BLOCK,)),
        ],
        compiler_params=pltpu.CompilerParams(vmem_limit_bytes=16 * MIB),
        name="pack_rows",
    )(mine, above, below, *in_hbm(current))


def three_parts(x):
    high = x.astype(BF16)
    rest = x - high.astype(F32)
    middle = rest.astype(BF16)
    return high, middle, (rest - middle.astype(F32)).astype(BF16)


def prepare_kernel(table, measured, seen):
    by_place = table[...]
    by_row = by_place.T

    def one(j, carry):
        by_column = sum(dot(part, by_place) for part in three_parts(measured[j]))
        seen[j] = sum(dot(by_row, part) for part in three_parts(by_column))
        return carry

    lax.fori_loop(0, measured.shape[0], one, 0)


def prepare(measured):
    return pl.pallas_call(
        prepare_kernel,
        out_shape=jax.ShapeDtypeStruct(measured.shape, F32),
        in_specs=[whole_spec(VM), whole_spec(VM)],
        out_specs=whole_spec(VM),
        compiler_params=pltpu.CompilerParams(vmem_limit_bytes=16 * MIB),
        cost_estimate=cost(6),
        name="prepare",
    )(sort_table(), measured)


PIECE = 32


def times_right(x, table):
    high, low = x[:, :PS], x[:, PS:]
    return dot(jnp.concatenate([high, low, high], 1), jnp.concatenate([table[0], table[0], table[1]], 0))


def times_left(table, x):
    high, low = x[:PS, :], x[PS:, :]
    return dot(jnp.concatenate([table[0], table[0], table[1]], 1), jnp.concatenate([high, low, high], 0))


def put_columns(ref, rows, at, first, second):
    for place, part in ((at, first), (at + HALF, second)):
        high, low = halves(part)
        ref[rows, place : place + HALF] = high
        ref[rows, place + PS : place + PS + HALF] = low


def put_rows(ref, number, at, first, second):
    for place, part in ((at, first), (at + HALF, second)):
        high, low = halves(part)
        ref[number, place : place + PIECE, :] = high
        ref[number, PS + place : PS + place + PIECE, :] = low


def visit_stages(live, reach, column, at, current, halo, probe, seen, j, tables, held, scratch, emit):
    turned, window, wide, tall, product = scratch
    even, even_t, odd, odd_t = (tables.at[k] for k in range(4))
    right, left = column % PS, (PS - column % PS) % PS
    shift = reach % 8
    base = pl.multiple_of(PS - reach // 8 * 8, 8)
    own_from = jnp.where(live, reach, 0)
    weight_of = live.astype(F32)

    def rows_of(start, count=PIECE):
        return slice(start, start + count)

    def is_inside(start):
        return row((PIECE, PS)) + start >= own_from

    for start in range(0, PS, PIECE):
        inside = is_inside(start)
        rows = rows_of(start)
        for plane in range(2):
            below = halo[pl.ds(pl.multiple_of(at + start, 8), PIECE), lanes_of(plane)]
            window[plane, rows, :] = jnp.where(inside, load_wrapped(current, plane, rows, column), below)
            groups = probe[plane, pl.ds(pl.multiple_of(base + start - 8, 8), PIECE + 8), :].reshape(-1, 8, PS)
            groups = pltpu.roll(groups, shift, 1)
            lowered_rows = jnp.where(row((PIECE // 8, 8, PS)) < shift, groups[:-1], groups[1:]).reshape(PIECE, PS)
            turned[plane, rows, :] = pltpu.roll(lowered_rows, right, 1)
        w_real, w_imag = window[0, rows, :], window[1, rows, :]
        p_real, p_imag = turned[0, rows, :], turned[1, rows, :]
        real = p_real * w_real - p_imag * w_imag
        imag = p_real * w_imag + p_imag * w_real
        put_columns(wide, rows, 0, real[:, :HALF] + real[:, HALF:], imag[:, :HALF] + imag[:, HALF:])
        put_columns(wide, rows, 2 * PS, real[:, :HALF] - real[:, HALF:], imag[:, :HALF] - imag[:, HALF:])
    yield
    product[0] = times_right(wide[:, : 2 * PS], even)
    product[1] = times_right(wide[:, 2 * PS :], odd)
    yield
    for start in range(0, HALF, PIECE):
        top, bottom = [product[k, rows_of(start), :] for k in range(2)], [product[k, rows_of(HALF + start), :] for k in range(2)]
        plus, minus = [a + b for a, b in zip(top, bottom)], [a - b for a, b in zip(top, bottom)]
        for number, part in enumerate((plus, minus)):
            real = jnp.concatenate([x[:, :HALF] for x in part], 1)
            imag = jnp.concatenate([x[:, HALF:] for x in part], 1)
            put_rows(tall, number, start, real, imag)
    yield
    product[0] = times_left(even_t, tall[0])
    product[1] = times_left(odd_t, tall[1])
    yield
    for number in range(2):
        for start in range(0, HALF, PIECE):
            real, imag = product[number, rows_of(start), :], product[number, rows_of(HALF + start), :]
            weight = (real * real + imag * imag - seen[j, rows_of(number * HALF + start), :]) * weight_of
            put_rows(tall, number, start, weight * real, weight * imag)
    yield
    product[0] = times_left(even, tall[0])
    product[1] = times_left(odd, tall[1])
    yield
    for start in range(0, HALF, PIECE):
        real, imag = [product[k, rows_of(start), :] for k in range(2)], [product[k, rows_of(HALF + start), :] for k in range(2)]
        for place, real_part, imag_part in (
            (start, real[0] + real[1], imag[0] + imag[1]),
            (HALF + start, real[0] - real[1], imag[0] - imag[1]),
        ):
            rows = rows_of(place)
            put_columns(wide, rows, 0, real_part[:, :HALF], imag_part[:, :HALF])
            put_columns(wide, rows, 2 * PS, real_part[:, HALF:], imag_part[:, HALF:])
    yield
    product[0] = times_right(wide[:, : 2 * PS], even_t)
    product[1] = times_right(wide[:, 2 * PS :], odd_t)
    yield
    for start in range(0, PS, PIECE):
        rows = rows_of(start)
        first, second = product[0, rows, :], product[1, rows, :]
        plus, minus = first + second, first - second
        real = jnp.concatenate([plus[:, :HALF], minus[:, :HALF]], 1)
        imag = jnp.concatenate([plus[:, HALF:], minus[:, HALF:]], 1)
        w_real, w_imag = window[0, rows, :], window[1, rows, :]
        p_real, p_imag = turned[0, rows, :], turned[1, rows, :]
        emit(start, is_inside(start), (p_real * real + p_imag * imag, p_real * imag - p_imag * real))
        for plane, term in enumerate((w_real * real + w_imag * imag, w_real * imag - w_imag * real)):
            groups = pltpu.roll(pltpu.roll(term, left, 1).reshape(-1, 8, PS), (8 - shift) % 8, 1)
            stays = row(groups.shape) < 8 - shift
            here = pl.ds(pl.multiple_of(base + start, 8), PIECE)
            before = pl.ds(pl.multiple_of(base + start - 8, 8), PIECE)
            held[plane, here, :] += jnp.where(stays, groups, 0.0).reshape(PIECE, PS)
            held[plane, before, :] += jnp.where(stays, 0.0, groups).reshape(PIECE, PS)
    yield


def stage_scratch():
    return [
        pltpu.VMEM((2, PS, PS), F32),
        pltpu.VMEM((2, PS, PS), F32),
        pltpu.VMEM((PS, 4 * PS), BF16),
        pltpu.VMEM((2, 2 * PS, PS), BF16),
        pltpu.VMEM((2, PS, PS), F32),
    ]


def visit_all(mine, below, current, halo, probe, seen, tables, held, scratch, emit):
    slots = (mine.shape[0] - 1) // 2
    ways = len(scratch) // 5

    def some(turn, at):
        stages = []
        for way in range(ways):
            j = jnp.minimum(ways * turn + way, slots - 1)
            live = ways * turn + way < mine[2 * slots]
            reach, column = mine[2 * j], mine[2 * j + 1]
            whole, shared = lengths(mine, below, j)
            place = pl.multiple_of(jnp.minimum(at, (slots - 1) * PS), STEP)
            stages.append(
                visit_stages(
                    live, reach, column, place, current, halo, probe, seen, j, tables, held, scratch[5 * way : 5 * way + 5],
                    functools.partial(emit, live, column, place, shared),
                )
            )
            at = at + jnp.where(live, whole, 0)
        open_stages = list(stages)
        step = 0
        while open_stages:
            for way, stage in enumerate(stages):
                if stage in open_stages and way <= step and next(stage, True) is True:
                    open_stages.remove(stage)
            step += 1
        return at

    lax.fori_loop(0, (mine[2 * slots] + ways - 1) // ways, some, 0)


def split_gradient(held, odd, used, keep, send):
    real = held[0, :PS, :] + held[0, PS:, :]
    imag = held[1, :PS, :] + held[1, PS:, :]
    keep[:PS, :] = jnp.where(odd, imag, real)
    send[:PS, :] = jnp.where(odd, real, imag)
    number = jnp.full((EXTRA, PS), used.astype(F32))
    keep[PS:, :] = number
    send[PS:, :] = number


def lanes_of(plane):
    return slice(plane * PS, (plane + 1) * PS)


def first_kernel(
    is_odd, mine, above, below, scale, object_field, halo_sure, halo_core, halo_cross, probe, measured, tables,
    out_changed, out_halo, out_leaving, keep, send, cross_first, core_first, cross_rest, core_rest,
    current, out, under, halo, leaving, cross, core, probe_held, seen, tables_held, held, arrivals, departures, *scratch,
):
    slots = (mine.shape[0] - 1) // 2
    used = mine[2 * slots]
    odd = is_odd[0] == 1
    factor = scale[0]
    total = halo.shape[0]
    all_below, shared_below = sum_lengths(mine, below)
    shared_above = sum_lengths(above, mine)[1]
    loads = [
        (used >= 0, pltpu.make_async_copy(source, target, arrivals.at[number]))
        for number, (source, target) in enumerate(
            ((object_field, current), (tables, tables_held), (probe, probe_held), (measured, seen))
        )
    ]
    loads += block_copies(halo_sure, 0, halo, 0, SURE, all_below, arrivals, 4)
    after = 4 + SURE // BLOCK
    for needed, source in ((~odd, halo_core), (odd, halo_cross)):
        more = jnp.where(needed, all_below - SURE, 0)
        loads += block_copies(source, 0, halo, SURE, total - SURE, more, arrivals, after)
    start_all(loads)
    under[...] = jnp.zeros_like(under)
    held[...] = jnp.zeros_like(held)
    loads[0][1].wait()
    out[...] = current[...]
    wait_all(loads[1:])

    def emit(live, column, place, shared, start, inside, terms):
        rows = slice(start, start + PIECE)
        for plane in range(2):
            change = terms[plane] * -factor
            own, other = jnp.where(inside, change, 0.0), jnp.where(inside, 0.0, change)
            add_wrapped(out, plane, rows, column, own)
            add_wrapped(under, plane, rows, column, other)
            leaving[pl.ds(pl.multiple_of(place + start, STEP), PIECE), lanes_of(plane)] = other

    visit_all(mine, below, current, halo, probe_held, seen, tables_held, held, scratch, emit)
    sends = [(used >= 0, pltpu.make_async_copy(out, out_changed, departures.at[0]))]
    sends += block_copies(leaving, 0, out_leaving, 0, total, all_below, departures, 1)
    start_all(sends)
    split_gradient(held, odd, used, keep, send)

    def store(to_cross, place, value):
        @pl.when(to_cross)
        def _():
            cross[pl.ds(place, STEP), :] = value

        @pl.when(~to_cross)
        def _():
            core[pl.ds(place, STEP), :] = value

    def rising(j, at, place, at_shared):
        rows = pl.ds(at, STEP)
        planes = [
            load_wrapped(out, plane, rows, above[2 * j + 1]) - load_wrapped(current, plane, rows, above[2 * j + 1])
            for plane in range(2)
        ]
        store(~odd, at_shared, jnp.concatenate(planes, axis=1))

    each_shared_piece(above, mine, rising)

    def falling(j, at, place, at_shared):
        store(odd, at_shared, leaving[pl.ds(place, STEP), :])

    each_shared_piece(mine, below, falling)
    in_cross, in_core = jnp.where(odd, shared_below, shared_above), jnp.where(odd, shared_above, shared_below)
    count = total // BLOCK
    pieces = []
    for number, (source, first, rest, rows) in enumerate(((cross, cross_first, cross_rest, in_cross), (core, core_first, core_rest, in_core))):
        at = 1 + count * (1 + number)
        pieces += block_copies(source, 0, first, 0, SHARED, rows, departures, at)
        pieces += block_copies(source, SHARED, rest, 0, total - SHARED, rows - SHARED, departures, at + SHARED // BLOCK)
    start_all(pieces)

    def renew(j, start, place, inside):
        rows = pl.ds(place, STRETCH)
        within = row((STRETCH, PS)) < inside
        for plane in range(2):
            change = load_wrapped(under, plane, pl.ds(start, STRETCH), mine[2 * j + 1])
            halo[rows, lanes_of(plane)] += jnp.where(within, change, 0.0)

    each_stretch(mine, below, renew)
    last = block_copies(halo, 0, out_halo, 0, total, all_below, departures, 1 + 3 * count)
    start_all(last)
    wait_all(sends + pieces + last)


def in_hbm(*arrays):
    return [pltpu.with_memory_space_constraint(array, pltpu.HBM) for array in arrays]


def cost(microseconds):
    return pl.CostEstimate(flops=microseconds * 10**9, bytes_accessed=microseconds * 2 * 10**6, transcendentals=0)


def array(*shape):
    return jax.ShapeDtypeStruct(shape, F32)


def visit_scratch(tile, total, measured, tables):
    return [
        pltpu.VMEM((2, 2 * PS, PS), F32),
        pltpu.VMEM(measured, F32),
        pltpu.VMEM(tables, BF16),
        pltpu.VMEM((2, 2 * PS, PS), F32),
    ]


def first_visits(is_odd, mine, above, below, scale, current, halo, probe, measured, tables):
    total = halo[0].shape[0] + halo[1].shape[0]
    rest = total - SHARED
    blocks = total // BLOCK
    anywhere = whole_spec(pl.ANY)
    tile, row_list = pltpu.VMEM(current.shape, F32), pltpu.VMEM((total, 2 * PS), F32)
    return pl.pallas_call(
        first_kernel,
        out_shape=(array(*current.shape), array(total, 2 * PS), array(total, 2 * PS))
        + (array(PS + EXTRA, PS),) * 2
        + (array(SHARED, 2 * PS),) * 2
        + (array(rest, 2 * PS),) * 2,
        in_specs=[whole_spec(SM)] * 5 + [anywhere] * 7,
        out_specs=(anywhere,) * 3 + (whole_spec(VM),) * 2 + (anywhere,) * 4,
        scratch_shapes=[tile] * 3 + [row_list] * 4 + visit_scratch(current.shape, total, measured.shape, tables.shape)
        + [pltpu.SemaphoreType.DMA((4 + blocks,)), pltpu.SemaphoreType.DMA((1 + 4 * blocks,))]
        + stage_scratch() * WAYS,
        compiler_params=pltpu.CompilerParams(vmem_limit_bytes=VISIT_LIMIT),
        cost_estimate=cost(12),
        name="first_visits",
    )(is_odd, mine, above, below, scale, *in_hbm(current, *halo, probe, measured, tables))


def second_kernel(
    is_odd, mine, above, below, scale, changed, old_halo, old_leaving, cross_first, other_first, core_first, cross_rest,
    core_rest, probe, measured, tables,
    out_changed, leaving_sure, leaving_rest, keep, send,
    current, out, halo, leaving, base, cross, core, probe_held, seen, tables_held, held, arrivals, departures, *scratch,
):
    slots = (mine.shape[0] - 1) // 2
    used = mine[2 * slots]
    odd = is_odd[0] == 1
    factor = scale[0]
    total = halo.shape[0]
    count = total // BLOCK
    all_below, shared_below = sum_lengths(mine, below)
    shared_above = sum_lengths(above, mine)[1]
    in_cross, in_core = jnp.where(odd, shared_below, shared_above), jnp.where(odd, shared_above, shared_below)
    loads = [
        (used >= 0, pltpu.make_async_copy(source, target, arrivals.at[number]))
        for number, (source, target) in enumerate(
            ((changed, current), (tables, tables_held), (probe, probe_held), (measured, seen))
        )
    ]
    at_other = is_odd[1] == 1
    pieces = block_copies(cross_first, 0, cross, 0, SHARED, jnp.where(at_other, 0, in_cross), arrivals, 4)
    pieces += block_copies(other_first, 0, cross, 0, SHARED, jnp.where(at_other, in_cross, 0), arrivals, 4)
    pieces += block_copies(cross_rest, 0, cross, SHARED, total - SHARED, in_cross - SHARED, arrivals, 4 + SHARED // BLOCK)
    pieces += block_copies(core_first, 0, core, 0, SHARED, in_core, arrivals, 4 + count)
    pieces += block_copies(core_rest, 0, core, SHARED, total - SHARED, in_core - SHARED, arrivals, 4 + count + SHARED // BLOCK)
    lists = block_copies(old_halo, 0, halo, 0, total, all_below, arrivals, 4 + 2 * count)
    lists += block_copies(old_leaving, 0, base, 0, total, all_below, arrivals, 4 + 3 * count)
    start_all(loads[:1] + pieces + lists + loads[1:])
    held[...] = jnp.zeros_like(held)
    wait_all(loads[:1] + pieces)

    def from_above(j, at, place, at_shared):
        rows = pl.ds(at_shared, STEP)
        part = jnp.where(odd, core[rows, :], cross[rows, :])
        for plane in range(2):
            add_wrapped(current, plane, pl.ds(at, STEP), above[2 * j + 1], part[:, lanes_of(plane)])

    each_shared_piece(above, mine, from_above)
    out[...] = current[...]
    wait_all(lists + loads[1:])

    def renew(j, at, place, at_shared):
        rows = pl.ds(at_shared, STEP)
        halo[pl.ds(place, STEP), :] += jnp.where(odd, cross[rows, :], core[rows, :])

    each_shared_piece(mine, below, renew)

    def emit(live, column, place, shared, start, inside, terms):
        rows = slice(start, start + PIECE)
        unsent = row((PIECE, PS)) + start < shared
        for plane in range(2):
            lanes, here = lanes_of(plane), pl.ds(pl.multiple_of(place + start, STEP), PIECE)
            change = terms[plane] * -factor
            add_wrapped(out, plane, rows, column, jnp.where(inside, change, 0.0))
            leaving[here, lanes] = jnp.where(inside, 0.0, change) + jnp.where(unsent, base[here, lanes], 0.0)

    visit_all(mine, below, current, halo, probe_held, seen, tables_held, held, scratch, emit)
    sends = block_copies(leaving, 0, leaving_sure, 0, SURE, all_below, departures, 1)
    sends += block_copies(leaving, SURE, leaving_rest, 0, total - SURE, all_below - SURE, departures, 1 + SURE // BLOCK)
    sends += [(used >= 0, pltpu.make_async_copy(out, out_changed, departures.at[0]))]
    start_all(sends)
    split_gradient(held, odd, used, keep, send)
    wait_all(sends)


def second_visits(is_odd, mine, above, below, scale, changed, halo, base, pieces, probe, measured, tables):
    total = halo.shape[0]
    blocks = total // BLOCK
    anywhere = whole_spec(pl.ANY)
    tile, row_list = pltpu.VMEM(changed.shape, F32), pltpu.VMEM((total, 2 * PS), F32)
    return pl.pallas_call(
        second_kernel,
        out_shape=(array(*changed.shape), array(SURE, 2 * PS), array(total - SURE, 2 * PS)) + (array(PS + EXTRA, PS),) * 2,
        in_specs=[whole_spec(SM)] * 5 + [anywhere] * 11,
        out_specs=(anywhere,) * 3 + (whole_spec(VM),) * 2,
        scratch_shapes=[tile] * 2 + [row_list] * 5 + visit_scratch(changed.shape, total, measured.shape, tables.shape)
        + [pltpu.SemaphoreType.DMA((4 + 4 * blocks,)), pltpu.SemaphoreType.DMA((1 + blocks,))]
        + stage_scratch() * WAYS,
        compiler_params=pltpu.CompilerParams(vmem_limit_bytes=VISIT_LIMIT),
        cost_estimate=cost(12),
        name="second_visits",
    )(is_odd, mine, above, below, scale, *in_hbm(changed, halo, base, *pieces, probe, measured, tables))


def finish_kernel(is_odd, mine, above, changed, sure, core_rest, cross_rest, out, arrived, arrivals):
    odd = is_odd[0] == 1
    total = arrived.shape[0]
    all_above = sum_lengths(above, mine)[0]
    load = pltpu.make_async_copy(changed, out, arrivals.at[0])
    load.start()
    loads = block_copies(sure, 0, arrived, 0, SURE, all_above, arrivals, 1)
    for needed, source in ((odd, core_rest), (~odd, cross_rest)):
        more = jnp.where(needed, all_above - SURE, 0)
        loads += block_copies(source, 0, arrived, SURE, total - SURE, more, arrivals, 1 + SURE // BLOCK)
    start_all(loads)
    load.wait()
    wait_all(loads)

    def stretch(j, start, place, used):
        within = row((STRETCH, PS)) < used
        for plane in range(2):
            part = jnp.where(within, arrived[pl.ds(place, STRETCH), lanes_of(plane)], 0.0)
            add_wrapped(out, plane, pl.ds(start, STRETCH), above[2 * j + 1], part)

    each_stretch(above, mine, stretch)


def finish(is_odd, mine, above, changed, sure, core_rest, cross_rest):
    anywhere = whole_spec(pl.ANY)
    total = sure.shape[0] + core_rest.shape[0]
    return pl.pallas_call(
        finish_kernel,
        out_shape=jax.ShapeDtypeStruct(changed.shape, F32),
        in_specs=[whole_spec(SM)] * 3 + [anywhere] * 4,
        out_specs=whole_spec(VM),
        scratch_shapes=[pltpu.VMEM((total, 2 * PS), F32), pltpu.SemaphoreType.DMA((1 + total // BLOCK,))],
        compiler_params=pltpu.CompilerParams(vmem_limit_bytes=20 * MIB),
        name="add_arriving",
    )(is_odd, mine, above, *in_hbm(changed, sure, core_rest, cross_rest))


def tied(kernel, name, inputs, in_specs, outs, out_specs, ties):
    count, found = len(inputs), len(outs)

    def body(*refs):
        kernel(*refs[:count], *refs[count + len(ties) : count + len(ties) + found])

    anywhere = whole_spec(pl.ANY)
    results = pl.pallas_call(
        body,
        out_shape=tuple(outs) + tuple(jax.ShapeDtypeStruct(t.shape, t.dtype) for t in ties),
        in_specs=list(in_specs) + [anywhere] * len(ties),
        out_specs=tuple(out_specs) + (anywhere,) * len(ties),
        input_output_aliases={count + k: found + k for k in range(len(ties))},
        compiler_params=pltpu.CompilerParams(vmem_limit_bytes=8 * MIB),
        name=name,
    )(*inputs, *ties)
    return results[:found], list(results[found:])


def halve_kernel(side, kept, got, keep, send):
    half = keep.shape[0] - EXTRA
    total = kept[...] + got[...]
    low, high = total[:half], total[half : 2 * half]
    first = side[0] == 0
    keep[:half, :] = jnp.where(first, low, high)
    send[:half, :] = jnp.where(first, high, low)
    keep[half:, :] = total[2 * half :]
    send[half:, :] = total[2 * half :]


def sum_kernel(kept, got, out):
    out[...] = kept[...] + got[...]


def join_kernel(side, mine, other, out):
    height = mine.shape[0] - EXTRA
    first = side[0] == 0
    out[:height, :] = jnp.where(first, mine[:height, :], other[:height, :])
    out[height : 2 * height, :] = jnp.where(first, other[:height, :], mine[:height, :])
    out[2 * height :, :] = mine[height:, :]


def move_kernel(side, mine, other, probe, out, twice, scale):
    first = side[0] == 0
    step = 4.0 / mine[PS : PS + 1, :]
    real = probe[0] - step * jnp.where(first, mine[:PS, :], other[:PS, :])
    imag = probe[1] - step * jnp.where(first, other[:PS, :], mine[:PS, :])
    out[0] = real
    out[1] = imag
    for part in range(2):
        rows = slice(part * PS, (part + 1) * PS)
        twice[0, rows, :] = real
        twice[1, rows, :] = imag
    scale[0] = 2.0 / jnp.max(real * real + imag * imag)


def moved_probe(probe, keep, send, tie):
    count = lax.axis_size("ty")
    me = lax.axis_index("ty")
    bits = [1 << k for k in range((count - 1).bit_length())]
    vm, sm = whole_spec(VM), whole_spec(SM)

    def swap(value, bit):
        return lax.ppermute(value, "ty", [(i, i ^ bit) for i in range(count)])

    def side_of(bit):
        return (me // bit % 2).reshape(1)

    def call(step, kernel, name, inputs, in_specs, outs):
        ties, back = tie(step)
        found, ties = tied(kernel, name, inputs, in_specs, outs, [vm] * len(outs), ties)
        back(ties)
        return found

    got = swap(send, 1)
    shape = array((keep.shape[0] - EXTRA) // 2 + EXTRA, PS)
    keep, send = call(0, halve_kernel, "halve_sum", (side_of(2), keep, got), [sm, vm, vm], [shape, shape])
    value, bit = keep, 2
    got = swap(send, 2)
    step = 1
    for bit in bits[2:] + [0]:
        (value,) = call(step, sum_kernel, "add_sum", (value, got), [vm, vm], [array(value.shape[0], PS)])
        step += 1
        if bit:
            got = swap(value, bit)
    other = swap(value, 2)
    shape = array(2 * (value.shape[0] - EXTRA) + EXTRA, PS)
    (value,) = call(step, join_kernel, "join_sum", (side_of(2), value, other), [sm, vm, vm], [shape])
    other = swap(value, 1)
    return pl.pallas_call(
        move_kernel,
        out_shape=(
            jax.ShapeDtypeStruct(probe.shape, F32),
            jax.ShapeDtypeStruct((2, 2 * PS, PS), F32),
            jax.ShapeDtypeStruct((1,), F32),
        ),
        in_specs=[sm, vm, vm, vm],
        out_specs=(vm, vm, sm),
        compiler_params=pltpu.CompilerParams(vmem_limit_bytes=8 * MIB),
        name="move_probe",
    )(side_of(1), value, other, probe)


def unwritten(shape):
    return pl.pallas_call(
        lambda out: None, out_shape=shape, out_specs=whole_spec(pl.ANY), compiler_params=pltpu.CompilerParams(has_side_effects=False), name="unwritten"
    )()


def shifted(value, steps):
    count = lax.axis_size("ty")
    first, last = (max(0, -steps), min(count, count - steps))
    return lax.ppermute(value, "ty", [(source, source + steps) for source in range(first, last)])


def pairs_from(first, step=2):
    return [(k, k + 1) for k in range(first, lax.axis_size("ty") - 1, step)]


def swapped(value, pairs):
    return lax.ppermute(value, "ty", pairs + [(b, a) for a, b in pairs])


def raised(value, pairs):
    return lax.ppermute(value, "ty", [(b, a) for a, b in pairs])


def lowered(value, pairs):
    return lax.ppermute(value, "ty", pairs)


def if_needed(rows, move, value):
    shape = jax.ShapeDtypeStruct(value.shape, value.dtype)

    def part(height):
        def branch(kept):
            if height == 0:
                return unwritten(shape)
            if height == kept.shape[0]:
                return move(kept)
            rest = jax.ShapeDtypeStruct((kept.shape[0] - height, kept.shape[1]), kept.dtype)
            return jnp.concatenate([move(kept[:height]), unwritten(rest)])

        return branch

    heights = [0]
    while heights[-1] < value.shape[0]:
        heights.append(min(max(BLOCK, 2 * heights[-1]), value.shape[0]))
    number = sum((rows > height).astype(jnp.int32) for height in heights[:-1])
    return lax.switch(number, [part(height) for height in heights], value)


def on_device(object_field, probe_field, scan_offsets, tile_counts, measured):
    rows = object_field.shape[1]
    tile = lax.axis_index("ty")
    odd = tile % 2 == 1
    is_odd = jnp.stack([tile % 2, ((tile + 1) % 4 < 2).astype(jnp.int32)])
    core, cross = pairs_from(0), pairs_from(1)
    local_rows = scan_offsets[:, 0] - tile * rows
    mine = jnp.concatenate([jnp.stack([local_rows, scan_offsets[:, 1]], 1).reshape(-1), tile_counts])
    above, below = shifted(mine, 1), shifted(mine, -1)
    sure, rest, sizes = pack(mine, above, below, object_field)
    cross_whole = jnp.where(odd, sizes[2], sizes[0])
    cross_shared = jnp.where(odd, sizes[3], sizes[1])
    halo = (
        shifted(sure, -1),
        raised(rest, core),
        if_needed(cross_whole - SURE, lambda part: raised(part, cross), rest),
    )
    seen = prepare(measured)
    tables = jnp.asarray(dft_tables())
    twice = jnp.concatenate([probe_field, probe_field], 1)
    scale = (2.0 / jnp.max(probe_field[0] * probe_field[0] + probe_field[1] * probe_field[1])).reshape(1)
    changed, halo, leaving, keep, send, cross_first, core_first, cross_rest, core_rest = first_visits(
        is_odd, mine, above, below, scale, object_field, halo, twice, seen, tables
    )
    arrived = {}

    def tie_exchange(step):
        if step == 0:
            def back(ties):
                arrived["core"] = swapped(ties[0], core)
            return [core_first], back
        if step == 1:
            def back(ties):
                arrived["core"] = ties[0]
                arrived["cross"] = swapped(ties[1], pairs_from(1, 4))
                arrived["core_rest"] = swapped(ties[2], core)
            return [arrived["core"], cross_first, core_rest], back
        if step == OTHER_TIE:
            def back(ties):
                arrived["cross"], arrived["core_rest"] = ties[:2]
                arrived["other"] = swapped(ties[2], pairs_from(3, 4))
            return [arrived["cross"], arrived["core_rest"], cross_first], back
        return [], lambda ties: None

    probe_now, twice, scale = moved_probe(probe_field, keep, send, tie_exchange)
    pieces = [
        arrived["cross"],
        arrived["other"],
        arrived["core"],
        if_needed(cross_shared - SHARED, lambda part: swapped(part, cross), cross_rest),
        arrived["core_rest"],
    ]
    changed, leaving, leaving_rest, keep, send = second_visits(
        is_odd, mine, above, below, scale, changed, halo, leaving, pieces, twice, seen, tables
    )
    arriving = [shifted(leaving, 1), lowered(leaving_rest, core)]

    def tie_arriving(step):
        if step == 1:
            def back(ties):
                arriving[:] = ties
            return arriving[:], back
        if step == LAST_TIE:
            by_cross = if_needed(cross_whole - SURE, lambda part: lowered(part, cross), leaving_rest)
            finished = finish(is_odd, mine, above, changed, *arriving, by_cross)

            def back(ties):
                arriving.append(ties[0])
            return [finished], back
        return [], lambda ties: None

    probe_now, _, _ = moved_probe(probe_now, keep, send, tie_arriving)
    return arriving[2], probe_now


def solution(mesh):
    return jax.shard_map(
        on_device,
        mesh=mesh,
        in_specs=(
            P(None, ("groups", "ty"), None),
            P("groups", None, None),
            P(("groups", "ty"), None),
            P(("groups", "ty")),
            P(("groups", "ty"), None, None),
        ),
        out_specs=(P(None, ("groups", "ty"), None), P("groups", None, None)),
        check_vma=False,
    )
```
